32 devices in a mesh: fine: 8 (over z, x), coarse: 4 (over y, core).
Axes of the slice: x: 2, y: 2, z: 4, core: 2. Of those that a mesh axis runs over, the one named last changes fastest.
Arguments:
- rhs: float32 [65536], P(('fine', 'coarse')), may hold values from -6 to 6
- fine_values: bfloat16 [7, 64, 65536], P(None, None, ('fine', 'coarse')), may hold values from -0.0501 to 1.05
- fine_columns: int32 [7, 1024], P(None, ('fine', 'coarse')), may hold values from 0 to 63, as said below
- smoother: bfloat16 [64, 65536], P(None, ('fine', 'coarse')), may hold values from -0.0601 to 1.0625
- reaction: float32 [65536], P(('fine', 'coarse')), may hold values from 0.2 to 2
- pit_counts: int32 [32], P(('fine', 'coarse')), may hold values from 1 to 32, 288 in all
- weights: float32 [65536], P(('fine', 'coarse')), may hold values from 0.04 to 0.4
- coarse_order: int32 [1024], P(('fine', 'coarse')), may hold values from 0 to 1023, each once
- coarse_values: bfloat16 [7, 64, 1024], P(None, None, 'coarse'), may hold values from -0.0501 to 1.05
- coarse_rows: int32 [7, 16], P(None, 'coarse'), may hold values from 0 to 15, as said below
- coarse_inverse: bfloat16 [64, 1024], P(None, 'coarse'), may hold values from -0.0301 to 0.5313
Outputs:
- solution: float32 [65536], P(('fine', 'coarse'))
- correction: float32 [1024], P('coarse')
The draws below stay inside these ranges and needn't reach their ends.
Inputs may be any that keep to these rules, and one draw needn't show every extreme that they name: fine_columns[0, a] = a % 32 + 16, the aggregate itself. `coarse_order`: each coarse unknown once. coarse_rows[0, j] = j.
All inputs are finite; a program needn't handle non-finite values. No bound on the sum of `pit_counts` on one device may be relied on, other than what follows from the above.
Results may differ from the reference program's by a relative error of at most 0.0003.
Values sent between devices are 32-bit elements; how exact they have to be, the bound alone decides.
No kernel may reach another device: no remote copies, remote signals or barrier semaphores. Data moves between devices by JAX's collectives and lax.ppermute only.
A program may use at most 64 MiB of HBM per device.

```python
import math
import jax
import jax.numpy as jnp
import numpy as np
from jax import lax

AGGREGATE_CELLS = 64
FINE_NBRS = 7
COARSE_NBRS = 7
SWEEPS = 4
AGG_DEV = 32
HALO = 16
SECTIONS = 32
AGGS = 1024
CELLS = 65536
COARSE_GROUPS = 16


def block_noise(key, shape, reach):
    return jax.random.uniform(key, shape, jnp.float32, -reach, reach)


def draw_fine_values(key, part):
    shape = (FINE_NBRS, AGGREGATE_CELLS, CELLS)
    slot_no = lax.broadcasted_iota(jnp.int32, shape, 0)
    out_dof = lax.broadcasted_iota(jnp.int32, shape, 1)
    in_dof = lax.broadcasted_iota(jnp.int32, shape, 2) % AGGREGATE_CELLS
    diagonal_entries = jnp.where((slot_no == 0) & (out_dof == in_dof), 1.0, 0.0).astype(jnp.float32)
    return (diagonal_entries + block_noise(key, shape, 0.05)).astype(jnp.bfloat16)


def draw_fine_columns(key, part):
    shape = (FINE_NBRS, AGGS)
    offsets = jax.random.randint(key, shape, -HALO, HALO + 1, jnp.int32)
    slot_no = lax.broadcasted_iota(jnp.int32, shape, 0)
    local_agg = lax.broadcasted_iota(jnp.int32, shape, 1) % AGG_DEV
    offsets = jnp.where(slot_no == 0, 0, offsets)
    offsets = jnp.where((slot_no == 1) & (local_agg == 0), -HALO, offsets)
    offsets = jnp.where((slot_no == 2) & (local_agg == AGG_DEV - 1), HALO, offsets)
    return (HALO + local_agg + offsets).astype(jnp.int32)


def draw_smoother(key, part):
    shape = (AGGREGATE_CELLS, CELLS)
    out_dof = lax.broadcasted_iota(jnp.int32, shape, 0)
    in_dof = lax.broadcasted_iota(jnp.int32, shape, 1) % AGGREGATE_CELLS
    diagonal_entries = jnp.where(out_dof == in_dof, 1.0, 0.0).astype(jnp.float32)
    return (diagonal_entries + block_noise(key, shape, 0.06)).astype(jnp.bfloat16)


def draw_coarse_values(key, part):
    shape = (COARSE_NBRS, AGGREGATE_CELLS, AGGS)
    slot_no = lax.broadcasted_iota(jnp.int32, shape, 0)
    out_dof = lax.broadcasted_iota(jnp.int32, shape, 1)
    in_dof = lax.broadcasted_iota(jnp.int32, shape, 2) % AGGREGATE_CELLS
    diagonal_entries = jnp.where((slot_no == 0) & (out_dof == in_dof), 1.0, 0.0).astype(jnp.float32)
    return (diagonal_entries + block_noise(key, shape, 0.05)).astype(jnp.bfloat16)


def draw_coarse_rows(key, part):
    shape = (COARSE_NBRS, COARSE_GROUPS)
    picked = jax.random.randint(key, shape, 0, COARSE_GROUPS, jnp.int32)
    slot_no = lax.broadcasted_iota(jnp.int32, shape, 0)
    own_block = lax.broadcasted_iota(jnp.int32, shape, 1)
    return jnp.where(slot_no == 0, own_block, picked).astype(jnp.int32)


def draw_coarse_inverse(key, part):
    shape = (AGGREGATE_CELLS, AGGS)
    out_dof = lax.broadcasted_iota(jnp.int32, shape, 0)
    in_dof = lax.broadcasted_iota(jnp.int32, shape, 1) % AGGREGATE_CELLS
    diagonal_entries = jnp.where(out_dof == in_dof, 0.5, 0.0).astype(jnp.float32)
    return (diagonal_entries + block_noise(key, shape, 0.03)).astype(jnp.bfloat16)


def steps_of(rng, shape, pieces, low, top_value):
    gain, own = 1.0, jax.random.fold_in(rng, 6)
    for position, blocks in pieces:
        steps = jnp.exp(jax.random.uniform(jax.random.fold_in(own, position), (blocks,), jnp.float32, low / len(pieces), top_value / len(pieces)))
        gain = gain * jnp.repeat(steps, shape[position] // blocks).reshape([-1 if axis == position else 1 for axis in range(len(shape))])
    return gain


def length_profile(amount, total, most, lean):
    portions = [(1 << 20) // math.isqrt(standing ** lean) + 1 for standing in range(2, amount + 1)]
    surplus, counts = total - most - (amount - 1), [1] * (amount - 1)
    while surplus > 0:
        candidates = [i for i in range(amount - 1) if counts[i] < most]
        pool, budget = sum([portions[i] for i in candidates]), surplus
        for i in candidates:
            addition = min(most - counts[i], max(1, budget * portions[i] // pool), surplus)
            counts[i] = counts[i] + addition
            surplus = surplus - addition
    return np.array([most] + counts)


def uneven(stream_key, count, total, most, slope):
    if count == 2:
        one = jax.random.randint(stream_key, (), max(1, total - most), min(most, total - 1) + 1)
        return jnp.stack([one, total - one])
    tallies = jnp.asarray(length_profile(count, total, most, slope), jnp.int32)
    pairs = (count - 1) // 2
    source_of, taker = tallies[1:1 + 2 * pairs:2], tallies[2:2 + 2 * pairs:2]
    slack = jnp.minimum(source_of - 1, most - taker)
    shifted = jax.random.randint(jax.random.fold_in(stream_key, 1), (pairs,), 0, 1 << 20) % (slack + 1)
    tallies = tallies.at[1:1 + 2 * pairs:2].set(source_of - shifted).at[2:2 + 2 * pairs:2].set(taker + shifted)
    return tallies[jax.random.permutation(jax.random.fold_in(stream_key, 2), count)]


def noise(rng, extent, spread, limit, cuts=(), held_as=jnp.bfloat16):
    loudness = steps_of(rng, extent, cuts, -0.22, 0.18) if cuts else 1.0
    entries = jax.random.normal(rng, extent, jnp.float32) * spread * loudness
    return jnp.minimum(jnp.maximum(entries, -limit), limit).astype(held_as)


def setup_inputs(seed: int = 0) -> dict:
    key_list = jax.random.split(jax.random.key(seed), 12)
    rhs = noise(key_list[0], (CELLS,), 1.0, 6.0, ((0, 32),), jnp.float32)
    fine_values = draw_fine_values(jax.random.fold_in(key_list[11], 71), 0)
    fine_columns = draw_fine_columns(jax.random.fold_in(key_list[11], 71), 0)
    smoother = draw_smoother(jax.random.fold_in(key_list[11], 71), 0)
    reaction = jnp.clip(jnp.exp(math.log(2.0) - 2.3025851 * jax.random.uniform(key_list[4], (CELLS,), jnp.float32) ** steps_of(key_list[4], (CELLS,), ((0, 32),), -0.2, 0.2)), 0.2, 2.0)
    pit_counts = uneven(key_list[5], SECTIONS, SECTIONS + AGGS // 4, AGG_DEV, 2).astype(jnp.int32)
    weights = jnp.clip(jnp.exp(math.log(0.4) - 2.3025851 * jax.random.uniform(key_list[6], (CELLS,), jnp.float32) ** steps_of(key_list[6], (CELLS,), ((0, 32),), -0.2, 0.2)), 0.04, 0.4)
    coarse_order = jax.random.permutation(key_list[7], AGGS).astype(jnp.int32)
    coarse_values = draw_coarse_values(jax.random.fold_in(key_list[11], 71), 0)
    coarse_rows = draw_coarse_rows(jax.random.fold_in(key_list[11], 71), 0)
    coarse_inverse = draw_coarse_inverse(jax.random.fold_in(key_list[11], 71), 0)
    return dict(rhs=rhs, fine_values=fine_values, fine_columns=fine_columns, smoother=smoother, reaction=reaction, pit_counts=pit_counts, weights=weights, coarse_order=coarse_order, coarse_values=coarse_values, coarse_rows=coarse_rows, coarse_inverse=coarse_inverse)


def smooth_all(input_vector, smoother):
    inverse_f = smoother.astype(jnp.float32).reshape(AGGREGATE_CELLS, AGGS, AGGREGATE_CELLS)
    return jnp.einsum("oni,ni->no", inverse_f, input_vector.reshape(AGGS, AGGREGATE_CELLS), precision=lax.Precision.HIGHEST).reshape(-1)


def fine_apply(input_vector, fine_values, fine_columns, pit_react):
    padded = jnp.pad(input_vector.reshape(AGGS, AGGREGATE_CELLS), ((HALO, HALO), (0, 0)))

    def section(number):
        start = (number * AGG_DEV).astype(jnp.int32)
        columns = lax.dynamic_slice_in_dim(fine_columns, start, AGG_DEV, 1)
        picked = padded[start + columns]
        fine_value_entries = lax.dynamic_slice_in_dim(fine_values, start * AGGREGATE_CELLS, AGG_DEV * AGGREGATE_CELLS, 2)
        fine_value_entries = fine_value_entries.astype(jnp.float32).reshape(FINE_NBRS, AGGREGATE_CELLS, AGG_DEV, AGGREGATE_CELLS)
        return jnp.einsum("kobi,kbi->bo", fine_value_entries, picked, precision=lax.Precision.HIGHEST).reshape(-1)

    result = lax.map(section, jnp.arange(SECTIONS, dtype=jnp.int32)).reshape(-1)
    return result + pit_react * input_vector


def coarse_scale(input_vector, coarse_inverse):
    inverse_f = coarse_inverse.astype(jnp.float32).reshape(AGGREGATE_CELLS, COARSE_GROUPS, AGGREGATE_CELLS)
    return jnp.einsum("oji,ji->jo", inverse_f, input_vector.reshape(COARSE_GROUPS, AGGREGATE_CELLS), precision=lax.Precision.HIGHEST).reshape(-1)


def coarse_apply(input_vector, coarse_values, coarse_rows):
    fine_value_entries = coarse_values.astype(jnp.float32).reshape(COARSE_NBRS, AGGREGATE_CELLS, COARSE_GROUPS, AGGREGATE_CELLS)
    block_product = jnp.einsum("vfmd,md->vfm", fine_value_entries, input_vector.reshape(COARSE_GROUPS, AGGREGATE_CELLS), precision=lax.Precision.HIGHEST)
    dof_rows = coarse_rows[:, None, :] * AGGREGATE_CELLS + jnp.arange(AGGREGATE_CELLS, dtype=jnp.int32)[None, :, None]
    return jax.ops.segment_sum(block_product.reshape(-1), dof_rows.reshape(-1).astype(jnp.int32), num_segments=AGGS)


def reference(rhs, fine_values, fine_columns, smoother, reaction, pit_counts, weights, coarse_order, coarse_values, coarse_rows, coarse_inverse):
    agg_ids = jnp.arange(AGGS, dtype=jnp.int32)
    pit_aggs = (agg_ids % AGG_DEV < pit_counts[agg_ids // AGG_DEV]).astype(jnp.float32)
    pit_react = jnp.repeat(pit_aggs, AGGREGATE_CELLS) * reaction
    smoothed = smooth_all(rhs, smoother)
    residual = rhs - fine_apply(smoothed, fine_values, fine_columns, pit_react)
    restricted = jnp.sum((weights * residual).reshape(AGGS, AGGREGATE_CELLS), axis=1)
    coarse_right_side = jax.ops.segment_sum(restricted, coarse_order, num_segments=AGGS)
    correction = coarse_scale(coarse_right_side, coarse_inverse)
    for sweep_no in range(SWEEPS - 1):
        image_all = coarse_apply(correction, coarse_values, coarse_rows)
        correction = correction + coarse_scale(coarse_right_side - image_all, coarse_inverse)
    corrected = smoothed + weights * jnp.repeat(correction[coarse_order], AGGREGATE_CELLS)
    solution = corrected + smooth_all(rhs - fine_apply(corrected, fine_values, fine_columns, pit_react), smoother)
    return (solution, correction)
```

```python
import functools

import jax
import jax.numpy as jnp
from jax import lax
from jax.experimental import pallas as pl
from jax.experimental.pallas import tpu as pltpu
from jax.sharding import PartitionSpec as P

CELLS = 64
LANES = 128
HALO_ROWS = 8
SWEEPS = 4
BOTH = ("fine", "coarse")
f32, bf16, i32 = jnp.float32, jnp.bfloat16, jnp.int32
VMEM_LIMIT = 24 * 1024 * 1024


def iota(shape, axis):
    return lax.broadcasted_iota(i32, shape, axis)


def split(x):
    high = x.astype(bf16)
    return high, (x - high.astype(f32)).astype(bf16)


def dot(a, b):
    return lax.dot_general(a, b, (((1,), (0,)), ((), ())), preferred_element_type=f32)


def dot_t(a, b):
    return lax.dot_general(a, b, (((1,), (1,)), ((), ())), preferred_element_type=f32)


def cell_sums(high_ref, low_ref):
    width = high_ref.shape[1]
    pairs = width // LANES
    row, lane = iota((2 * pairs, width), 0), iota((2 * pairs, width), 1)
    member = (lane // CELLS == 2 * (row % pairs) + row // pairs).astype(bf16)
    sums = dot_t(member, high_ref[...]) + dot_t(member, low_ref[...])
    return jnp.concatenate([sums[:pairs], sums[pairs:]], axis=1)


def apply_smoother(vector, smoother_ref, high_ref, low_ref):
    for p in range(vector.shape[0]):
        cols = pl.ds(p * LANES, LANES)
        product = smoother_ref[:, cols].astype(f32) * vector[p : p + 1, :]
        high_ref[:, cols], low_ref[:, cols] = split(product)
    return cell_sums(high_ref, low_ref)


def apply_fine(window, fine_ref, columns_ref, picked_ref, high_ref, low_ref):
    nbrs, _, width = fine_ref.shape
    pairs = width // LANES
    rows = window.shape[0]
    both = jnp.concatenate([window, pltpu.roll(window, CELLS, 1)], axis=0)
    high, low = split(both)
    table = jnp.concatenate([high, low], axis=0)
    aggs = columns_ref.shape[1]
    at, who = iota((pairs, aggs), 1), iota((pairs, aggs), 0)
    entry = iota((pairs, 4 * rows), 1) % (2 * rows)
    halves = []
    for half in range(2):
        parts = []
        for k in range(nbrs):
            chosen = jnp.where(at == 2 * who + half, columns_ref[k : k + 1, :].astype(f32), 0.0)
            block = jnp.sum(chosen, axis=1, keepdims=True).astype(i32)
            place = block // 2 + jnp.where(block % 2 == half, 0, rows)
            parts.append((entry == place).astype(bf16))
        halves.append(dot(jnp.concatenate(parts, axis=0), table))
    lane = iota(halves[0].shape, 1)
    picked_ref[...] = jnp.where(lane < CELLS, halves[0], halves[1])
    for p in range(pairs):
        cols = pl.ds(p * LANES, LANES)
        total = None
        for k in range(nbrs):
            term = fine_ref[k, :, cols].astype(f32) * picked_ref[pl.ds(k * pairs + p, 1), :]
            total = term if total is None else total + term
        high_ref[:, cols], low_ref[:, cols] = split(total)
    return cell_sums(high_ref, low_ref)


def as_columns(row, pairs):
    shape = (pairs, row.shape[1])
    at, who = iota(shape, 1), iota(shape, 0)
    return [
        jnp.sum(jnp.where(at == 2 * who + half, row, 0.0), axis=1, keepdims=True)
        for half in range(2)
    ]


def by_half(columns, shape):
    return jnp.where(iota(shape, 1) < CELLS, columns[0], columns[1])


def start_kernel(rhs_ref, weights_ref, order_ref, smoother_ref, near_ref, onward_ref, own_ref, high_ref, low_ref):
    pairs = rhs_ref.shape[0]
    smoothed = apply_smoother(rhs_ref[...], smoother_ref, high_ref, low_ref)
    order = by_half(as_columns(order_ref[...].astype(f32), pairs), (pairs, LANES))
    even = lax.axis_index("coarse") % 2 == 0
    for i, part in enumerate((smoothed, weights_ref[...], order)):
        own_ref[i] = part
        bottom, top = part[:HALO_ROWS], part[pairs - HALO_ROWS :]
        near_ref[i] = jnp.where(even, top, bottom)
        onward_ref[i] = jnp.where(even, bottom, top)


def window_of(near_ref, far_ref, own_ref, device, devices):
    even = device % 2 == 0
    near, far = near_ref[...], far_ref[...]
    low = jnp.where(device == 0, 0.0, jnp.where(even, far, near))
    high = jnp.where(device == devices - 1, 0.0, jnp.where(even, near, far))
    return [jnp.concatenate([low[i], own_ref[i], high[i]], axis=0) for i in range(3)]


def device_index():
    return lax.axis_index("fine") * lax.axis_size("coarse") + lax.axis_index("coarse")


def reaction_of(reaction_ref, counts_ref):
    shape = reaction_ref.shape
    agg = 2 * iota(shape, 0) + iota(shape, 1) // CELLS
    return jnp.where(agg < counts_ref[0], reaction_ref[...], 0.0)


def residual_kernel(
    devices, counts_ref, near_ref, far_ref, own_ref, rhs_ref, reaction_ref, columns_ref, fine_ref,
    out_ref, picked_ref, high_ref, low_ref,
):
    smoothed, _, _ = window_of(near_ref, far_ref, own_ref, device_index(), devices)
    image = apply_fine(smoothed, fine_ref, columns_ref, picked_ref, high_ref, low_ref)
    image = image + reaction_of(reaction_ref, counts_ref) * own_ref[0]
    weighted = own_ref[1] * (rhs_ref[...] - image)
    pairs = weighted.shape[0]
    shape = (pairs, LANES)
    lane, who = iota(shape, 1), iota(shape, 0)
    row = jnp.zeros((1, LANES), f32)
    for half in range(2):
        inside = lane // CELLS == half
        restricted = jnp.sum(jnp.where(inside, weighted, 0.0), axis=1, keepdims=True)
        order = jnp.max(jnp.where(inside, own_ref[2], 0.0), axis=1, keepdims=True)
        spread = jnp.where(lane == 2 * who + half, restricted, 0.0)
        spread = spread + jnp.where(lane == 2 * (pairs + who) + half, order, 0.0)
        row = row + jnp.sum(spread, axis=0, keepdims=True)
    out_ref[...] = jnp.broadcast_to(row, out_ref.shape)


def finish(corr, own_ref, window, rhs_ref, reaction_ref, counts_ref, columns_ref, fine_ref, smoother_ref,
           out_ref, picked_ref, high_ref, low_ref):
    smoothed, weights, _ = window
    corrected = smoothed + weights * corr
    pairs = rhs_ref.shape[0]
    mine = corrected[HALO_ROWS : HALO_ROWS + pairs]
    image = apply_fine(corrected, fine_ref, columns_ref, picked_ref, high_ref, low_ref)
    image = image + reaction_of(reaction_ref, counts_ref) * mine
    out_ref[...] = mine + apply_smoother(rhs_ref[...] - image, smoother_ref, high_ref, low_ref)


def pack_kernel(rows_ref, values_ref, inverse_ref, out_ref):
    nbrs, own_blocks = rows_ref.shape
    deep = values_ref.shape[0]
    out_ref[pl.ds(0, deep), :] = values_ref[...].astype(f32)
    out_ref[pl.ds(deep, CELLS), :] = inverse_ref[...].astype(f32)
    shape = (8, out_ref.shape[1])
    lane = iota(shape, 1)
    rows = jnp.zeros(shape, f32)
    for k in range(nbrs):
        for j in range(own_blocks):
            here = (lane // 32 == k) & (lane % 16 == j)
            rows = jnp.where(here, rows_ref[k, j].astype(f32), rows)
    out_ref[pl.ds(deep + CELLS, 8), :] = rows


def solve_kernel(
    devices, counts_ref, gathered_ref, near_ref, far_ref, own_ref, rhs_ref, reaction_ref, columns_ref, fine_ref,
    smoother_ref, part0_ref, part1_ref, part2_ref, part3_ref,
    out_ref, correction_ref, blocks_ref, inverse_ref, picked_ref, high_ref, low_ref,
):
    part_refs = (part0_ref, part1_ref, part2_ref, part3_ref)
    me = lax.axis_index("coarse")
    parts = len(part_refs)
    width = part0_ref.shape[1]
    own_blocks = width // CELLS
    groups = parts * own_blocks
    unknowns = groups * CELLS
    nbrs = (part0_ref.shape[0] - 8) // CELLS - 1
    deep = nbrs * CELLS
    for i, ref in enumerate(part_refs):
        blocks_ref[i] = ref[pl.ds(0, deep), :].astype(bf16)
        inverse_ref[i] = ref[pl.ds(deep, CELLS), :].astype(bf16)

    def place(group):
        return jnp.bitwise_xor(group // own_blocks, me) * own_blocks + group % own_blocks

    lane = iota((1, width), 1)
    target = jnp.zeros((1, width), f32)
    for i, ref in enumerate(part_refs):
        rows = ref[pl.ds(deep + CELLS, 8), :][0:1, :]
        rows = jnp.where((lane % 16 < own_blocks) & (lane < 32 * nbrs), rows, 0.0)
        target = target + (rows if i == 0 else pltpu.roll(rows, i * own_blocks, 1))
    target = place(target.astype(i32))
    scatter = ((iota((groups, width), 0) == target) & (lane < 32 * nbrs)).astype(bf16)[:, : 32 * nbrs]

    gathered = gathered_ref[...]
    devs = gathered.shape[0]
    lane = iota((8, LANES), 1)
    lefts, rights = [], []
    for start in range(0, devs, 32):
        value = jnp.zeros((8, LANES), f32)
        order = jnp.zeros((8, LANES), f32)
        for i in range(4):
            piece = gathered[start + 8 * i : start + 8 * i + 8]
            here = lane // 32 == i
            value = jnp.where(here, pltpu.roll(piece, 32 * i, 1) if i else piece, value)
            order = jnp.where(here, pltpu.roll(piece, (32 * i + 96) % LANES, 1) if i != 1 else piece, order)
        order = order.astype(i32)
        group, unit = place(order // CELLS), order % CELLS
        for s in range(8):
            left = jnp.where(iota((groups, LANES), 0) == group[s : s + 1], value[s : s + 1], 0.0)
            lefts.append(jnp.concatenate(split(left), axis=0))
            rights.append((iota((CELLS, LANES), 0) == unit[s : s + 1]).astype(bf16))
    right_side = dot_t(jnp.concatenate(lefts, axis=1), jnp.concatenate(rights, axis=1))
    right_side = right_side[:groups] + right_side[groups:]

    own_block = iota((groups, unknowns), 1) // CELLS == iota((groups, unknowns), 0)

    def spread(x):
        wide = jnp.concatenate([x] * (LANES // CELLS), axis=1)
        wide = jnp.concatenate([wide] * (unknowns // LANES), axis=1)
        return jnp.concatenate(split(jnp.where(own_block, wide, 0.0)), axis=0)

    def product(x, ref):
        wide = spread(x)
        total = None
        for i in range(parts):
            term = dot_t(wide[:, i * width : (i + 1) * width], ref[i])
            total = term if total is None else total + term
        return total[:groups] + total[groups:]

    correction = product(right_side, inverse_ref)
    for _ in range(SWEEPS - 1):
        sums = product(correction, blocks_ref)
        pieces = []
        for k in range(nbrs):
            pieces += split(sums[:, k * CELLS : (k + 1) * CELLS])
        image = jnp.zeros((groups, CELLS), f32)
        high, low = pieces[0::2], pieces[1::2]
        stacked = jnp.concatenate([p for pair in zip(high, low) for p in pair], axis=0)
        image = dot(scatter, stacked)
        correction = correction + product(right_side - image, inverse_ref)
    correction_ref[...] = correction[:own_blocks]

    window = window_of(near_ref, far_ref, own_ref, device_index(), devices)
    order = window[2].astype(i32)
    rows = order.shape[0]
    unit = jnp.concatenate([order[:, :CELLS], order[:, CELLS:]], axis=0)
    pick = (iota(unit.shape, 1) == unit % CELLS).astype(bf16)
    values = dot_t(pick, jnp.concatenate(split(correction), axis=0))
    group = place(unit[:, : 2 * groups] // CELLS)
    values = jnp.sum(jnp.where(iota(values.shape, 1) % groups == group, values, 0.0), axis=1, keepdims=True)
    corr = by_half([values[:rows], values[rows:]], (rows, LANES))
    finish(corr, own_ref, window, rhs_ref, reaction_ref, counts_ref, columns_ref, fine_ref, smoother_ref,
           out_ref, picked_ref, high_ref, low_ref)


def finish_kernel(
    devices, counts_ref, corr_ref, near_ref, far_ref, own_ref, rhs_ref, reaction_ref, columns_ref, fine_ref,
    smoother_ref, out_ref, picked_ref, high_ref, low_ref,
):
    window = window_of(near_ref, far_ref, own_ref, device_index(), devices)
    finish(corr_ref[...], own_ref, window, rhs_ref, reaction_ref, counts_ref, columns_ref, fine_ref, smoother_ref,
           out_ref, picked_ref, high_ref, low_ref)


def call(kernel, out_shape, smem=(), scratch=(), count=0):
    specs = [pl.BlockSpec(memory_space=pltpu.SMEM if i in smem else pltpu.VMEM) for i in range(count)]
    return pl.pallas_call(
        kernel,
        out_shape=out_shape,
        in_specs=specs,
        out_specs=jax.tree.map(lambda _: pl.BlockSpec(memory_space=pltpu.VMEM), out_shape),
        scratch_shapes=list(scratch),
        compiler_params=pltpu.CompilerParams(vmem_limit_bytes=VMEM_LIMIT),
    )


def shape_of(*dims):
    return jax.ShapeDtypeStruct(dims, f32)


def coarse_by_parts(restricted, coarse_order, coarse_values, coarse_rows, coarse_inverse):
    own = coarse_inverse.shape[1]
    own_blocks = own // CELLS
    total = own * lax.axis_size("coarse")
    start = lax.axis_index("coarse") * own
    side = jnp.zeros((total,), f32).at[coarse_order].add(restricted)
    side = lax.dynamic_slice_in_dim(lax.psum(side, BOTH), start, own)
    values = coarse_values.astype(f32).reshape(-1, CELLS, own_blocks, CELLS)
    inverse = coarse_inverse.astype(f32).reshape(CELLS, own_blocks, CELLS)

    def scale(x):
        x = x.reshape(own_blocks, CELLS)
        return jnp.einsum("oji,ji->jo", inverse, x, precision=lax.Precision.HIGHEST).reshape(-1)

    correction = scale(side)
    for _ in range(SWEEPS - 1):
        x = correction.reshape(own_blocks, CELLS)
        sums = jnp.einsum("vfmd,md->vmf", values, x, precision=lax.Precision.HIGHEST)
        image = jax.ops.segment_sum(
            sums.reshape(-1, CELLS), coarse_rows.reshape(-1), num_segments=total // CELLS
        ).reshape(-1)
        image = lax.dynamic_slice_in_dim(lax.psum(image, "coarse"), start, own)
        correction = correction + scale(side - image)
    return correction, lax.all_gather(correction, "coarse", axis=0, tiled=True)


def shards(
    devices, rhs, fine_values, fine_columns, smoother, reaction, pit_counts, weights, coarse_order,
    coarse_values, coarse_rows, coarse_inverse,
):
    cells = rhs.shape[0]
    pairs = cells // LANES
    aggs = 2 * pairs
    nbrs = fine_columns.shape[0]
    parts = lax.axis_size("coarse")
    rhs, reaction, weights = (x.reshape(pairs, LANES) for x in (rhs, reaction, weights))
    rows = pairs + 2 * HALO_ROWS
    products = [pltpu.VMEM((CELLS, cells), bf16)] * 2
    scratch = [pltpu.VMEM((nbrs * pairs, LANES), f32)] + products
    edge = shape_of(3, HALO_ROWS, LANES)

    near, onward, own = call(
        start_kernel, (edge, edge, shape_of(3, pairs, LANES)), scratch=products, count=4
    )(rhs, weights, coarse_order.reshape(1, aggs), smoother)

    partner = [(d, d ^ 1) for d in range(devices)]
    chain = []
    for d in range(devices):
        target = d + 2 if d % 2 == 0 else d - 2
        chain.append((d, target if 0 <= target < devices else d ^ 1))
    far = lax.ppermute(lax.ppermute(onward, BOTH, partner), BOTH, chain)
    near = lax.ppermute(near, BOTH, partner)

    copied = parts == 4 and devices % 32 == 0 and devices <= 64
    if copied:
        deep = coarse_values.shape[0] * CELLS
        width = coarse_inverse.shape[1]
        packed = call(pack_kernel, shape_of(deep + CELLS + 8, width), smem=(0,), count=3)(
            coarse_rows, coarse_values.reshape(deep, width), coarse_inverse
        )
        other = lax.ppermute(packed, "coarse", [(c, c ^ 2) for c in range(parts)])
        swap = [(c, c ^ 1) for c in range(parts)]
        pieces = (packed, lax.ppermute(packed, "coarse", swap), other, lax.ppermute(other, "coarse", swap))

    sent = call(
        functools.partial(residual_kernel, devices), shape_of(devices, LANES), smem=(0,), scratch=scratch, count=8
    )(pit_counts, near, far, own, rhs, reaction, fine_columns, fine_values)

    common = (near, far, own, rhs, reaction, fine_columns, fine_values, smoother)
    if copied:
        gathered = lax.all_to_all(sent, BOTH, 0, 0, tiled=True)
        result, correction = call(
            functools.partial(solve_kernel, devices),
            (shape_of(pairs, LANES), shape_of(width // CELLS, CELLS)),
            smem=(0,),
            scratch=[pltpu.VMEM((parts, deep, width), bf16), pltpu.VMEM((parts, CELLS, width), bf16)] + scratch,
            count=14,
        )(pit_counts, gathered, *common, *pieces)
        correction = correction.reshape(-1)
    else:
        correction, everywhere = coarse_by_parts(
            sent[0, :aggs], coarse_order, coarse_values, coarse_rows, coarse_inverse
        )
        index = device_index()
        low = jnp.where(index == 0, 0.0, jnp.where(index % 2 == 0, far[2], near[2]))
        high = jnp.where(index == devices - 1, 0.0, jnp.where(index % 2 == 0, near[2], far[2]))
        order = jnp.concatenate([low, own[2], high], axis=0).astype(i32)
        corr = jnp.repeat(everywhere[order[:, ::CELLS]], CELLS, axis=1)
        result = call(
            functools.partial(finish_kernel, devices), shape_of(pairs, LANES), smem=(0,), scratch=scratch, count=10
        )(pit_counts, corr, *common)
    return result.reshape(-1), correction


def solution(mesh):
    devices = mesh.shape["fine"] * mesh.shape["coarse"]
    in_specs = (
        P(BOTH),
        P(None, None, BOTH),
        P(None, BOTH),
        P(None, BOTH),
        P(BOTH),
        P(BOTH),
        P(BOTH),
        P(BOTH),
        P(None, None, "coarse"),
        P(None, "coarse"),
        P(None, "coarse"),
    )
    return jax.shard_map(
        functools.partial(shards, devices),
        mesh=mesh,
        in_specs=in_specs,
        out_specs=(P(BOTH), P("coarse")),
        check_vma=False,
    )
```

```python
import functools

import jax
import jax.numpy as jnp
from jax import lax
from jax.experimental import pallas as pl
from jax.experimental.pallas import tpu as pltpu
from jax.sharding import PartitionSpec as P

CELLS = 64
LANES = 128
HALO_ROWS = 8
SWEEPS = 4
BOTH = ("fine", "coarse")
f32, bf16, i32 = jnp.float32, jnp.bfloat16, jnp.int32
VMEM_LIMIT = 24 * 1024 * 1024


def iota(shape, axis):
    return lax.broadcasted_iota(i32, shape, axis)


def split(x):
    high = x.astype(bf16)
    return high, (x - high.astype(f32)).astype(bf16)


def dot(a, b):
    return lax.dot_general(a, b, (((1,), (0,)), ((), ())), preferred_element_type=f32)


def dot_t(a, b):
    return lax.dot_general(a, b, (((1,), (1,)), ((), ())), preferred_element_type=f32)


def cell_sums(high_ref, low_ref):
    width = high_ref.shape[1]
    pairs = width // LANES
    row, lane = iota((2 * pairs, width), 0), iota((2 * pairs, width), 1)
    member = (lane // CELLS == 2 * (row % pairs) + row // pairs).astype(bf16)
    sums = dot_t(member, high_ref[...]) + dot_t(member, low_ref[...])
    return jnp.concatenate([sums[:pairs], sums[pairs:]], axis=1)


def apply_smoother(vector, smoother_ref, high_ref, low_ref):
    for p in range(vector.shape[0]):
        cols = pl.ds(p * LANES, LANES)
        product = smoother_ref[:, cols].astype(f32) * vector[p : p + 1, :]
        high_ref[:, cols], low_ref[:, cols] = split(product)
    return cell_sums(high_ref, low_ref)


def selection(columns, half_rows, pairs):
    nbrs, aggs = columns.shape
    at, who = iota((pairs, aggs), 1), iota((pairs, aggs), 0)
    entry = iota((pairs, 4 * half_rows), 1) % (2 * half_rows)
    parts = []
    for half in range(2):
        for k in range(nbrs):
            chosen = jnp.where(at == 2 * who + half, columns[k : k + 1].astype(f32), 0.0)
            block = jnp.sum(chosen, axis=1, keepdims=True).astype(i32)
            place = block // 2 + jnp.where(block % 2 == half, 0, half_rows)
            parts.append((entry == place).astype(bf16))
    return jnp.concatenate(parts, axis=0)


def pick(window, selected):
    high, low = split(jnp.concatenate([window, pltpu.roll(window, CELLS, 1)], axis=0))
    picked = dot(selected, jnp.concatenate([high, low], axis=0))
    count = selected.shape[0] // 2
    lane = iota((count, LANES), 1)
    return jnp.where(lane < CELLS, picked[:count], picked[count:])


def apply_fine(window, fine_ref, selected, picked_ref, high_ref, low_ref):
    nbrs, _, width = fine_ref.shape
    pairs = width // LANES
    picked_ref[...] = pick(window, selected)
    for p in range(pairs):
        cols = pl.ds(p * LANES, LANES)
        total = None
        for k in range(nbrs):
            term = fine_ref[k, :, cols].astype(f32) * picked_ref[pl.ds(k * pairs + p, 1), :]
            total = term if total is None else total + term
        high_ref[:, cols], low_ref[:, cols] = split(total)
    return cell_sums(high_ref, low_ref)


def as_columns(row, pairs):
    shape = (pairs, row.shape[1])
    at, who = iota(shape, 1), iota(shape, 0)
    return [
        jnp.sum(jnp.where(at == 2 * who + half, row, 0.0), axis=1, keepdims=True)
        for half in range(2)
    ]


def by_half(columns, shape):
    return jnp.where(iota(shape, 1) < CELLS, columns[0], columns[1])


def fetch(sem_ref, *pairs):
    copies = [pltpu.make_async_copy(src, dst, sem_ref.at[i]) for i, (src, dst) in enumerate(pairs)]
    for copy in copies:
        copy.start()
    return copies


def start_kernel(
    rhs_any, weights_any, order_any, smoother_any, near_ref, onward_ref, own_ref,
    rhs_ref, weights_ref, order_ref, smoother_ref, high_ref, low_ref, sem_ref,
):
    copies = fetch(
        sem_ref, (smoother_any, smoother_ref), (rhs_any, rhs_ref), (weights_any, weights_ref), (order_any, order_ref)
    )
    for copy in copies:
        copy.wait()
    pairs = rhs_ref.shape[0]
    smoothed = apply_smoother(rhs_ref[...], smoother_ref, high_ref, low_ref)
    order = by_half(as_columns(order_ref[...].astype(f32), pairs), (pairs, LANES))
    even = lax.axis_index("coarse") % 2 == 0
    for i, part in enumerate((smoothed, weights_ref[...], order)):
        own_ref[i] = part
        bottom, top = part[:HALO_ROWS], part[pairs - HALO_ROWS :]
        near_ref[i] = jnp.where(even, top, bottom)
        onward_ref[i] = jnp.where(even, bottom, top)


def window_of(near_ref, far_ref, own_ref, device, devices):
    even = device % 2 == 0
    near, far = near_ref[...], far_ref[...]
    low = jnp.where(device == 0, 0.0, jnp.where(even, far, near))
    high = jnp.where(device == devices - 1, 0.0, jnp.where(even, near, far))
    return [jnp.concatenate([low[i], own_ref[i], high[i]], axis=0) for i in range(3)]


def device_index():
    return lax.axis_index("fine") * lax.axis_size("coarse") + lax.axis_index("coarse")


def prepare_kernel(
    counts_ref, own_ref, rhs_any, reaction_any, columns_any, fine_any, selected_ref, weighed_ref, local_ref,
    rhs_ref, reaction_ref, columns_ref, fine_ref, wide_ref, sem_ref,
):
    copies = fetch(
        sem_ref, (fine_any, fine_ref), (columns_any, columns_ref), (rhs_any, rhs_ref), (reaction_any, reaction_ref)
    )
    for copy in copies[1:]:
        copy.wait()
    pairs = rhs_ref.shape[0]
    nbrs, _, width = fine_ref.shape
    weights = own_ref[1]
    agg = 2 * iota((pairs, LANES), 0) + iota((pairs, LANES), 1) // CELLS
    reaction = jnp.where(agg < counts_ref[0], reaction_ref[...], 0.0)
    local_ref[0] = weights * rhs_ref[...]
    local_ref[1] = weights * reaction
    local_ref[2] = rhs_ref[...]
    local_ref[3] = reaction
    selected_ref[...] = selection(columns_ref[...], pairs + 2 * HALO_ROWS, pairs)
    by_agg = jnp.concatenate([weights[:, :CELLS], weights[:, CELLS:]], axis=0)
    row, lane = iota((2 * pairs, width), 0), iota((2 * pairs, width), 1)
    member = (lane // CELLS == 2 * (row % pairs) + row // pairs).astype(bf16)
    wide = None
    for part in split(by_agg):
        term = lax.dot_general(part, member, (((0,), (0,)), ((), ())), preferred_element_type=f32)
        wide = term if wide is None else wide + term
    wide_ref[...] = wide
    copies[0].wait()
    for p in range(pairs):
        cols = pl.ds(p * LANES, LANES)
        scale = wide_ref[:, cols]
        for k in range(nbrs):
            term = fine_ref[k, :, cols].astype(f32) * scale
            total = term[:8]
            for r in range(8, CELLS, 8):
                total = total + term[r : r + 8]
            weighed_ref[k * pairs + p] = total


def residual_kernel(
    devices, near_ref, far_ref, own_ref, selected_ref, weighed_ref, local_ref, out_ref, picked_ref,
):
    smoothed, _, _ = window_of(near_ref, far_ref, own_ref, device_index(), devices)
    picked_ref[...] = pick(smoothed, selected_ref[...])
    pairs = own_ref.shape[1]
    nbrs = picked_ref.shape[0] // pairs
    images = []
    for p in range(pairs):
        total = None
        for k in range(nbrs):
            term = weighed_ref[k * pairs + p] * picked_ref[pl.ds(k * pairs + p, 1), :]
            total = term if total is None else total + term
        images.append(jnp.sum(total, axis=0, keepdims=True))
    weighted = local_ref[0] - local_ref[1] * own_ref[0] - jnp.concatenate(images, axis=0)
    shape = (pairs, LANES)
    lane, who = iota(shape, 1), iota(shape, 0)
    row = jnp.zeros((1, LANES), f32)
    for half in range(2):
        inside = lane // CELLS == half
        restricted = jnp.sum(jnp.where(inside, weighted, 0.0), axis=1, keepdims=True)
        order = jnp.max(jnp.where(inside, own_ref[2], 0.0), axis=1, keepdims=True)
        spread = jnp.where(lane == 2 * who + half, restricted, 0.0)
        spread = spread + jnp.where(lane == 2 * (pairs + who) + half, order, 0.0)
        row = row + jnp.sum(spread, axis=0, keepdims=True)
    out_ref[...] = jnp.broadcast_to(row, out_ref.shape)


def finish(corr, near_ref, far_ref, own_ref, local_ref, devices, selected_ref, fine_ref, smoother_ref, result_ref,
           picked_ref, high_ref, low_ref):
    smoothed, weights, _ = window_of(near_ref, far_ref, own_ref, device_index(), devices)
    corrected = smoothed + weights * corr
    pairs = own_ref.shape[1]
    mine = corrected[HALO_ROWS : HALO_ROWS + pairs]
    image = apply_fine(corrected, fine_ref, selected_ref[...], picked_ref, high_ref, low_ref)
    image = image + local_ref[3] * mine
    result_ref[...] = mine + apply_smoother(local_ref[2] - image, smoother_ref, high_ref, low_ref)


def pack_kernel(rows_any, values_any, inverse_any, out_ref, rows_ref, values_ref, inverse_ref, sem_ref):
    copies = fetch(sem_ref, (values_any, values_ref), (inverse_any, inverse_ref), (rows_any, rows_ref))
    for copy in copies:
        copy.wait()
    own_blocks, nbrs = rows_ref.shape
    deep, width = values_ref.shape
    out_ref[pl.ds(0, deep), :] = values_ref[...].astype(f32)
    out_ref[pl.ds(deep, CELLS), :] = inverse_ref[...].astype(f32)
    lane, block = iota((own_blocks, width), 1), iota((own_blocks, width), 0)
    rows = jnp.zeros((own_blocks, width), f32)
    for k in range(nbrs):
        here = (lane // 32 == k) & (lane % 16 == block)
        rows = jnp.where(here, rows_ref[:, k : k + 1].astype(f32), rows)
    out_ref[pl.ds(deep + CELLS, 8), :] = jnp.broadcast_to(jnp.sum(rows, axis=0, keepdims=True), (8, width))


def solve_kernel(
    devices, gathered_ref, near_ref, far_ref, own_ref, selected_ref, local_ref,
    part0_ref, part1_ref, part2_ref, part3_ref, fine_any, smoother_any,
    out_any, correction_any,
    blocks_ref, inverse_ref, result_ref, correction_ref,
    fine_ref, smoother_ref, picked_ref, high_ref, low_ref, sem_ref, out_sem_ref,
):
    copies = fetch(sem_ref, (fine_any, fine_ref), (smoother_any, smoother_ref))
    part_refs = (part0_ref, part1_ref, part2_ref, part3_ref)
    me = lax.axis_index("coarse")
    parts = len(part_refs)
    width = part0_ref.shape[1]
    own_blocks = width // CELLS
    groups = parts * own_blocks
    unknowns = groups * CELLS
    nbrs = (part0_ref.shape[0] - 8) // CELLS - 1
    deep = nbrs * CELLS
    for i, ref in enumerate(part_refs):
        blocks_ref[i] = ref[pl.ds(0, deep), :].astype(bf16)
        inverse_ref[i] = ref[pl.ds(deep, CELLS), :].astype(bf16)

    def place(group):
        return jnp.bitwise_xor(group // own_blocks, me) * own_blocks + group % own_blocks

    lane = iota((1, width), 1)
    target = jnp.zeros((1, width), f32)
    for i, ref in enumerate(part_refs):
        rows = ref[pl.ds(deep + CELLS, 8), :][0:1, :]
        rows = jnp.where((lane % 16 < own_blocks) & (lane < 32 * nbrs), rows, 0.0)
        target = target + (rows if i == 0 else pltpu.roll(rows, i * own_blocks, 1))
    target = place(target.astype(i32))
    scatter = ((iota((groups, width), 0) == target) & (lane < 32 * nbrs)).astype(bf16)[:, : 32 * nbrs]

    gathered = gathered_ref[...]
    devs = gathered.shape[0]
    lane = iota((8, LANES), 1)
    lefts, rights = [], []
    for start in range(0, devs, 32):
        value = jnp.zeros((8, LANES), f32)
        order = jnp.zeros((8, LANES), f32)
        for i in range(4):
            piece = gathered[start + 8 * i : start + 8 * i + 8]
            here = lane // 32 == i
            value = jnp.where(here, pltpu.roll(piece, 32 * i, 1) if i else piece, value)
            order = jnp.where(here, pltpu.roll(piece, (32 * i + 96) % LANES, 1) if i != 1 else piece, order)
        order = order.astype(i32)
        group, unit = place(order // CELLS), order % CELLS
        for s in range(8):
            left = jnp.where(iota((groups, LANES), 0) == group[s : s + 1], value[s : s + 1], 0.0)
            lefts.append(jnp.concatenate(split(left), axis=0))
            rights.append((iota((CELLS, LANES), 0) == unit[s : s + 1]).astype(bf16))
    right_side = dot_t(jnp.concatenate(lefts, axis=1), jnp.concatenate(rights, axis=1))
    right_side = right_side[:groups] + right_side[groups:]

    own_block = iota((groups, unknowns), 1) // CELLS == iota((groups, unknowns), 0)

    def spread(x):
        wide = jnp.concatenate([x] * (LANES // CELLS), axis=1)
        wide = jnp.concatenate([wide] * (unknowns // LANES), axis=1)
        return jnp.concatenate(split(jnp.where(own_block, wide, 0.0)), axis=0)

    def product(x, ref):
        wide = spread(x)
        total = None
        for i in range(parts):
            term = dot_t(wide[:, i * width : (i + 1) * width], ref[i])
            total = term if total is None else total + term
        return total[:groups] + total[groups:]

    correction = product(right_side, inverse_ref)
    for _ in range(SWEEPS - 1):
        sums = product(correction, blocks_ref)
        pieces = []
        for k in range(nbrs):
            pieces += split(sums[:, k * CELLS : (k + 1) * CELLS])
        image = jnp.zeros((groups, CELLS), f32)
        high, low = pieces[0::2], pieces[1::2]
        stacked = jnp.concatenate([p for pair in zip(high, low) for p in pair], axis=0)
        image = dot(scatter, stacked)
        correction = correction + product(right_side - image, inverse_ref)
    for r in range(own_blocks // 2):
        both = [correction[2 * r : 2 * r + 1], correction[2 * r + 1 : 2 * r + 2]]
        correction_ref[r : r + 1, :] = jnp.concatenate(both, axis=1)
    correction_copy = pltpu.make_async_copy(correction_ref, correction_any, out_sem_ref.at[0])
    correction_copy.start()

    order = window_of(near_ref, far_ref, own_ref, device_index(), devices)[2].astype(i32)
    rows = order.shape[0]
    unit = jnp.concatenate([order[:, :CELLS], order[:, CELLS:]], axis=0)
    chosen = (iota(unit.shape, 1) == unit % CELLS).astype(bf16)
    values = dot_t(chosen, jnp.concatenate(split(correction), axis=0))
    group = place(unit[:, : 2 * groups] // CELLS)
    values = jnp.sum(jnp.where(iota(values.shape, 1) % groups == group, values, 0.0), axis=1, keepdims=True)
    corr = by_half([values[:rows], values[rows:]], (rows, LANES))
    for copy in copies:
        copy.wait()
    finish(corr, near_ref, far_ref, own_ref, local_ref, devices, selected_ref, fine_ref, smoother_ref, result_ref,
           picked_ref, high_ref, low_ref)
    result_copy = pltpu.make_async_copy(result_ref, out_any, out_sem_ref.at[1])
    result_copy.start()
    correction_copy.wait()
    result_copy.wait()


def finish_kernel(
    devices, corr_ref, near_ref, far_ref, own_ref, selected_ref, local_ref, fine_any, smoother_any, result_ref,
    fine_ref, smoother_ref, picked_ref, high_ref, low_ref, sem_ref,
):
    copies = fetch(sem_ref, (fine_any, fine_ref), (smoother_any, smoother_ref))
    for copy in copies:
        copy.wait()
    finish(corr_ref[...], near_ref, far_ref, own_ref, local_ref, devices, selected_ref, fine_ref, smoother_ref,
           result_ref, picked_ref, high_ref, low_ref)


def call(kernel, out_shape, ins, outs=None, scratch=()):
    spaces = dict(s=pltpu.SMEM, v=pltpu.VMEM, a=pl.ANY)
    many = isinstance(out_shape, tuple)
    specs = tuple(pl.BlockSpec(memory_space=spaces[c]) for c in outs or "v" * (len(out_shape) if many else 1))
    run = pl.pallas_call(
        kernel,
        out_shape=out_shape,
        in_specs=[pl.BlockSpec(memory_space=spaces[c]) for c in ins],
        out_specs=specs if many else specs[0],
        scratch_shapes=list(scratch),
        compiler_params=pltpu.CompilerParams(vmem_limit_bytes=VMEM_LIMIT),
    )

    def placed(*operands):
        return run(*(pltpu.with_memory_space_constraint(x, pltpu.HBM) if c == "a" else x for x, c in zip(operands, ins)))

    return placed


def shape_of(*dims):
    return jax.ShapeDtypeStruct(dims, f32)


def coarse_by_parts(restricted, coarse_order, coarse_values, coarse_rows, coarse_inverse):
    own = coarse_inverse.shape[1]
    own_blocks = own // CELLS
    total = own * lax.axis_size("coarse")
    start = lax.axis_index("coarse") * own
    side = jnp.zeros((total,), f32).at[coarse_order].add(restricted)
    side = lax.dynamic_slice_in_dim(lax.psum(side, BOTH), start, own)
    values = coarse_values.astype(f32).reshape(-1, CELLS, own_blocks, CELLS)
    inverse = coarse_inverse.astype(f32).reshape(CELLS, own_blocks, CELLS)

    def scale(x):
        x = x.reshape(own_blocks, CELLS)
        return jnp.einsum("oji,ji->jo", inverse, x, precision=lax.Precision.HIGHEST).reshape(-1)

    correction = scale(side)
    for _ in range(SWEEPS - 1):
        x = correction.reshape(own_blocks, CELLS)
        sums = jnp.einsum("vfmd,md->vmf", values, x, precision=lax.Precision.HIGHEST)
        image = jax.ops.segment_sum(
            sums.reshape(-1, CELLS), coarse_rows.reshape(-1), num_segments=total // CELLS
        ).reshape(-1)
        image = lax.dynamic_slice_in_dim(lax.psum(image, "coarse"), start, own)
        correction = correction + scale(side - image)
    return correction, lax.all_gather(correction, "coarse", axis=0, tiled=True)


def shards(
    devices, rhs, fine_values, fine_columns, smoother, reaction, pit_counts, weights, coarse_order,
    coarse_values, coarse_rows, coarse_inverse,
):
    cells = rhs.shape[0]
    pairs = cells // LANES
    aggs = 2 * pairs
    nbrs = fine_columns.shape[0]
    parts = lax.axis_size("coarse")
    rhs, reaction, weights = (x.reshape(pairs, LANES) for x in (rhs, reaction, weights))
    rows = pairs + 2 * HALO_ROWS
    vector = pltpu.VMEM((pairs, LANES), f32)
    fine_buffer = pltpu.VMEM(fine_values.shape, bf16)
    smoother_buffer = pltpu.VMEM(smoother.shape, bf16)
    products = [pltpu.VMEM((CELLS, cells), bf16)] * 2
    picked = pltpu.VMEM((nbrs * pairs, LANES), f32)
    copies = pltpu.SemaphoreType.DMA((4,))
    edge = shape_of(3, HALO_ROWS, LANES)

    near, onward, own = call(
        start_kernel, (edge, edge, shape_of(3, pairs, LANES)), "aaaa",
        scratch=[vector, vector, pltpu.VMEM((1, aggs), i32), smoother_buffer, *products, copies],
    )(rhs, weights, coarse_order.reshape(1, aggs), smoother)

    partner = [(d, d ^ 1) for d in range(devices)]
    chain = []
    for d in range(devices):
        target = d + 2 if d % 2 == 0 else d - 2
        chain.append((d, target if 0 <= target < devices else d ^ 1))
    onward = lax.ppermute(onward, BOTH, partner)
    near = lax.ppermute(near, BOTH, partner)
    far = lax.ppermute(onward, BOTH, chain)

    copied = parts == 4 and devices % 32 == 0 and devices <= 64
    if copied:
        deep = coarse_values.shape[0] * CELLS
        width = coarse_inverse.shape[1]
        coarse_values, _ = lax.optimization_barrier((coarse_values, own))
        packed = call(pack_kernel, shape_of(deep + CELLS + 8, width), "aaa", scratch=[
            pltpu.VMEM(coarse_rows.shape[::-1], i32), pltpu.VMEM((deep, width), bf16),
            pltpu.VMEM(coarse_inverse.shape, bf16), copies,
        ])(
            coarse_rows.T, coarse_values.reshape(deep, width), coarse_inverse
        )
        other = lax.ppermute(packed, "coarse", [(c, c ^ 2) for c in range(parts)])
        swap = [(c, c ^ 1) for c in range(parts)]
        beside = lax.ppermute(packed, "coarse", swap)

    selected, weighed, local = call(
        prepare_kernel,
        (jax.ShapeDtypeStruct((aggs * nbrs, 4 * rows), bf16), shape_of(nbrs * pairs, 8, LANES), shape_of(4, pairs, LANES)),
        "svaaaa",
        scratch=[vector, vector, pltpu.VMEM(fine_columns.shape, i32), fine_buffer, pltpu.VMEM((CELLS, cells), f32), copies],
    )(pit_counts, own, rhs, reaction, fine_columns, fine_values)

    sent = call(
        functools.partial(residual_kernel, devices), shape_of(devices, LANES), "vvvvvv", scratch=[picked]
    )(near, far, own, selected, weighed, local)

    finish_scratch = [ fine_buffer, smoother_buffer, picked, *products, copies]
    common = (near, far, own, selected, local)
    fetched = (fine_values, smoother)
    if copied:
        gathered = lax.all_to_all(sent, BOTH, 0, 0, tiled=True)
        other, gathered = lax.optimization_barrier((other, gathered))
        pieces = (packed, beside, other, lax.ppermute(other, "coarse", swap))
        result, correction = call(
            functools.partial(solve_kernel, devices),
            (shape_of(pairs, LANES), shape_of(width // LANES, LANES)),
            "vvvvvvvvvvaa",
            outs="aa",
            scratch=[
                pltpu.VMEM((parts, deep, width), bf16), pltpu.VMEM((parts, CELLS, width), bf16),
                vector, pltpu.VMEM((width // LANES, LANES), f32), *finish_scratch, pltpu.SemaphoreType.DMA((2,)),
            ],
        )(gathered, *common, *pieces, *fetched)
        correction = correction.reshape(-1)
    else:
        correction, everywhere = coarse_by_parts(
            sent[0, :aggs], coarse_order, coarse_values, coarse_rows, coarse_inverse
        )
        index = device_index()
        low = jnp.where(index == 0, 0.0, jnp.where(index % 2 == 0, far[2], near[2]))
        high = jnp.where(index == devices - 1, 0.0, jnp.where(index % 2 == 0, near[2], far[2]))
        order = jnp.concatenate([low, own[2], high], axis=0).astype(i32)
        corr = jnp.repeat(everywhere[order[:, ::CELLS]], CELLS, axis=1)
        result = call(
            functools.partial(finish_kernel, devices), shape_of(pairs, LANES), "vvvvvvaa", scratch=finish_scratch
        )(corr, *common, *fetched)
    return result.reshape(-1), correction


def solution(mesh):
    devices = mesh.shape["fine"] * mesh.shape["coarse"]
    in_specs = (
        P(BOTH),
        P(None, None, BOTH),
        P(None, BOTH),
        P(None, BOTH),
        P(BOTH),
        P(BOTH),
        P(BOTH),
        P(BOTH),
        P(None, None, "coarse"),
        P(None, "coarse"),
        P(None, "coarse"),
    )
    return jax.shard_map(
        functools.partial(shards, devices),
        mesh=mesh,
        in_specs=in_specs,
        out_specs=(P(BOTH), P("coarse")),
        check_vma=False,
    )
```

```python
import functools

import jax
import jax.numpy as jnp
from jax import lax
from jax.experimental import pallas as pl
from jax.experimental.pallas import tpu as pltpu
from jax.sharding import PartitionSpec as P

CELLS = 64
LANES = 128
HALO_ROWS = 8
SWEEPS = 4
EARLY = 3
BOTH = ("fine", "coarse")
f32, bf16, i32 = jnp.float32, jnp.bfloat16, jnp.int32
VMEM_LIMIT = 24 * 1024 * 1024


def iota(shape, axis):
    return lax.broadcasted_iota(i32, shape, axis)


def split(x):
    high = x.astype(bf16)
    return high, (x - high.astype(f32)).astype(bf16)


def dot(a, b):
    return lax.dot_general(a, b, (((1,), (0,)), ((), ())), preferred_element_type=f32)


def dot_t(a, b):
    return lax.dot_general(a, b, (((1,), (1,)), ((), ())), preferred_element_type=f32)


def cell_sums(high_ref, low_ref):
    width = high_ref.shape[1]
    pairs = width // LANES
    row, lane = iota((2 * pairs, width), 0), iota((2 * pairs, width), 1)
    member = (lane // CELLS == 2 * (row % pairs) + row // pairs).astype(bf16)
    sums = dot_t(member, high_ref[...]) + dot_t(member, low_ref[...])
    return jnp.concatenate([sums[:pairs], sums[pairs:]], axis=1)


def apply_smoother(vector, smoother_ref, high_ref, low_ref):
    for p in range(vector.shape[0]):
        cols = pl.ds(p * LANES, LANES)
        product = smoother_ref[:, cols].astype(f32) * vector[p : p + 1, :]
        high_ref[:, cols], low_ref[:, cols] = split(product)
    return cell_sums(high_ref, low_ref)


def selection(columns, half_rows, pairs):
    nbrs, aggs = columns.shape
    at, who = iota((pairs, aggs), 1), iota((pairs, aggs), 0)
    entry = iota((pairs, 4 * half_rows), 1) % (2 * half_rows)
    parts = []
    for half in range(2):
        for k in range(nbrs):
            chosen = jnp.where(at == 2 * who + half, columns[k : k + 1].astype(f32), 0.0)
            block = jnp.sum(chosen, axis=1, keepdims=True).astype(i32)
            place = block // 2 + jnp.where(block % 2 == half, 0, half_rows)
            parts.append((entry == place).astype(bf16))
    return jnp.concatenate(parts, axis=0)


def pick(window, selected):
    high, low = split(jnp.concatenate([window, pltpu.roll(window, CELLS, 1)], axis=0))
    picked = dot(selected, jnp.concatenate([high, low], axis=0))
    count = selected.shape[0] // 2
    lane = iota((count, LANES), 1)
    return jnp.where(lane < CELLS, picked[:count], picked[count:])


def apply_fine(window, fine_ref, selected, picked_ref, high_ref, low_ref):
    nbrs, _, width = fine_ref.shape
    pairs = width // LANES
    picked_ref[...] = pick(window, selected)
    for p in range(pairs):
        cols = pl.ds(p * LANES, LANES)
        total = None
        for k in range(nbrs):
            term = fine_ref[k, :, cols].astype(f32) * picked_ref[pl.ds(k * pairs + p, 1), :]
            total = term if total is None else total + term
        high_ref[:, cols], low_ref[:, cols] = split(total)
    return cell_sums(high_ref, low_ref)


def as_columns(row, pairs):
    shape = (pairs, row.shape[1])
    at, who = iota(shape, 1), iota(shape, 0)
    return [
        jnp.sum(jnp.where(at == 2 * who + half, row, 0.0), axis=1, keepdims=True)
        for half in range(2)
    ]


def by_half(columns, shape):
    return jnp.where(iota(shape, 1) < CELLS, columns[0], columns[1])


def fetch(sem_ref, *pairs):
    copies = [pltpu.make_async_copy(src, dst, sem_ref.at[i]) for i, (src, dst) in enumerate(pairs)]
    for copy in copies:
        copy.start()
    return copies


def start(rhs_ref, weights_ref, order_ref, smoother_ref, near_ref, onward_ref, own_ref, high_ref, low_ref):
    pairs = rhs_ref.shape[0]
    smoothed = apply_smoother(rhs_ref[...], smoother_ref, high_ref, low_ref)
    order = by_half(as_columns(order_ref[...].astype(f32), pairs), (pairs, LANES))
    even = lax.axis_index("coarse") % 2 == 0
    for i, part in enumerate((smoothed, weights_ref[...], order)):
        own_ref[i] = part
        bottom, top = part[:HALO_ROWS], part[pairs - HALO_ROWS :]
        near_ref[i] = jnp.where(even, top, bottom)
        onward_ref[i] = jnp.where(even, bottom, top)


def start_kernel(
    rhs_any, weights_any, order_any, smoother_any, near_ref, onward_ref, own_ref,
    rhs_ref, weights_ref, order_ref, smoother_ref, high_ref, low_ref, sem_ref,
):
    copies = fetch(
        sem_ref, (smoother_any, smoother_ref), (rhs_any, rhs_ref), (weights_any, weights_ref), (order_any, order_ref)
    )
    for copy in copies:
        copy.wait()
    start(rhs_ref, weights_ref, order_ref, smoother_ref, near_ref, onward_ref, own_ref, high_ref, low_ref)


def start_pack_kernel(
    rhs_any, weights_any, order_any, smoother_any, rows_any, values_any, inverse_any,
    near_ref, onward_ref, own_ref, packed_ref, first_ref, second_ref,
    rhs_ref, weights_ref, order_ref, smoother_ref, rows_ref, values_ref, inverse_ref, high_ref, low_ref, sem_ref,
):
    copies = fetch(
        sem_ref, (smoother_any, smoother_ref), (rhs_any, rhs_ref), (weights_any, weights_ref), (order_any, order_ref),
        (values_any, values_ref), (inverse_any, inverse_ref), (rows_any, rows_ref),
    )
    for copy in copies[:4]:
        copy.wait()
    start(rhs_ref, weights_ref, order_ref, smoother_ref, near_ref, onward_ref, own_ref, high_ref, low_ref)
    for copy in copies[4:]:
        copy.wait()
    own_blocks, nbrs = rows_ref.shape
    deep, width = values_ref.shape
    lane, block = iota((own_blocks, width), 1), iota((own_blocks, width), 0)
    rows = jnp.zeros((own_blocks, width), f32)
    for k in range(nbrs):
        here = (lane // 32 == k) & (lane % 16 == block)
        rows = jnp.where(here, rows_ref[:, k : k + 1].astype(f32), rows)
    rows = jnp.broadcast_to(jnp.sum(rows, axis=0, keepdims=True), (8, width))
    early = first_ref.shape[0] - 8
    first_ref[pl.ds(0, 8), :] = rows
    packed_ref[pl.ds(0, 8), :] = rows
    for r in range(0, deep, CELLS):
        values = values_ref[pl.ds(r, CELLS), :].astype(f32)
        packed_ref[pl.ds(8 + r, CELLS), :] = values
        if r < early:
            first_ref[pl.ds(8 + r, CELLS), :] = values
        else:
            second_ref[pl.ds(r - early, CELLS), :] = values
    inverse = inverse_ref[...].astype(f32)
    packed_ref[pl.ds(8 + deep, CELLS), :] = inverse
    second_ref[pl.ds(deep - early, CELLS), :] = inverse


def window_of(near_ref, far_ref, own_ref, device, devices):
    even = device % 2 == 0
    near, far = near_ref[...], far_ref[...]
    low = jnp.where(device == 0, 0.0, jnp.where(even, far, near))
    high = jnp.where(device == devices - 1, 0.0, jnp.where(even, near, far))
    return [jnp.concatenate([low[i], own_ref[i], high[i]], axis=0) for i in range(3)]


def device_index():
    return lax.axis_index("fine") * lax.axis_size("coarse") + lax.axis_index("coarse")


def prepare_kernel(
    counts_ref, own_ref, rhs_any, reaction_any, columns_any, fine_any, selected_ref, weighed_ref, local_ref,
    rhs_ref, reaction_ref, columns_ref, fine_ref, wide_ref, sem_ref,
):
    copies = fetch(
        sem_ref, (fine_any, fine_ref), (columns_any, columns_ref), (rhs_any, rhs_ref), (reaction_any, reaction_ref)
    )
    for copy in copies[1:]:
        copy.wait()
    pairs = rhs_ref.shape[0]
    nbrs, _, width = fine_ref.shape
    weights = own_ref[1]
    agg = 2 * iota((pairs, LANES), 0) + iota((pairs, LANES), 1) // CELLS
    reaction = jnp.where(agg < counts_ref[0], reaction_ref[...], 0.0)
    local_ref[0] = weights * rhs_ref[...]
    local_ref[1] = weights * reaction
    local_ref[2] = rhs_ref[...]
    local_ref[3] = reaction
    selected_ref[...] = selection(columns_ref[...], pairs + 2 * HALO_ROWS, pairs)
    by_agg = jnp.concatenate([weights[:, :CELLS], weights[:, CELLS:]], axis=0)
    row, lane = iota((2 * pairs, width), 0), iota((2 * pairs, width), 1)
    member = (lane // CELLS == 2 * (row % pairs) + row // pairs).astype(bf16)
    wide = None
    for part in split(by_agg):
        term = lax.dot_general(part, member, (((0,), (0,)), ((), ())), preferred_element_type=f32)
        wide = term if wide is None else wide + term
    wide_ref[...] = wide
    copies[0].wait()
    for p in range(pairs):
        cols = pl.ds(p * LANES, LANES)
        scale = wide_ref[:, cols]
        for k in range(nbrs):
            term = fine_ref[k, :, cols].astype(f32) * scale
            total = term[:8]
            for r in range(8, CELLS, 8):
                total = total + term[r : r + 8]
            weighed_ref[k * pairs + p] = total


def residual_kernel(
    devices, near_ref, far_ref, own_ref, selected_ref, weighed_ref, local_ref, out_ref, picked_ref,
):
    smoothed, _, _ = window_of(near_ref, far_ref, own_ref, device_index(), devices)
    picked_ref[...] = pick(smoothed, selected_ref[...])
    pairs = own_ref.shape[1]
    nbrs = picked_ref.shape[0] // pairs
    images = []
    for p in range(pairs):
        total = None
        for k in range(nbrs):
            term = weighed_ref[k * pairs + p] * picked_ref[pl.ds(k * pairs + p, 1), :]
            total = term if total is None else total + term
        images.append(jnp.sum(total, axis=0, keepdims=True))
    weighted = local_ref[0] - local_ref[1] * own_ref[0] - jnp.concatenate(images, axis=0)
    shape = (pairs, LANES)
    lane, who = iota(shape, 1), iota(shape, 0)
    row = jnp.zeros((1, LANES), f32)
    for half in range(2):
        inside = lane // CELLS == half
        restricted = jnp.sum(jnp.where(inside, weighted, 0.0), axis=1, keepdims=True)
        order = jnp.max(jnp.where(inside, own_ref[2], 0.0), axis=1, keepdims=True)
        spread = jnp.where(lane == 2 * who + half, restricted, 0.0)
        spread = spread + jnp.where(lane == 2 * (pairs + who) + half, order, 0.0)
        row = row + jnp.sum(spread, axis=0, keepdims=True)
    out_ref[...] = jnp.broadcast_to(row, out_ref.shape)


def finish(corr, near_ref, far_ref, own_ref, local_ref, devices, selected_ref, fine_ref, smoother_ref, result_ref,
           picked_ref, high_ref, low_ref):
    smoothed, weights, _ = window_of(near_ref, far_ref, own_ref, device_index(), devices)
    corrected = smoothed + weights * corr
    pairs = own_ref.shape[1]
    mine = corrected[HALO_ROWS : HALO_ROWS + pairs]
    image = apply_fine(corrected, fine_ref, selected_ref[...], picked_ref, high_ref, low_ref)
    image = image + local_ref[3] * mine
    result_ref[...] = mine + apply_smoother(local_ref[2] - image, smoother_ref, high_ref, low_ref)


def solve_kernel(
    devices, gathered_ref, near_ref, far_ref, own_ref, selected_ref, local_ref,
    mine_ref, beside_ref, first2_ref, second2_ref, first3_ref, second3_ref, fine_any, smoother_any,
    out_any, correction_any,
    blocks_ref, inverse_ref, result_ref, correction_ref,
    fine_ref, smoother_ref, picked_ref, high_ref, low_ref, sem_ref, out_sem_ref,
):
    copies = fetch(sem_ref, (fine_any, fine_ref), (smoother_any, smoother_ref))
    me = lax.axis_index("coarse")
    parts = blocks_ref.shape[0]
    deep, width = blocks_ref.shape[1:]
    nbrs = deep // CELLS
    own_blocks = width // CELLS
    groups = parts * own_blocks
    unknowns = groups * CELLS
    early = first2_ref.shape[0] - 8
    row_refs = (mine_ref, beside_ref, first2_ref, first3_ref)
    for i, ref in enumerate((mine_ref, beside_ref)):
        blocks_ref[i] = ref[pl.ds(8, deep), :].astype(bf16)
        inverse_ref[i] = ref[pl.ds(8 + deep, CELLS), :].astype(bf16)
    for i, first, second in ((2, first2_ref, second2_ref), (3, first3_ref, second3_ref)):
        blocks_ref[i, pl.ds(0, early), :] = first[pl.ds(8, early), :].astype(bf16)
        blocks_ref[i, pl.ds(early, deep - early), :] = second[pl.ds(0, deep - early), :].astype(bf16)
        inverse_ref[i] = second[pl.ds(deep - early, CELLS), :].astype(bf16)

    def place(group):
        return jnp.bitwise_xor(group // own_blocks, me) * own_blocks + group % own_blocks

    lane = iota((1, width), 1)
    target = jnp.zeros((1, width), f32)
    for i, ref in enumerate(row_refs):
        rows = ref[pl.ds(0, 8), :][0:1, :]
        rows = jnp.where((lane % 16 < own_blocks) & (lane < 32 * nbrs), rows, 0.0)
        target = target + (rows if i == 0 else pltpu.roll(rows, i * own_blocks, 1))
    target = place(target.astype(i32))
    scatter = ((iota((groups, width), 0) == target) & (lane < 32 * nbrs)).astype(bf16)[:, : 32 * nbrs]

    gathered = gathered_ref[...]
    devs = gathered.shape[0]
    lane = iota((8, LANES), 1)
    lefts, rights = [], []
    for start in range(0, devs, 32):
        value = jnp.zeros((8, LANES), f32)
        order = jnp.zeros((8, LANES), f32)
        for i in range(4):
            piece = gathered[start + 8 * i : start + 8 * i + 8]
            here = lane // 32 == i
            value = jnp.where(here, pltpu.roll(piece, 32 * i, 1) if i else piece, value)
            order = jnp.where(here, pltpu.roll(piece, (32 * i + 96) % LANES, 1) if i != 1 else piece, order)
        order = order.astype(i32)
        group, unit = place(order // CELLS), order % CELLS
        for s in range(8):
            left = jnp.where(iota((groups, LANES), 0) == group[s : s + 1], value[s : s + 1], 0.0)
            lefts.append(jnp.concatenate(split(left), axis=0))
            rights.append((iota((CELLS, LANES), 0) == unit[s : s + 1]).astype(bf16))
    right_side = dot_t(jnp.concatenate(lefts, axis=1), jnp.concatenate(rights, axis=1))
    right_side = right_side[:groups] + right_side[groups:]

    own_block = iota((groups, unknowns), 1) // CELLS == iota((groups, unknowns), 0)

    def spread(x):
        wide = jnp.concatenate([x] * (LANES // CELLS), axis=1)
        wide = jnp.concatenate([wide] * (unknowns // LANES), axis=1)
        return jnp.concatenate(split(jnp.where(own_block, wide, 0.0)), axis=0)

    def product(x, ref):
        wide = spread(x)
        total = None
        for i in range(parts):
            term = dot_t(wide[:, i * width : (i + 1) * width], ref[i])
            total = term if total is None else total + term
        return total[:groups] + total[groups:]

    correction = product(right_side, inverse_ref)
    for _ in range(SWEEPS - 1):
        sums = product(correction, blocks_ref)
        pieces = []
        for k in range(nbrs):
            pieces += split(sums[:, k * CELLS : (k + 1) * CELLS])
        image = jnp.zeros((groups, CELLS), f32)
        high, low = pieces[0::2], pieces[1::2]
        stacked = jnp.concatenate([p for pair in zip(high, low) for p in pair], axis=0)
        image = dot(scatter, stacked)
        correction = correction + product(right_side - image, inverse_ref)
    for r in range(own_blocks // 2):
        both = [correction[2 * r : 2 * r + 1], correction[2 * r + 1 : 2 * r + 2]]
        correction_ref[r : r + 1, :] = jnp.concatenate(both, axis=1)
    correction_copy = pltpu.make_async_copy(correction_ref, correction_any, out_sem_ref.at[0])
    correction_copy.start()

    order = window_of(near_ref, far_ref, own_ref, device_index(), devices)[2].astype(i32)
    rows = order.shape[0]
    unit = jnp.concatenate([order[:, :CELLS], order[:, CELLS:]], axis=0)
    chosen = (iota(unit.shape, 1) == unit % CELLS).astype(bf16)
    values = dot_t(chosen, jnp.concatenate(split(correction), axis=0))
    group = place(unit[:, : 2 * groups] // CELLS)
    values = jnp.sum(jnp.where(iota(values.shape, 1) % groups == group, values, 0.0), axis=1, keepdims=True)
    corr = by_half([values[:rows], values[rows:]], (rows, LANES))
    for copy in copies:
        copy.wait()
    finish(corr, near_ref, far_ref, own_ref, local_ref, devices, selected_ref, fine_ref, smoother_ref, result_ref,
           picked_ref, high_ref, low_ref)
    result_copy = pltpu.make_async_copy(result_ref, out_any, out_sem_ref.at[1])
    result_copy.start()
    correction_copy.wait()
    result_copy.wait()


def finish_kernel(
    devices, corr_ref, near_ref, far_ref, own_ref, selected_ref, local_ref, fine_any, smoother_any, result_ref,
    fine_ref, smoother_ref, picked_ref, high_ref, low_ref, sem_ref,
):
    copies = fetch(sem_ref, (fine_any, fine_ref), (smoother_any, smoother_ref))
    for copy in copies:
        copy.wait()
    finish(corr_ref[...], near_ref, far_ref, own_ref, local_ref, devices, selected_ref, fine_ref, smoother_ref,
           result_ref, picked_ref, high_ref, low_ref)


def call(kernel, out_shape, ins, outs=None, scratch=()):
    spaces = dict(s=pltpu.SMEM, v=pltpu.VMEM, a=pl.ANY)
    many = isinstance(out_shape, tuple)
    specs = tuple(pl.BlockSpec(memory_space=spaces[c]) for c in outs or "v" * (len(out_shape) if many else 1))
    run = pl.pallas_call(
        kernel,
        out_shape=out_shape,
        in_specs=[pl.BlockSpec(memory_space=spaces[c]) for c in ins],
        out_specs=specs if many else specs[0],
        scratch_shapes=list(scratch),
        compiler_params=pltpu.CompilerParams(vmem_limit_bytes=VMEM_LIMIT),
    )

    def placed(*operands):
        return run(*(pltpu.with_memory_space_constraint(x, pltpu.HBM) if c == "a" else x for x, c in zip(operands, ins)))

    return placed


def shape_of(*dims):
    return jax.ShapeDtypeStruct(dims, f32)


def coarse_by_parts(restricted, coarse_order, coarse_values, coarse_rows, coarse_inverse):
    own = coarse_inverse.shape[1]
    own_blocks = own // CELLS
    total = own * lax.axis_size("coarse")
    start = lax.axis_index("coarse") * own
    side = jnp.zeros((total,), f32).at[coarse_order].add(restricted)
    side = lax.dynamic_slice_in_dim(lax.psum(side, BOTH), start, own)
    values = coarse_values.astype(f32).reshape(-1, CELLS, own_blocks, CELLS)
    inverse = coarse_inverse.astype(f32).reshape(CELLS, own_blocks, CELLS)

    def scale(x):
        x = x.reshape(own_blocks, CELLS)
        return jnp.einsum("oji,ji->jo", inverse, x, precision=lax.Precision.HIGHEST).reshape(-1)

    correction = scale(side)
    for _ in range(SWEEPS - 1):
        x = correction.reshape(own_blocks, CELLS)
        sums = jnp.einsum("vfmd,md->vmf", values, x, precision=lax.Precision.HIGHEST)
        image = jax.ops.segment_sum(
            sums.reshape(-1, CELLS), coarse_rows.reshape(-1), num_segments=total // CELLS
        ).reshape(-1)
        image = lax.dynamic_slice_in_dim(lax.psum(image, "coarse"), start, own)
        correction = correction + scale(side - image)
    return correction, lax.all_gather(correction, "coarse", axis=0, tiled=True)


def shards(
    devices, rhs, fine_values, fine_columns, smoother, reaction, pit_counts, weights, coarse_order,
    coarse_values, coarse_rows, coarse_inverse,
):
    cells = rhs.shape[0]
    pairs = cells // LANES
    aggs = 2 * pairs
    nbrs = fine_columns.shape[0]
    parts = lax.axis_size("coarse")
    rhs, reaction, weights = (x.reshape(pairs, LANES) for x in (rhs, reaction, weights))
    rows = pairs + 2 * HALO_ROWS
    vector = pltpu.VMEM((pairs, LANES), f32)
    fine_buffer = pltpu.VMEM(fine_values.shape, bf16)
    smoother_buffer = pltpu.VMEM(smoother.shape, bf16)
    products = [pltpu.VMEM((CELLS, cells), bf16)] * 2
    picked = pltpu.VMEM((nbrs * pairs, LANES), f32)
    copies = pltpu.SemaphoreType.DMA((4,))
    edge = shape_of(3, HALO_ROWS, LANES)

    copied = parts == 4 and devices % 32 == 0 and devices <= 64
    start_shapes = (edge, edge, shape_of(3, pairs, LANES))
    start_ins = (rhs, weights, coarse_order.reshape(1, aggs), smoother)
    start_scratch = [vector, vector, pltpu.VMEM((1, aggs), i32), smoother_buffer]
    if copied:
        deep = coarse_values.shape[0] * CELLS
        width = coarse_inverse.shape[1]
        early = EARLY * CELLS
        near, onward, own, packed, first, second = call(
            start_pack_kernel,
            (*start_shapes, shape_of(8 + deep + CELLS, width), shape_of(8 + early, width),
             shape_of(deep - early + CELLS, width)),
            "aaaaaaa",
            scratch=[
                *start_scratch, pltpu.VMEM(coarse_rows.shape[::-1], i32), pltpu.VMEM((deep, width), bf16),
                pltpu.VMEM(coarse_inverse.shape, bf16), *products, pltpu.SemaphoreType.DMA((7,)),
            ],
        )(*start_ins, coarse_rows.T, coarse_values.reshape(deep, width), coarse_inverse)
        swap = [(c, c ^ 1) for c in range(parts)]
        across = [(c, c ^ 2) for c in range(parts)]
        first2 = lax.ppermute(first, "coarse", across)
    else:
        near, onward, own = call(start_kernel, start_shapes, "aaaa", scratch=[*start_scratch, *products, copies])(
            *start_ins
        )

    partner = [(d, d ^ 1) for d in range(devices)]
    chain = []
    for d in range(devices):
        target = d + 2 if d % 2 == 0 else d - 2
        chain.append((d, target if 0 <= target < devices else d ^ 1))
    onward = lax.ppermute(onward, BOTH, partner)
    near = lax.ppermute(near, BOTH, partner)

    if copied:
        packed, onward = lax.optimization_barrier((packed, onward))
        beside = lax.ppermute(packed, "coarse", swap)
    far = lax.ppermute(onward, BOTH, chain)
    selected, weighed, local = call(
        prepare_kernel,
        (jax.ShapeDtypeStruct((aggs * nbrs, 4 * rows), bf16), shape_of(nbrs * pairs, 8, LANES), shape_of(4, pairs, LANES)),
        "svaaaa",
        scratch=[vector, vector, pltpu.VMEM(fine_columns.shape, i32), fine_buffer, pltpu.VMEM((CELLS, cells), f32), copies],
    )(pit_counts, own, rhs, reaction, fine_columns, fine_values)

    if copied:
        first2, second, far, near, selected, beside = lax.optimization_barrier(
            (first2, second, far, near, selected, beside)
        )
        second2 = lax.ppermute(second, "coarse", across)
        first3 = lax.ppermute(first2, "coarse", swap)

    sent = call(
        functools.partial(residual_kernel, devices), shape_of(devices, LANES), "vvvvvv", scratch=[picked]
    )(near, far, own, selected, weighed, local)

    finish_scratch = [ fine_buffer, smoother_buffer, picked, *products, copies]
    common = (near, far, own, selected, local)
    fetched = (fine_values, smoother)
    if copied:
        first3, sent = lax.optimization_barrier((first3, sent))
        gathered = lax.all_to_all(sent, BOTH, 0, 0, tiled=True)
        second2, gathered = lax.optimization_barrier((second2, gathered))
        pieces = (packed, beside, first2, second2, first3, lax.ppermute(second2, "coarse", swap))
        result, correction = call(
            functools.partial(solve_kernel, devices),
            (shape_of(pairs, LANES), shape_of(width // LANES, LANES)),
            "vvvvvv" + "vvvvvv" + "aa",
            outs="aa",
            scratch=[
                pltpu.VMEM((parts, deep, width), bf16), pltpu.VMEM((parts, CELLS, width), bf16),
                vector, pltpu.VMEM((width // LANES, LANES), f32), *finish_scratch, pltpu.SemaphoreType.DMA((2,)),
            ],
        )(gathered, *common, *pieces, *fetched)
        correction = correction.reshape(-1)
    else:
        correction, everywhere = coarse_by_parts(
            sent[0, :aggs], coarse_order, coarse_values, coarse_rows, coarse_inverse
        )
        index = device_index()
        low = jnp.where(index == 0, 0.0, jnp.where(index % 2 == 0, far[2], near[2]))
        high = jnp.where(index == devices - 1, 0.0, jnp.where(index % 2 == 0, near[2], far[2]))
        order = jnp.concatenate([low, own[2], high], axis=0).astype(i32)
        corr = jnp.repeat(everywhere[order[:, ::CELLS]], CELLS, axis=1)
        result = call(
            functools.partial(finish_kernel, devices), shape_of(pairs, LANES), "vvvvvvaa", scratch=finish_scratch
        )(corr, *common, *fetched)
    return result.reshape(-1), correction


def solution(mesh):
    devices = mesh.shape["fine"] * mesh.shape["coarse"]
    in_specs = (
        P(BOTH),
        P(None, None, BOTH),
        P(None, BOTH),
        P(None, BOTH),
        P(BOTH),
        P(BOTH),
        P(BOTH),
        P(BOTH),
        P(None, None, "coarse"),
        P(None, "coarse"),
        P(None, "coarse"),
    )
    return jax.shard_map(
        functools.partial(shards, devices),
        mesh=mesh,
        in_specs=in_specs,
        out_specs=(P(BOTH), P("coarse")),
        check_vma=False,
    )
```

```python
import functools

import jax
import jax.numpy as jnp
from jax import lax
from jax.experimental import pallas as pl
from jax.experimental.pallas import tpu as pltpu
from jax.sharding import PartitionSpec as P

CELLS = 64
LANES = 128
HALO_ROWS = 8
SWEEPS = 4
EARLY = 2
BOTH = ("fine", "coarse")
f32, bf16, i32 = jnp.float32, jnp.bfloat16, jnp.int32
VMEM_LIMIT = 24 * 1024 * 1024


def iota(shape, axis):
    return lax.broadcasted_iota(i32, shape, axis)


def split(x):
    high = x.astype(bf16)
    return high, (x - high.astype(f32)).astype(bf16)


def dot(a, b):
    return lax.dot_general(a, b, (((1,), (0,)), ((), ())), preferred_element_type=f32)


def dot_t(a, b):
    return lax.dot_general(a, b, (((1,), (1,)), ((), ())), preferred_element_type=f32)


def cell_sums(high_ref, low_ref):
    width = high_ref.shape[1]
    pairs = width // LANES
    row, lane = iota((2 * pairs, width), 0), iota((2 * pairs, width), 1)
    member = (lane // CELLS == 2 * (row % pairs) + row // pairs).astype(bf16)
    sums = dot_t(member, high_ref[...]) + dot_t(member, low_ref[...])
    return jnp.concatenate([sums[:pairs], sums[pairs:]], axis=1)


def apply_smoother(vector, smoother_ref, high_ref, low_ref):
    for p in range(vector.shape[0]):
        cols = pl.ds(p * LANES, LANES)
        product = smoother_ref[:, cols].astype(f32) * vector[p : p + 1, :]
        high_ref[:, cols], low_ref[:, cols] = split(product)
    return cell_sums(high_ref, low_ref)


def selection(columns, half_rows, pairs):
    nbrs, aggs = columns.shape
    at, who = iota((pairs, aggs), 1), iota((pairs, aggs), 0)
    entry = iota((pairs, 4 * half_rows), 1) % (2 * half_rows)
    parts = []
    for half in range(2):
        for k in range(nbrs):
            chosen = jnp.where(at == 2 * who + half, columns[k : k + 1].astype(f32), 0.0)
            block = jnp.sum(chosen, axis=1, keepdims=True).astype(i32)
            place = block // 2 + jnp.where(block % 2 == half, 0, half_rows)
            parts.append((entry == place).astype(bf16))
    return jnp.concatenate(parts, axis=0)


def pick(window, selected):
    high, low = split(jnp.concatenate([window, pltpu.roll(window, CELLS, 1)], axis=0))
    picked = dot(selected, jnp.concatenate([high, low], axis=0))
    count = selected.shape[0] // 2
    lane = iota((count, LANES), 1)
    return jnp.where(lane < CELLS, picked[:count], picked[count:])


def apply_fine(window, fine_ref, selected, picked_ref, high_ref, low_ref):
    nbrs, _, width = fine_ref.shape
    pairs = width // LANES
    picked_ref[...] = pick(window, selected)
    for p in range(pairs):
        cols = pl.ds(p * LANES, LANES)
        total = None
        for k in range(nbrs):
            term = fine_ref[k, :, cols].astype(f32) * picked_ref[pl.ds(k * pairs + p, 1), :]
            total = term if total is None else total + term
        high_ref[:, cols], low_ref[:, cols] = split(total)
    return cell_sums(high_ref, low_ref)


def as_columns(row, pairs):
    shape = (pairs, row.shape[1])
    at, who = iota(shape, 1), iota(shape, 0)
    return [
        jnp.sum(jnp.where(at == 2 * who + half, row, 0.0), axis=1, keepdims=True)
        for half in range(2)
    ]


def by_half(columns, shape):
    return jnp.where(iota(shape, 1) < CELLS, columns[0], columns[1])


def fetch(sem_ref, *pairs):
    copies = [pltpu.make_async_copy(src, dst, sem_ref.at[i]) for i, (src, dst) in enumerate(pairs)]
    for copy in copies:
        copy.start()
    return copies


def start(rhs_ref, weights_ref, order_ref, smoother_ref, near_ref, onward_ref, own_ref, high_ref, low_ref):
    pairs = rhs_ref.shape[0]
    smoothed = apply_smoother(rhs_ref[...], smoother_ref, high_ref, low_ref)
    order = by_half(as_columns(order_ref[...].astype(f32), pairs), (pairs, LANES))
    even = lax.axis_index("coarse") % 2 == 0
    for i, part in enumerate((smoothed, weights_ref[...], order)):
        own_ref[i] = part
        bottom, top = part[:HALO_ROWS], part[pairs - HALO_ROWS :]
        near_ref[i] = jnp.where(even, top, bottom)
        onward_ref[i] = jnp.where(even, bottom, top)


def start_kernel(
    rhs_any, weights_any, order_any, smoother_any, near_ref, onward_ref, own_ref,
    rhs_ref, weights_ref, order_ref, smoother_ref, high_ref, low_ref, sem_ref,
):
    copies = fetch(
        sem_ref, (smoother_any, smoother_ref), (rhs_any, rhs_ref), (weights_any, weights_ref), (order_any, order_ref)
    )
    for copy in copies:
        copy.wait()
    start(rhs_ref, weights_ref, order_ref, smoother_ref, near_ref, onward_ref, own_ref, high_ref, low_ref)


def start_pack_kernel(
    rhs_any, weights_any, order_any, smoother_any, rows_any, values_any, inverse_any,
    near_ref, onward_ref, own_ref, packed_ref, first_ref, second_ref,
    rhs_ref, weights_ref, order_ref, smoother_ref, rows_ref, values_ref, inverse_ref, high_ref, low_ref, sem_ref,
):
    copies = fetch(
        sem_ref, (smoother_any, smoother_ref), (rhs_any, rhs_ref), (weights_any, weights_ref), (order_any, order_ref),
        (values_any, values_ref), (inverse_any, inverse_ref), (rows_any, rows_ref),
    )
    for copy in copies[:4]:
        copy.wait()
    start(rhs_ref, weights_ref, order_ref, smoother_ref, near_ref, onward_ref, own_ref, high_ref, low_ref)
    for copy in copies[4:]:
        copy.wait()
    own_blocks, nbrs = rows_ref.shape
    deep, width = values_ref.shape
    lane, block = iota((own_blocks, width), 1), iota((own_blocks, width), 0)
    rows = jnp.zeros((own_blocks, width), f32)
    for k in range(nbrs):
        here = (lane // 32 == k) & (lane % 16 == block)
        rows = jnp.where(here, rows_ref[:, k : k + 1].astype(f32), rows)
    rows = jnp.broadcast_to(jnp.sum(rows, axis=0, keepdims=True), (8, width))
    inverse = inverse_ref[...].astype(f32)
    for ref in (packed_ref, first_ref):
        ref[pl.ds(0, 8), :] = rows
        ref[pl.ds(8, CELLS), :] = inverse
    base = 8 + CELLS
    early = first_ref.shape[0] - base
    for r in range(0, deep, CELLS):
        values = values_ref[pl.ds(r, CELLS), :].astype(f32)
        packed_ref[pl.ds(base + r, CELLS), :] = values
        if r < early:
            first_ref[pl.ds(base + r, CELLS), :] = values
        else:
            second_ref[pl.ds(r - early, CELLS), :] = values


def window_of(near_ref, far_ref, own_ref, device, devices):
    even = device % 2 == 0
    near, far = near_ref[...], far_ref[...]
    low = jnp.where(device == 0, 0.0, jnp.where(even, far, near))
    high = jnp.where(device == devices - 1, 0.0, jnp.where(even, near, far))
    return [jnp.concatenate([low[i], own_ref[i], high[i]], axis=0) for i in range(3)]


def device_index():
    return lax.axis_index("fine") * lax.axis_size("coarse") + lax.axis_index("coarse")


def prepare_kernel(
    counts_ref, own_ref, rhs_any, reaction_any, columns_any, fine_any, selected_ref, weighed_ref, local_ref,
    rhs_ref, reaction_ref, columns_ref, fine_ref, wide_ref, sem_ref,
):
    copies = fetch(
        sem_ref, (fine_any, fine_ref), (columns_any, columns_ref), (rhs_any, rhs_ref), (reaction_any, reaction_ref)
    )
    for copy in copies[1:]:
        copy.wait()
    pairs = rhs_ref.shape[0]
    nbrs, _, width = fine_ref.shape
    weights = own_ref[1]
    agg = 2 * iota((pairs, LANES), 0) + iota((pairs, LANES), 1) // CELLS
    reaction = jnp.where(agg < counts_ref[0], reaction_ref[...], 0.0)
    local_ref[0] = weights * rhs_ref[...]
    local_ref[1] = weights * reaction
    local_ref[2] = rhs_ref[...]
    local_ref[3] = reaction
    selected_ref[...] = selection(columns_ref[...], pairs + 2 * HALO_ROWS, pairs)
    by_agg = jnp.concatenate([weights[:, :CELLS], weights[:, CELLS:]], axis=0)
    row, lane = iota((2 * pairs, width), 0), iota((2 * pairs, width), 1)
    member = (lane // CELLS == 2 * (row % pairs) + row // pairs).astype(bf16)
    wide = None
    for part in split(by_agg):
        term = lax.dot_general(part, member, (((0,), (0,)), ((), ())), preferred_element_type=f32)
        wide = term if wide is None else wide + term
    wide_ref[...] = wide
    copies[0].wait()
    for p in range(pairs):
        cols = pl.ds(p * LANES, LANES)
        scale = wide_ref[:, cols]
        for k in range(nbrs):
            term = fine_ref[k, :, cols].astype(f32) * scale
            total = term[:8]
            for r in range(8, CELLS, 8):
                total = total + term[r : r + 8]
            weighed_ref[k * pairs + p] = total


def residual_kernel(
    devices, near_ref, far_ref, own_ref, selected_ref, weighed_ref, local_ref, out_ref, picked_ref,
):
    smoothed, _, _ = window_of(near_ref, far_ref, own_ref, device_index(), devices)
    picked_ref[...] = pick(smoothed, selected_ref[...])
    pairs = own_ref.shape[1]
    nbrs = picked_ref.shape[0] // pairs
    images = []
    for p in range(pairs):
        total = None
        for k in range(nbrs):
            term = weighed_ref[k * pairs + p] * picked_ref[pl.ds(k * pairs + p, 1), :]
            total = term if total is None else total + term
        images.append(jnp.sum(total, axis=0, keepdims=True))
    weighted = local_ref[0] - local_ref[1] * own_ref[0] - jnp.concatenate(images, axis=0)
    shape = (pairs, LANES)
    lane, who = iota(shape, 1), iota(shape, 0)
    row = jnp.zeros((1, LANES), f32)
    for half in range(2):
        inside = lane // CELLS == half
        restricted = jnp.sum(jnp.where(inside, weighted, 0.0), axis=1, keepdims=True)
        order = jnp.max(jnp.where(inside, own_ref[2], 0.0), axis=1, keepdims=True)
        spread = jnp.where(lane == 2 * who + half, restricted, 0.0)
        spread = spread + jnp.where(lane == 2 * (pairs + who) + half, order, 0.0)
        row = row + jnp.sum(spread, axis=0, keepdims=True)
    out_ref[...] = jnp.broadcast_to(row, out_ref.shape)


def finish(corr, near_ref, far_ref, own_ref, local_ref, devices, selected_ref, fine_ref, smoother_ref, result_ref,
           picked_ref, high_ref, low_ref):
    smoothed, weights, _ = window_of(near_ref, far_ref, own_ref, device_index(), devices)
    corrected = smoothed + weights * corr
    pairs = own_ref.shape[1]
    mine = corrected[HALO_ROWS : HALO_ROWS + pairs]
    image = apply_fine(corrected, fine_ref, selected_ref[...], picked_ref, high_ref, low_ref)
    image = image + local_ref[3] * mine
    result_ref[...] = mine + apply_smoother(local_ref[2] - image, smoother_ref, high_ref, low_ref)


def solve_kernel(
    devices, gathered_ref, near_ref, far_ref, own_ref, selected_ref, local_ref,
    mine_ref, beside_ref, first2_ref, second2_ref, first3_ref, second3_ref, fine_any, smoother_any,
    out_any, correction_any,
    blocks_ref, inverse_ref, result_ref, correction_ref,
    fine_ref, smoother_ref, picked_ref, high_ref, low_ref, sem_ref, out_sem_ref,
):
    copies = fetch(sem_ref, (fine_any, fine_ref), (smoother_any, smoother_ref))
    me = lax.axis_index("coarse")
    parts = blocks_ref.shape[0]
    deep, width = blocks_ref.shape[1:]
    nbrs = deep // CELLS
    own_blocks = width // CELLS
    groups = parts * own_blocks
    unknowns = groups * CELLS
    base = 8 + CELLS
    early = first2_ref.shape[0] - base
    row_refs = (mine_ref, beside_ref, first2_ref, first3_ref)
    for i, ref in enumerate((mine_ref, beside_ref)):
        blocks_ref[i] = ref[pl.ds(base, deep), :].astype(bf16)
    for i, first, second in ((2, first2_ref, second2_ref), (3, first3_ref, second3_ref)):
        blocks_ref[i, pl.ds(0, early), :] = first[pl.ds(base, early), :].astype(bf16)
        blocks_ref[i, pl.ds(early, deep - early), :] = second[...].astype(bf16)
    for i, ref in enumerate(row_refs):
        inverse_ref[i] = ref[pl.ds(8, CELLS), :].astype(bf16)

    def place(group):
        return jnp.bitwise_xor(group // own_blocks, me) * own_blocks + group % own_blocks

    lane = iota((1, width), 1)
    target = jnp.zeros((1, width), f32)
    for i, ref in enumerate(row_refs):
        rows = ref[pl.ds(0, 8), :][0:1, :]
        rows = jnp.where((lane % 16 < own_blocks) & (lane < 32 * nbrs), rows, 0.0)
        target = target + (rows if i == 0 else pltpu.roll(rows, i * own_blocks, 1))
    target = place(target.astype(i32))
    scatter = ((iota((groups, width), 0) == target) & (lane < 32 * nbrs)).astype(bf16)[:, : 32 * nbrs]

    gathered = gathered_ref[...]
    devs = gathered.shape[0]
    lane = iota((8, LANES), 1)
    lefts, rights = [], []
    for start in range(0, devs, 32):
        value = jnp.zeros((8, LANES), f32)
        order = jnp.zeros((8, LANES), f32)
        for i in range(4):
            piece = gathered[start + 8 * i : start + 8 * i + 8]
            here = lane // 32 == i
            value = jnp.where(here, pltpu.roll(piece, 32 * i, 1) if i else piece, value)
            order = jnp.where(here, pltpu.roll(piece, (32 * i + 96) % LANES, 1) if i != 1 else piece, order)
        order = order.astype(i32)
        group, unit = place(order // CELLS), order % CELLS
        for s in range(8):
            left = jnp.where(iota((groups, LANES), 0) == group[s : s + 1], value[s : s + 1], 0.0)
            lefts.append(jnp.concatenate(split(left), axis=0))
            rights.append((iota((CELLS, LANES), 0) == unit[s : s + 1]).astype(bf16))
    right_side = dot_t(jnp.concatenate(lefts, axis=1), jnp.concatenate(rights, axis=1))
    right_side = right_side[:groups] + right_side[groups:]

    own_block = iota((groups, unknowns), 1) // CELLS == iota((groups, unknowns), 0)

    def spread(x):
        wide = jnp.concatenate([x] * (LANES // CELLS), axis=1)
        wide = jnp.concatenate([wide] * (unknowns // LANES), axis=1)
        return jnp.concatenate(split(jnp.where(own_block, wide, 0.0)), axis=0)

    def product(x, ref):
        wide = spread(x)
        total = None
        for i in range(parts):
            term = dot_t(wide[:, i * width : (i + 1) * width], ref[i])
            total = term if total is None else total + term
        return total[:groups] + total[groups:]

    correction = product(right_side, inverse_ref)
    for _ in range(SWEEPS - 1):
        sums = product(correction, blocks_ref)
        pieces = []
        for k in range(nbrs):
            pieces += split(sums[:, k * CELLS : (k + 1) * CELLS])
        image = jnp.zeros((groups, CELLS), f32)
        high, low = pieces[0::2], pieces[1::2]
        stacked = jnp.concatenate([p for pair in zip(high, low) for p in pair], axis=0)
        image = dot(scatter, stacked)
        correction = correction + product(right_side - image, inverse_ref)
    for r in range(own_blocks // 2):
        both = [correction[2 * r : 2 * r + 1], correction[2 * r + 1 : 2 * r + 2]]
        correction_ref[r : r + 1, :] = jnp.concatenate(both, axis=1)
    correction_copy = pltpu.make_async_copy(correction_ref, correction_any, out_sem_ref.at[0])
    correction_copy.start()

    order = window_of(near_ref, far_ref, own_ref, device_index(), devices)[2].astype(i32)
    rows = order.shape[0]
    unit = jnp.concatenate([order[:, :CELLS], order[:, CELLS:]], axis=0)
    chosen = (iota(unit.shape, 1) == unit % CELLS).astype(bf16)
    values = dot_t(chosen, jnp.concatenate(split(correction), axis=0))
    group = place(unit[:, : 2 * groups] // CELLS)
    values = jnp.sum(jnp.where(iota(values.shape, 1) % groups == group, values, 0.0), axis=1, keepdims=True)
    corr = by_half([values[:rows], values[rows:]], (rows, LANES))
    for copy in copies:
        copy.wait()
    finish(corr, near_ref, far_ref, own_ref, local_ref, devices, selected_ref, fine_ref, smoother_ref, result_ref,
           picked_ref, high_ref, low_ref)
    result_copy = pltpu.make_async_copy(result_ref, out_any, out_sem_ref.at[1])
    result_copy.start()
    correction_copy.wait()
    result_copy.wait()


def finish_kernel(
    devices, corr_ref, near_ref, far_ref, own_ref, selected_ref, local_ref, fine_any, smoother_any, result_ref,
    fine_ref, smoother_ref, picked_ref, high_ref, low_ref, sem_ref,
):
    copies = fetch(sem_ref, (fine_any, fine_ref), (smoother_any, smoother_ref))
    for copy in copies:
        copy.wait()
    finish(corr_ref[...], near_ref, far_ref, own_ref, local_ref, devices, selected_ref, fine_ref, smoother_ref,
           result_ref, picked_ref, high_ref, low_ref)


def call(kernel, out_shape, ins, outs=None, scratch=()):
    spaces = dict(s=pltpu.SMEM, v=pltpu.VMEM, a=pl.ANY)
    many = isinstance(out_shape, tuple)
    specs = tuple(pl.BlockSpec(memory_space=spaces[c]) for c in outs or "v" * (len(out_shape) if many else 1))
    run = pl.pallas_call(
        kernel,
        out_shape=out_shape,
        in_specs=[pl.BlockSpec(memory_space=spaces[c]) for c in ins],
        out_specs=specs if many else specs[0],
        scratch_shapes=list(scratch),
        compiler_params=pltpu.CompilerParams(vmem_limit_bytes=VMEM_LIMIT),
    )

    def placed(*operands):
        return run(*(pltpu.with_memory_space_constraint(x, pltpu.HBM) if c == "a" else x for x, c in zip(operands, ins)))

    return placed


def shape_of(*dims):
    return jax.ShapeDtypeStruct(dims, f32)


def coarse_by_parts(restricted, coarse_order, coarse_values, coarse_rows, coarse_inverse):
    own = coarse_inverse.shape[1]
    own_blocks = own // CELLS
    total = own * lax.axis_size("coarse")
    start = lax.axis_index("coarse") * own
    side = jnp.zeros((total,), f32).at[coarse_order].add(restricted)
    side = lax.dynamic_slice_in_dim(lax.psum(side, BOTH), start, own)
    values = coarse_values.astype(f32).reshape(-1, CELLS, own_blocks, CELLS)
    inverse = coarse_inverse.astype(f32).reshape(CELLS, own_blocks, CELLS)

    def scale(x):
        x = x.reshape(own_blocks, CELLS)
        return jnp.einsum("oji,ji->jo", inverse, x, precision=lax.Precision.HIGHEST).reshape(-1)

    correction = scale(side)
    for _ in range(SWEEPS - 1):
        x = correction.reshape(own_blocks, CELLS)
        sums = jnp.einsum("vfmd,md->vmf", values, x, precision=lax.Precision.HIGHEST)
        image = jax.ops.segment_sum(
            sums.reshape(-1, CELLS), coarse_rows.reshape(-1), num_segments=total // CELLS
        ).reshape(-1)
        image = lax.dynamic_slice_in_dim(lax.psum(image, "coarse"), start, own)
        correction = correction + scale(side - image)
    return correction, lax.all_gather(correction, "coarse", axis=0, tiled=True)


def shards(
    devices, rhs, fine_values, fine_columns, smoother, reaction, pit_counts, weights, coarse_order,
    coarse_values, coarse_rows, coarse_inverse,
):
    cells = rhs.shape[0]
    pairs = cells // LANES
    aggs = 2 * pairs
    nbrs = fine_columns.shape[0]
    parts = lax.axis_size("coarse")
    rhs, reaction, weights = (x.reshape(pairs, LANES) for x in (rhs, reaction, weights))
    rows = pairs + 2 * HALO_ROWS
    vector = pltpu.VMEM((pairs, LANES), f32)
    fine_buffer = pltpu.VMEM(fine_values.shape, bf16)
    smoother_buffer = pltpu.VMEM(smoother.shape, bf16)
    products = [pltpu.VMEM((CELLS, cells), bf16)] * 2
    picked = pltpu.VMEM((nbrs * pairs, LANES), f32)
    copies = pltpu.SemaphoreType.DMA((4,))
    edge = shape_of(3, HALO_ROWS, LANES)

    copied = parts == 4 and devices % 32 == 0 and devices <= 64
    start_shapes = (edge, edge, shape_of(3, pairs, LANES))
    start_ins = (rhs, weights, coarse_order.reshape(1, aggs), smoother)
    start_scratch = [vector, vector, pltpu.VMEM((1, aggs), i32), smoother_buffer]
    if copied:
        deep = coarse_values.shape[0] * CELLS
        width = coarse_inverse.shape[1]
        early = EARLY * CELLS
        near, onward, own, packed, first, second = call(
            start_pack_kernel,
            (*start_shapes, shape_of(8 + CELLS + deep, width), shape_of(8 + CELLS + early, width),
             shape_of(deep - early, width)),
            "aaaaaaa",
            scratch=[
                *start_scratch, pltpu.VMEM(coarse_rows.shape[::-1], i32), pltpu.VMEM((deep, width), bf16),
                pltpu.VMEM(coarse_inverse.shape, bf16), *products, pltpu.SemaphoreType.DMA((7,)),
            ],
        )(*start_ins, coarse_rows.T, coarse_values.reshape(deep, width), coarse_inverse)
        swap = [(c, c ^ 1) for c in range(parts)]
        across = [(c, c ^ 2) for c in range(parts)]
        first2 = lax.ppermute(first, "coarse", across)
    else:
        near, onward, own = call(start_kernel, start_shapes, "aaaa", scratch=[*start_scratch, *products, copies])(
            *start_ins
        )

    partner = [(d, d ^ 1) for d in range(devices)]
    chain = []
    for d in range(devices):
        target = d + 2 if d % 2 == 0 else d - 2
        chain.append((d, target if 0 <= target < devices else d ^ 1))
    onward = lax.ppermute(onward, BOTH, partner)
    near = lax.ppermute(near, BOTH, partner)

    far = lax.ppermute(onward, BOTH, chain)
    selected, weighed, local = call(
        prepare_kernel,
        (jax.ShapeDtypeStruct((aggs * nbrs, 4 * rows), bf16), shape_of(nbrs * pairs, 8, LANES), shape_of(4, pairs, LANES)),
        "svaaaa",
        scratch=[vector, vector, pltpu.VMEM(fine_columns.shape, i32), fine_buffer, pltpu.VMEM((CELLS, cells), f32), copies],
    )(pit_counts, own, rhs, reaction, fine_columns, fine_values)

    if copied:
        beside = lax.ppermute(packed, "coarse", swap)
        first2, second, far, near, selected = lax.optimization_barrier((first2, second, far, near, selected))
        second2 = lax.ppermute(second, "coarse", across)
        first3 = lax.ppermute(first2, "coarse", swap)

    sent = call(
        functools.partial(residual_kernel, devices), shape_of(devices, LANES), "vvvvvv", scratch=[picked]
    )(near, far, own, selected, weighed, local)

    finish_scratch = [ fine_buffer, smoother_buffer, picked, *products, copies]
    common = (near, far, own, selected, local)
    fetched = (fine_values, smoother)
    if copied:
        gathered = lax.all_to_all(sent, BOTH, 0, 0, tiled=True)
        first3, second2, gathered = lax.optimization_barrier((first3, second2, gathered))
        pieces = (packed, beside, first2, second2, first3, lax.ppermute(second2, "coarse", swap))
        result, correction = call(
            functools.partial(solve_kernel, devices),
            (shape_of(pairs, LANES), shape_of(width // LANES, LANES)),
            "vvvvvv" + "vvvvvv" + "aa",
            outs="aa",
            scratch=[
                pltpu.VMEM((parts, deep, width), bf16), pltpu.VMEM((parts, CELLS, width), bf16),
                vector, pltpu.VMEM((width // LANES, LANES), f32), *finish_scratch, pltpu.SemaphoreType.DMA((2,)),
            ],
        )(gathered, *common, *pieces, *fetched)
        correction = correction.reshape(-1)
    else:
        correction, everywhere = coarse_by_parts(
            sent[0, :aggs], coarse_order, coarse_values, coarse_rows, coarse_inverse
        )
        index = device_index()
        low = jnp.where(index == 0, 0.0, jnp.where(index % 2 == 0, far[2], near[2]))
        high = jnp.where(index == devices - 1, 0.0, jnp.where(index % 2 == 0, near[2], far[2]))
        order = jnp.concatenate([low, own[2], high], axis=0).astype(i32)
        corr = jnp.repeat(everywhere[order[:, ::CELLS]], CELLS, axis=1)
        result = call(
            functools.partial(finish_kernel, devices), shape_of(pairs, LANES), "vvvvvvaa", scratch=finish_scratch
        )(corr, *common, *fetched)
    return result.reshape(-1), correction


def solution(mesh):
    devices = mesh.shape["fine"] * mesh.shape["coarse"]
    in_specs = (
        P(BOTH),
        P(None, None, BOTH),
        P(None, BOTH),
        P(None, BOTH),
        P(BOTH),
        P(BOTH),
        P(BOTH),
        P(BOTH),
        P(None, None, "coarse"),
        P(None, "coarse"),
        P(None, "coarse"),
    )
    return jax.shard_map(
        functools.partial(shards, devices),
        mesh=mesh,
        in_specs=in_specs,
        out_specs=(P(BOTH), P("coarse")),
        check_vma=False,
    )
```

```python
import functools

import jax
import jax.numpy as jnp
from jax import lax
from jax.experimental import pallas as pl
from jax.experimental.pallas import tpu as pltpu
from jax.sharding import PartitionSpec as P

CELLS = 64
LANES = 128
HALO_ROWS = 8
SWEEPS = 4
EARLY = 2
BOTH = ("fine", "coarse")
f32, bf16, i32 = jnp.float32, jnp.bfloat16, jnp.int32
VMEM_LIMIT = 24 * 1024 * 1024


def iota(shape, axis):
    return lax.broadcasted_iota(i32, shape, axis)


def split(x):
    high = x.astype(bf16)
    return high, (x - high.astype(f32)).astype(bf16)


def dot(a, b):
    return lax.dot_general(a, b, (((1,), (0,)), ((), ())), preferred_element_type=f32)


def dot_t(a, b):
    return lax.dot_general(a, b, (((1,), (1,)), ((), ())), preferred_element_type=f32)


def cell_sums(high_ref, low_ref):
    width = high_ref.shape[1]
    pairs = width // LANES
    row, lane = iota((2 * pairs, width), 0), iota((2 * pairs, width), 1)
    member = (lane // CELLS == 2 * (row % pairs) + row // pairs).astype(bf16)
    sums = dot_t(member, high_ref[...]) + dot_t(member, low_ref[...])
    return jnp.concatenate([sums[:pairs], sums[pairs:]], axis=1)


def apply_smoother(vector, smoother_ref, high_ref, low_ref):
    for p in range(vector.shape[0]):
        cols = pl.ds(p * LANES, LANES)
        product = smoother_ref[:, cols].astype(f32) * vector[p : p + 1, :]
        high_ref[:, cols], low_ref[:, cols] = split(product)
    return cell_sums(high_ref, low_ref)


def selection(columns, half_rows, pairs):
    nbrs, aggs = columns.shape
    at, who = iota((pairs, aggs), 1), iota((pairs, aggs), 0)
    entry = iota((pairs, 4 * half_rows), 1) % (2 * half_rows)
    parts = []
    for half in range(2):
        for k in range(nbrs):
            chosen = jnp.where(at == 2 * who + half, columns[k : k + 1].astype(f32), 0.0)
            block = jnp.sum(chosen, axis=1, keepdims=True).astype(i32)
            place = block // 2 + jnp.where(block % 2 == half, 0, half_rows)
            parts.append((entry == place).astype(bf16))
    return jnp.concatenate(parts, axis=0)


def pick(window, selected):
    high, low = split(jnp.concatenate([window, pltpu.roll(window, CELLS, 1)], axis=0))
    picked = dot(selected, jnp.concatenate([high, low], axis=0))
    count = selected.shape[0] // 2
    lane = iota((count, LANES), 1)
    return jnp.where(lane < CELLS, picked[:count], picked[count:])


def apply_fine(window, fine_ref, selected, picked_ref, high_ref, low_ref):
    nbrs, _, width = fine_ref.shape
    pairs = width // LANES
    picked_ref[...] = pick(window, selected)
    for p in range(pairs):
        cols = pl.ds(p * LANES, LANES)
        total = None
        for k in range(nbrs):
            term = fine_ref[k, :, cols].astype(f32) * picked_ref[pl.ds(k * pairs + p, 1), :]
            total = term if total is None else total + term
        high_ref[:, cols], low_ref[:, cols] = split(total)
    return cell_sums(high_ref, low_ref)


def as_columns(row, pairs):
    shape = (pairs, row.shape[1])
    at, who = iota(shape, 1), iota(shape, 0)
    return [
        jnp.sum(jnp.where(at == 2 * who + half, row, 0.0), axis=1, keepdims=True)
        for half in range(2)
    ]


def by_half(columns, shape):
    return jnp.where(iota(shape, 1) < CELLS, columns[0], columns[1])


def fetch(sem_ref, *pairs):
    copies = [pltpu.make_async_copy(src, dst, sem_ref.at[i]) for i, (src, dst) in enumerate(pairs)]
    for copy in copies:
        copy.start()
    return copies


def start(rhs_ref, weights_ref, order_ref, smoother_ref, near_ref, onward_ref, own_ref, high_ref, low_ref):
    pairs = rhs_ref.shape[0]
    smoothed = apply_smoother(rhs_ref[...], smoother_ref, high_ref, low_ref)
    order = by_half(as_columns(order_ref[...].astype(f32), pairs), (pairs, LANES))
    even = lax.axis_index("coarse") % 2 == 0
    for i, part in enumerate((smoothed, weights_ref[...], order)):
        own_ref[i] = part
        bottom, top = part[:HALO_ROWS], part[pairs - HALO_ROWS :]
        near_ref[i] = jnp.where(even, top, bottom)
        onward_ref[i] = jnp.where(even, bottom, top)


def start_kernel(
    rhs_any, weights_any, order_any, smoother_any, near_ref, onward_ref, own_ref, smoother_ref,
    rhs_ref, weights_ref, order_ref, high_ref, low_ref, sem_ref,
):
    copies = fetch(
        sem_ref, (smoother_any, smoother_ref), (rhs_any, rhs_ref), (weights_any, weights_ref), (order_any, order_ref)
    )
    for copy in copies:
        copy.wait()
    start(rhs_ref, weights_ref, order_ref, smoother_ref, near_ref, onward_ref, own_ref, high_ref, low_ref)


def start_pack_kernel(
    rhs_any, weights_any, order_any, smoother_any, rows_any, values_any, inverse_any,
    near_ref, onward_ref, own_ref, smoother_ref, packed_ref, first_ref, second_ref,
    rhs_ref, weights_ref, order_ref, rows_ref, values_ref, inverse_ref, high_ref, low_ref, sem_ref,
):
    copies = fetch(
        sem_ref, (smoother_any, smoother_ref), (rhs_any, rhs_ref), (weights_any, weights_ref), (order_any, order_ref),
        (values_any, values_ref), (inverse_any, inverse_ref), (rows_any, rows_ref),
    )
    for copy in copies[:4]:
        copy.wait()
    start(rhs_ref, weights_ref, order_ref, smoother_ref, near_ref, onward_ref, own_ref, high_ref, low_ref)
    for copy in copies[4:]:
        copy.wait()
    own_blocks, nbrs = rows_ref.shape
    deep, width = values_ref.shape
    at, slot = iota((8, nbrs), 1), iota((8, nbrs), 0)
    block = iota((8, width), 1) // CELLS
    rows = jnp.zeros((8, width), f32)
    for j in range(own_blocks):
        targets = jnp.where(at == slot, rows_ref[j : j + 1, :].astype(f32), 0.0)
        rows = jnp.where(block == j, jnp.sum(targets, axis=1, keepdims=True), rows)
    inverse = inverse_ref[...].astype(f32)
    for ref in (packed_ref, first_ref):
        ref[pl.ds(0, 8), :] = rows
        ref[pl.ds(8, CELLS), :] = inverse
    base = 8 + CELLS
    early = first_ref.shape[0] - base
    for r in range(0, deep, CELLS):
        values = values_ref[pl.ds(r, CELLS), :].astype(f32)
        packed_ref[pl.ds(base + r, CELLS), :] = values
        if r < early:
            first_ref[pl.ds(base + r, CELLS), :] = values
        else:
            second_ref[pl.ds(r - early, CELLS), :] = values


def window_of(near_ref, far_ref, own_ref, device, devices):
    even = device % 2 == 0
    near, far = near_ref[...], far_ref[...]
    low = jnp.where(device == 0, 0.0, jnp.where(even, far, near))
    high = jnp.where(device == devices - 1, 0.0, jnp.where(even, near, far))
    return [jnp.concatenate([low[i], own_ref[i], high[i]], axis=0) for i in range(3)]


def device_index():
    return lax.axis_index("fine") * lax.axis_size("coarse") + lax.axis_index("coarse")


def prepare_kernel(
    counts_ref, own_ref, rhs_any, reaction_any, columns_any, fine_any, selected_ref, weighed_ref, local_ref, fine_ref,
    rhs_ref, reaction_ref, columns_ref, wide_ref, sem_ref,
):
    copies = fetch(
        sem_ref, (fine_any, fine_ref), (columns_any, columns_ref), (rhs_any, rhs_ref), (reaction_any, reaction_ref)
    )
    for copy in copies[1:]:
        copy.wait()
    pairs = rhs_ref.shape[0]
    nbrs, _, width = fine_ref.shape
    weights = own_ref[1]
    agg = 2 * iota((pairs, LANES), 0) + iota((pairs, LANES), 1) // CELLS
    reaction = jnp.where(agg < counts_ref[0], reaction_ref[...], 0.0)
    local_ref[0] = weights * rhs_ref[...]
    local_ref[1] = weights * reaction
    local_ref[2] = rhs_ref[...]
    local_ref[3] = reaction
    selected_ref[...] = selection(columns_ref[...], pairs + 2 * HALO_ROWS, pairs)
    by_agg = jnp.concatenate([weights[:, :CELLS], weights[:, CELLS:]], axis=0)
    row, lane = iota((2 * pairs, width), 0), iota((2 * pairs, width), 1)
    member = (lane // CELLS == 2 * (row % pairs) + row // pairs).astype(bf16)
    wide = None
    for part in split(by_agg):
        term = lax.dot_general(part, member, (((0,), (0,)), ((), ())), preferred_element_type=f32)
        wide = term if wide is None else wide + term
    wide_ref[...] = wide
    copies[0].wait()
    for p in range(pairs):
        cols = pl.ds(p * LANES, LANES)
        scale = wide_ref[:, cols]
        for k in range(nbrs):
            term = fine_ref[k, :, cols].astype(f32) * scale
            total = term[:8]
            for r in range(8, CELLS, 8):
                total = total + term[r : r + 8]
            weighed_ref[k * pairs + p] = total


def residual_kernel(
    devices, near_ref, far_ref, own_ref, selected_ref, weighed_ref, local_ref, out_ref, picked_ref,
):
    smoothed, _, _ = window_of(near_ref, far_ref, own_ref, device_index(), devices)
    picked_ref[...] = pick(smoothed, selected_ref[...])
    pairs = own_ref.shape[1]
    nbrs = picked_ref.shape[0] // pairs
    images = []
    for p in range(pairs):
        total = None
        for k in range(nbrs):
            term = weighed_ref[k * pairs + p] * picked_ref[pl.ds(k * pairs + p, 1), :]
            total = term if total is None else total + term
        images.append(jnp.sum(total, axis=0, keepdims=True))
    weighted = local_ref[0] - local_ref[1] * own_ref[0] - jnp.concatenate(images, axis=0)
    shape = (pairs, LANES)
    lane, who = iota(shape, 1), iota(shape, 0)
    row = jnp.zeros((1, LANES), f32)
    for half in range(2):
        inside = lane // CELLS == half
        restricted = jnp.sum(jnp.where(inside, weighted, 0.0), axis=1, keepdims=True)
        order = jnp.max(jnp.where(inside, own_ref[2], 0.0), axis=1, keepdims=True)
        spread = jnp.where(lane == 2 * who + half, restricted, 0.0)
        spread = spread + jnp.where(lane == 2 * (pairs + who) + half, order, 0.0)
        row = row + jnp.sum(spread, axis=0, keepdims=True)
    out_ref[...] = jnp.broadcast_to(row, out_ref.shape)


def finish(corr, near_ref, far_ref, own_ref, local_ref, devices, selected_ref, fine_ref, smoother_ref, result_ref,
           picked_ref, high_ref, low_ref):
    smoothed, weights, _ = window_of(near_ref, far_ref, own_ref, device_index(), devices)
    corrected = smoothed + weights * corr
    pairs = own_ref.shape[1]
    mine = corrected[HALO_ROWS : HALO_ROWS + pairs]
    image = apply_fine(corrected, fine_ref, selected_ref[...], picked_ref, high_ref, low_ref)
    image = image + local_ref[3] * mine
    result_ref[...] = mine + apply_smoother(local_ref[2] - image, smoother_ref, high_ref, low_ref)


def place(group, own_blocks):
    return jnp.bitwise_xor(group // own_blocks, lax.axis_index("coarse")) * own_blocks + group % own_blocks


def pairs_of(x):
    half = x.shape[0] // 2
    return jnp.concatenate([x[:half], x[half:]], axis=1)


def masked_rows(x, mask_lists, pair_at, held_ref):
    pairs = x.shape[0]
    high, low = split(x)
    held_ref[pl.ds(0, pairs), :] = high.astype(f32)
    held_ref[pl.ds(pairs, pairs), :] = low.astype(f32)
    parts = []
    for part in range(2):
        rows = [
            jnp.broadcast_to(held_ref[pl.ds(part * pairs + p, 1), :], (2 * pairs, LANES)).astype(bf16)
            for p in range(pairs)
        ]
        parts.append(rows)
    return jnp.concatenate(
        [
            jnp.concatenate([mask * rows[pair_at(c)] for c, mask in enumerate(masks)], axis=1)
            for masks in mask_lists
            for rows in parts
        ],
        axis=0,
    )


def inverse_product(x, inverse_ref, held_ref):
    pairs = x.shape[0]
    groups = 2 * pairs
    row, lane = iota((groups, LANES), 0), iota((groups, LANES), 1)
    masks = [((row % pairs == p) & (row // pairs == lane // CELLS)).astype(bf16) for p in range(pairs)]
    sums = dot(masked_rows(x, [masks], lambda c: c, held_ref), inverse_ref[...])
    return pairs_of(sums[:groups] + sums[groups:])


def slot_pair(rows_ref, first, count):
    turned = rows_ref[pl.ds(first, CELLS * count), :].astype(bf16).T
    return turned if count == 2 else jnp.concatenate([turned, jnp.zeros_like(turned)], axis=1)


def first_sweep_kernel(
    gathered_ref, mine_ref, beside_ref, first2_ref, second2_ref, first3_ref,
    side_ref, begun_ref, inverse_ref, target_ref, blocks_ref, held_ref,
):
    part_refs = (mine_ref, beside_ref, first2_ref, first3_ref)
    width = mine_ref.shape[1]
    own_blocks = width // CELLS
    pairs = side_ref.shape[0]
    groups = 2 * pairs
    base = 8 + CELLS
    nbrs = (mine_ref.shape[0] - base) // CELLS
    early = (first2_ref.shape[0] - base) // CELLS
    for i, ref in enumerate(part_refs):
        inverse_ref[pl.ds(i * width, width), :] = ref[pl.ds(8, CELLS), :].astype(bf16).T

    gathered = gathered_ref[...]
    devs = gathered.shape[0]
    lane = iota((8, LANES), 1)
    row = iota((groups, LANES), 0)
    number = 2 * (row % pairs) + row // pairs
    lefts, rights = [], []
    for start in range(0, devs, 32):
        value = jnp.zeros((8, LANES), f32)
        order = jnp.zeros((8, LANES), f32)
        for i in range(4):
            piece = gathered[start + 8 * i : start + 8 * i + 8]
            here = lane // 32 == i
            value = jnp.where(here, pltpu.roll(piece, 32 * i, 1) if i else piece, value)
            order = jnp.where(here, pltpu.roll(piece, (32 * i + 96) % LANES, 1) if i != 1 else piece, order)
        order = order.astype(i32)
        group, unit = place(order // CELLS, own_blocks), order % CELLS
        for s in range(8):
            left = jnp.where(number == group[s : s + 1], value[s : s + 1], 0.0)
            lefts.append(jnp.concatenate(split(left), axis=0))
            rights.append((iota((CELLS, LANES), 0) == unit[s : s + 1]).astype(bf16))
    side = dot_t(jnp.concatenate(lefts, axis=1), jnp.concatenate(rights, axis=1))
    side = pairs_of(side[:groups] + side[groups:])
    side_ref[...] = side
    begun_ref[...] = inverse_product(side, inverse_ref, held_ref)

    row = iota((groups, width), 0)
    number = 2 * (row % pairs) + row // pairs
    twos = (nbrs + 1) // 2
    half = twos * width * len(part_refs)
    for i, ref in enumerate(part_refs):
        targets = place(ref[pl.ds(0, 8), :].astype(i32), own_blocks)
        for k in range(2 * twos):
            cols = pl.ds(k % 2 * half + (i * twos + k // 2) * width, width)
            chosen = number == targets[k : k + 1] if k < nbrs else jnp.zeros(row.shape, jnp.bool_)
            target_ref[:, cols] = chosen.astype(bf16)
        for q in range(twos):
            rows = pl.ds((i * twos + q) * width, width)
            count = min(2, nbrs - 2 * q)
            if i < 2 or 2 * q < early:
                blocks_ref[rows, :] = slot_pair(ref, base + 2 * q * CELLS, count)
            elif i == 2:
                blocks_ref[rows, :] = slot_pair(second2_ref, (2 * q - early) * CELLS, count)


def solve_kernel(
    devices, side_ref, begun_ref, inverse_ref, target_ref, blocks_ref, near_ref, far_ref, own_ref, selected_ref,
    local_ref, second3_ref, fine_ref, smoother_ref,
    out_any, correction_any,
    last_ref, held_ref, result_ref, correction_ref,
    picked_ref, high_ref, low_ref, out_sem_ref,
):
    width = second3_ref.shape[1]
    own_blocks = width // CELLS
    groups, half = target_ref.shape[0], target_ref.shape[1] // 2
    pairs = groups // 2
    late = second3_ref.shape[0] // CELLS
    for q in range(0, late, 2):
        last_ref[pl.ds(q // 2 * width, width), :] = slot_pair(second3_ref, q * CELLS, min(2, late - q))
    per_part = half // LANES // (groups // own_blocks)
    per_block = width // LANES

    def pair_at(chunk):
        return chunk // per_part * per_block + chunk % per_block

    side = side_ref[...]
    correction = begun_ref[...]
    split_at = blocks_ref.shape[0]
    for _ in range(SWEEPS - 1):
        masks = [[target_ref[:, pl.ds(t * half + c, LANES)] for c in range(0, half, LANES)] for t in range(2)]
        spread = masked_rows(correction, masks, pair_at, held_ref)
        sums = dot(spread[:, :split_at], blocks_ref[...]) + dot(spread[:, split_at:], last_ref[...])
        image = sums[:groups] + sums[groups : 2 * groups]
        other = sums[2 * groups : 3 * groups] + sums[3 * groups :]
        image = pairs_of(image[:, :CELLS] + other[:, CELLS:])
        correction = correction + inverse_product(side - image, inverse_ref, held_ref)
    correction_ref[...] = correction[: own_blocks // 2]
    correction_copy = pltpu.make_async_copy(correction_ref, correction_any, out_sem_ref.at[0])
    correction_copy.start()

    order = window_of(near_ref, far_ref, own_ref, device_index(), devices)[2].astype(i32)
    rows = order.shape[0]
    unit = jnp.concatenate([order[:, :CELLS], order[:, CELLS:]], axis=0)
    chosen = (iota(unit.shape, 1) == unit % CELLS).astype(bf16)
    by_block = jnp.concatenate([correction[:, :CELLS], correction[:, CELLS:]], axis=0)
    values = dot_t(chosen, jnp.concatenate(split(by_block), axis=0))
    group = place(unit[:, : 2 * groups] // CELLS, own_blocks)
    group = group // 2 + group % 2 * pairs
    values = jnp.sum(jnp.where(iota(values.shape, 1) % groups == group, values, 0.0), axis=1, keepdims=True)
    corr = by_half([values[:rows], values[rows:]], (rows, LANES))
    finish(corr, near_ref, far_ref, own_ref, local_ref, devices, selected_ref, fine_ref, smoother_ref, result_ref,
           picked_ref, high_ref, low_ref)
    result_copy = pltpu.make_async_copy(result_ref, out_any, out_sem_ref.at[1])
    result_copy.start()
    correction_copy.wait()
    result_copy.wait()


def finish_kernel(
    devices, corr_ref, near_ref, far_ref, own_ref, selected_ref, local_ref, fine_ref, smoother_ref, result_ref,
    picked_ref, high_ref, low_ref,
):
    finish(corr_ref[...], near_ref, far_ref, own_ref, local_ref, devices, selected_ref, fine_ref, smoother_ref,
           result_ref, picked_ref, high_ref, low_ref)


def call(kernel, out_shape, ins, outs=None, scratch=()):
    spaces = dict(s=pltpu.SMEM, v=pltpu.VMEM, a=pl.ANY)
    many = isinstance(out_shape, tuple)
    specs = tuple(pl.BlockSpec(memory_space=spaces[c]) for c in outs or "v" * (len(out_shape) if many else 1))
    run = pl.pallas_call(
        kernel,
        out_shape=out_shape,
        in_specs=[pl.BlockSpec(memory_space=spaces[c]) for c in ins],
        out_specs=specs if many else specs[0],
        scratch_shapes=list(scratch),
        compiler_params=pltpu.CompilerParams(vmem_limit_bytes=VMEM_LIMIT),
    )

    def placed(*operands):
        return run(*(pltpu.with_memory_space_constraint(x, pltpu.HBM) if c == "a" else x for x, c in zip(operands, ins)))

    return placed


def shape_of(*dims):
    return jax.ShapeDtypeStruct(dims, f32)


def coarse_by_parts(restricted, coarse_order, coarse_values, coarse_rows, coarse_inverse):
    own = coarse_inverse.shape[1]
    own_blocks = own // CELLS
    total = own * lax.axis_size("coarse")
    start = lax.axis_index("coarse") * own
    side = jnp.zeros((total,), f32).at[coarse_order].add(restricted)
    side = lax.dynamic_slice_in_dim(lax.psum(side, BOTH), start, own)
    values = coarse_values.astype(f32).reshape(-1, CELLS, own_blocks, CELLS)
    inverse = coarse_inverse.astype(f32).reshape(CELLS, own_blocks, CELLS)

    def scale(x):
        x = x.reshape(own_blocks, CELLS)
        return jnp.einsum("oji,ji->jo", inverse, x, precision=lax.Precision.HIGHEST).reshape(-1)

    correction = scale(side)
    for _ in range(SWEEPS - 1):
        x = correction.reshape(own_blocks, CELLS)
        sums = jnp.einsum("vfmd,md->vmf", values, x, precision=lax.Precision.HIGHEST)
        image = jax.ops.segment_sum(
            sums.reshape(-1, CELLS), coarse_rows.reshape(-1), num_segments=total // CELLS
        ).reshape(-1)
        image = lax.dynamic_slice_in_dim(lax.psum(image, "coarse"), start, own)
        correction = correction + scale(side - image)
    return correction, lax.all_gather(correction, "coarse", axis=0, tiled=True)


def shards(
    devices, rhs, fine_values, fine_columns, smoother, reaction, pit_counts, weights, coarse_order,
    coarse_values, coarse_rows, coarse_inverse,
):
    cells = rhs.shape[0]
    pairs = cells // LANES
    aggs = 2 * pairs
    nbrs = fine_columns.shape[0]
    parts = lax.axis_size("coarse")
    rhs, reaction, weights = (x.reshape(pairs, LANES) for x in (rhs, reaction, weights))
    rows = pairs + 2 * HALO_ROWS
    vector = pltpu.VMEM((pairs, LANES), f32)
    products = [pltpu.VMEM((CELLS, cells), bf16)] * 2
    picked = pltpu.VMEM((nbrs * pairs, LANES), f32)
    copies = pltpu.SemaphoreType.DMA((4,))
    edge = shape_of(3, HALO_ROWS, LANES)

    copied = parts == 4 and devices % 32 == 0 and devices <= 64
    start_shapes = (
        edge, edge, shape_of(3, pairs, LANES), jax.ShapeDtypeStruct(smoother.shape, bf16)
    )
    start_ins = (rhs, weights, coarse_order.reshape(1, aggs), smoother)
    start_scratch = [vector, vector, pltpu.VMEM((1, aggs), i32)]
    if copied:
        deep = coarse_values.shape[0] * CELLS
        width = coarse_inverse.shape[1]
        early = EARLY * CELLS
        near, onward, own, smoother_here, packed, first, second = call(
            start_pack_kernel,
            (*start_shapes, shape_of(8 + CELLS + deep, width), shape_of(8 + CELLS + early, width),
             shape_of(deep - early, width)),
            "aaaaaaa",
            scratch=[
                *start_scratch, pltpu.VMEM(coarse_rows.shape[::-1], i32), pltpu.VMEM((deep, width), bf16),
                pltpu.VMEM(coarse_inverse.shape, bf16), *products, pltpu.SemaphoreType.DMA((7,)),
            ],
        )(*start_ins, coarse_rows.T, coarse_values.reshape(deep, width), coarse_inverse)
        swap = [(c, c ^ 1) for c in range(parts)]
        across = [(c, c ^ 2) for c in range(parts)]
        first2 = lax.ppermute(first, "coarse", across)
    else:
        near, onward, own, smoother_here = call(start_kernel, start_shapes, "aaaa", scratch=[*start_scratch, *products, copies])(
            *start_ins
        )

    partner = [(d, d ^ 1) for d in range(devices)]
    chain = []
    for d in range(devices):
        target = d + 2 if d % 2 == 0 else d - 2
        chain.append((d, target if 0 <= target < devices else d ^ 1))
    onward = lax.ppermute(onward, BOTH, partner)
    near = lax.ppermute(near, BOTH, partner)

    far = lax.ppermute(onward, BOTH, chain)
    selected, weighed, local, fine_here = call(
        prepare_kernel,
        (jax.ShapeDtypeStruct((aggs * nbrs, 4 * rows), bf16), shape_of(nbrs * pairs, 8, LANES), shape_of(4, pairs, LANES),
         jax.ShapeDtypeStruct(fine_values.shape, bf16)),
        "svaaaa",
        scratch=[vector, vector, pltpu.VMEM(fine_columns.shape, i32), pltpu.VMEM((CELLS, cells), f32), copies],
    )(pit_counts, own, rhs, reaction, fine_columns, fine_values)

    if copied:
        beside = lax.ppermute(packed, "coarse", swap)
        first2, second, far, near, selected = lax.optimization_barrier((first2, second, far, near, selected))
        second2 = lax.ppermute(second, "coarse", across)
        first3 = lax.ppermute(first2, "coarse", swap)

    sent = call(
        functools.partial(residual_kernel, devices), shape_of(devices, LANES), "vvvvvv", scratch=[picked]
    )(near, far, own, selected, weighed, local)

    finish_scratch = [picked, *products]
    common = (near, far, own, selected, local)
    fetched = (fine_here, smoother_here)
    if copied:
        gathered = lax.all_to_all(sent, BOTH, 0, 0, tiled=True)
        first3, second2, gathered = lax.optimization_barrier((first3, second2, gathered))
        second3 = lax.ppermute(second2, "coarse", swap)
        unknowns = parts * width
        groups = unknowns // CELLS
        twos, late = (nbrs + 1) // 2, (nbrs - EARLY + 1) // 2
        begun = call(
            first_sweep_kernel,
            (shape_of(unknowns // LANES, LANES), shape_of(unknowns // LANES, LANES),
             jax.ShapeDtypeStruct((unknowns, CELLS), bf16), jax.ShapeDtypeStruct((groups, 2 * twos * unknowns), bf16),
             jax.ShapeDtypeStruct((twos * unknowns - late * width, LANES), bf16)),
            "vvvvvv",
            scratch=[pltpu.VMEM((groups, LANES), f32)],
        )(gathered, packed, beside, first2, second2, first3)
        result, correction = call(
            functools.partial(solve_kernel, devices),
            (shape_of(pairs, LANES), shape_of(width // LANES, LANES)),
            "vvvvv" + "vvvvv" + "vvv",
            outs="aa",
            scratch=[
                pltpu.VMEM((late * width, LANES), bf16), pltpu.VMEM((groups, LANES), f32), vector,
                pltpu.VMEM((width // LANES, LANES), f32), *finish_scratch, pltpu.SemaphoreType.DMA((2,)),
            ],
        )(*begun, *common, second3, *fetched)
        correction = correction.reshape(-1)
    else:
        correction, everywhere = coarse_by_parts(
            sent[0, :aggs], coarse_order, coarse_values, coarse_rows, coarse_inverse
        )
        index = device_index()
        low = jnp.where(index == 0, 0.0, jnp.where(index % 2 == 0, far[2], near[2]))
        high = jnp.where(index == devices - 1, 0.0, jnp.where(index % 2 == 0, near[2], far[2]))
        order = jnp.concatenate([low, own[2], high], axis=0).astype(i32)
        corr = jnp.repeat(everywhere[order[:, ::CELLS]], CELLS, axis=1)
        result = call(
            functools.partial(finish_kernel, devices), shape_of(pairs, LANES), "vvvvvvvv", scratch=finish_scratch
        )(corr, *common, *fetched)
    return result.reshape(-1), correction


def solution(mesh):
    devices = mesh.shape["fine"] * mesh.shape["coarse"]
    in_specs = (
        P(BOTH),
        P(None, None, BOTH),
        P(None, BOTH),
        P(None, BOTH),
        P(BOTH),
        P(BOTH),
        P(BOTH),
        P(BOTH),
        P(None, None, "coarse"),
        P(None, "coarse"),
        P(None, "coarse"),
    )
    return jax.shard_map(
        functools.partial(shards, devices),
        mesh=mesh,
        in_specs=in_specs,
        out_specs=(P(BOTH), P("coarse")),
        check_vma=False,
    )
```

```python
import functools

import jax
import jax.numpy as jnp
from jax import lax
from jax.experimental import pallas as pl
from jax.experimental.pallas import tpu as pltpu
from jax.sharding import PartitionSpec as P

CELLS = 64
LANES = 128
HALO_ROWS = 8
SWEEPS = 4
EARLY = 2
BOTH = ("fine", "coarse")
f32, bf16, i32 = jnp.float32, jnp.bfloat16, jnp.int32
VMEM_LIMIT = 24 * 1024 * 1024


def iota(shape, axis):
    return lax.broadcasted_iota(i32, shape, axis)


def split(x):
    high = x.astype(bf16)
    return high, (x - high.astype(f32)).astype(bf16)


def dot(a, b):
    return lax.dot_general(a, b, (((1,), (0,)), ((), ())), preferred_element_type=f32)


def dot_t(a, b):
    return lax.dot_general(a, b, (((1,), (1,)), ((), ())), preferred_element_type=f32)


def cell_sums(high_ref, low_ref):
    width = high_ref.shape[1]
    pairs = width // LANES
    row, lane = iota((2 * pairs, width), 0), iota((2 * pairs, width), 1)
    member = (lane // CELLS == 2 * (row % pairs) + row // pairs).astype(bf16)
    sums = dot_t(member, high_ref[...]) + dot_t(member, low_ref[...])
    return jnp.concatenate([sums[:pairs], sums[pairs:]], axis=1)


def apply_smoother(vector, smoother_ref, high_ref, low_ref):
    for p in range(vector.shape[0]):
        cols = pl.ds(p * LANES, LANES)
        product = smoother_ref[:, cols].astype(f32) * vector[p : p + 1, :]
        high_ref[:, cols], low_ref[:, cols] = split(product)
    return cell_sums(high_ref, low_ref)


def selection(columns, half_rows, pairs):
    nbrs, aggs = columns.shape
    at, who = iota((pairs, aggs), 1), iota((pairs, aggs), 0)
    entry = iota((pairs, 4 * half_rows), 1) % (2 * half_rows)
    parts = []
    for half in range(2):
        for k in range(nbrs):
            chosen = jnp.where(at == 2 * who + half, columns[k : k + 1].astype(f32), 0.0)
            block = jnp.sum(chosen, axis=1, keepdims=True).astype(i32)
            place = block // 2 + jnp.where(block % 2 == half, 0, half_rows)
            parts.append((entry == place).astype(bf16))
    return jnp.concatenate(parts, axis=0)


def pick(window, selected):
    high, low = split(jnp.concatenate([window, pltpu.roll(window, CELLS, 1)], axis=0))
    picked = dot(selected, jnp.concatenate([high, low], axis=0))
    count = selected.shape[0] // 2
    lane = iota((count, LANES), 1)
    return jnp.where(lane < CELLS, picked[:count], picked[count:])


def apply_smoothed_fine(window, products_ref, selected, picked_ref, high_ref, low_ref):
    nbrs, _, width = products_ref.shape
    pairs = width // LANES
    picked_ref[...] = pick(window, selected)
    for p in range(pairs):
        cols = pl.ds(p * LANES, LANES)
        total = None
        for k in range(nbrs):
            term = products_ref[k, :, cols] * picked_ref[pl.ds(k * pairs + p, 1), :]
            total = term if total is None else total + term
        high_ref[:, cols], low_ref[:, cols] = split(total)
    return cell_sums(high_ref, low_ref)


def as_columns(row, pairs):
    shape = (pairs, row.shape[1])
    at, who = iota(shape, 1), iota(shape, 0)
    return [
        jnp.sum(jnp.where(at == 2 * who + half, row, 0.0), axis=1, keepdims=True)
        for half in range(2)
    ]


def by_half(columns, shape):
    return jnp.where(iota(shape, 1) < CELLS, columns[0], columns[1])


def fetch(sem_ref, *pairs):
    copies = [pltpu.make_async_copy(src, dst, sem_ref.at[i]) for i, (src, dst) in enumerate(pairs)]
    for copy in copies:
        copy.start()
    return copies


def start(rhs_ref, weights_ref, order_ref, smoother_ref, near_ref, onward_ref, own_ref, high_ref, low_ref):
    pairs = rhs_ref.shape[0]
    smoothed = apply_smoother(rhs_ref[...], smoother_ref, high_ref, low_ref)
    order = by_half(as_columns(order_ref[...].astype(f32), pairs), (pairs, LANES))
    even = lax.axis_index("coarse") % 2 == 0
    for i, part in enumerate((smoothed, weights_ref[...], order)):
        own_ref[i] = part
        bottom, top = part[:HALO_ROWS], part[pairs - HALO_ROWS :]
        near_ref[i] = jnp.where(even, top, bottom)
        onward_ref[i] = jnp.where(even, bottom, top)


def start_kernel(
    rhs_any, weights_any, order_any, smoother_any, near_ref, onward_ref, own_ref, smoother_ref,
    rhs_ref, weights_ref, order_ref, high_ref, low_ref, sem_ref,
):
    copies = fetch(
        sem_ref, (smoother_any, smoother_ref), (rhs_any, rhs_ref), (weights_any, weights_ref), (order_any, order_ref)
    )
    for copy in copies:
        copy.wait()
    start(rhs_ref, weights_ref, order_ref, smoother_ref, near_ref, onward_ref, own_ref, high_ref, low_ref)


def start_pack_kernel(
    rhs_any, weights_any, order_any, smoother_any, rows_any, values_any, inverse_any,
    near_ref, onward_ref, own_ref, smoother_ref, packed_ref, first_ref, second_ref,
    rhs_ref, weights_ref, order_ref, rows_ref, values_ref, inverse_ref, high_ref, low_ref, sem_ref,
):
    copies = fetch(
        sem_ref, (smoother_any, smoother_ref), (rhs_any, rhs_ref), (weights_any, weights_ref), (order_any, order_ref),
        (values_any, values_ref), (inverse_any, inverse_ref), (rows_any, rows_ref),
    )
    for copy in copies[:4]:
        copy.wait()
    start(rhs_ref, weights_ref, order_ref, smoother_ref, near_ref, onward_ref, own_ref, high_ref, low_ref)
    for copy in copies[4:]:
        copy.wait()
    own_blocks, nbrs = rows_ref.shape
    deep, width = values_ref.shape
    at, slot = iota((8, nbrs), 1), iota((8, nbrs), 0)
    block = iota((8, width), 1) // CELLS
    rows = jnp.zeros((8, width), f32)
    for j in range(own_blocks):
        targets = jnp.where(at == slot, rows_ref[j : j + 1, :].astype(f32), 0.0)
        rows = jnp.where(block == j, jnp.sum(targets, axis=1, keepdims=True), rows)
    inverse = inverse_ref[...].astype(f32)
    for ref in (packed_ref, first_ref):
        ref[pl.ds(0, 8), :] = rows
        ref[pl.ds(8, CELLS), :] = inverse
    base = 8 + CELLS
    early = first_ref.shape[0] - base
    for r in range(0, deep, CELLS):
        values = values_ref[pl.ds(r, CELLS), :].astype(f32)
        packed_ref[pl.ds(base + r, CELLS), :] = values
        if r < early:
            first_ref[pl.ds(base + r, CELLS), :] = values
        else:
            second_ref[pl.ds(r - early, CELLS), :] = values


def window_of(near_ref, far_ref, own_ref, device, devices):
    even = device % 2 == 0
    near, far = near_ref[...], far_ref[...]
    low = jnp.where(device == 0, 0.0, jnp.where(even, far, near))
    high = jnp.where(device == devices - 1, 0.0, jnp.where(even, near, far))
    return [jnp.concatenate([low[i], own_ref[i], high[i]], axis=0) for i in range(3)]


def device_index():
    return lax.axis_index("fine") * lax.axis_size("coarse") + lax.axis_index("coarse")


def prepare_kernel(
    counts_ref, own_ref, rhs_any, reaction_any, columns_any, fine_any, smoother_ref, selected_ref, weighed_ref, local_ref,
    products_ref, rhs_ref, reaction_ref, columns_ref, fine_ref, wide_ref, sem_ref,
):
    copies = fetch(
        sem_ref, (columns_any, columns_ref), (rhs_any, rhs_ref), (reaction_any, reaction_ref),
        *((fine_any.at[k], fine_ref.at[k]) for k in range(fine_ref.shape[0])),
    )
    for copy in copies[:3]:
        copy.wait()
    pairs = rhs_ref.shape[0]
    nbrs, _, width = fine_ref.shape
    weights = own_ref[1]
    agg = 2 * iota((pairs, LANES), 0) + iota((pairs, LANES), 1) // CELLS
    reaction = jnp.where(agg < counts_ref[0], reaction_ref[...], 0.0)
    local_ref[0] = weights * rhs_ref[...]
    local_ref[1] = weights * reaction
    selected_ref[...] = selection(columns_ref[...], pairs + 2 * HALO_ROWS, pairs)
    by_agg = jnp.concatenate([weights[:, :CELLS], weights[:, CELLS:]], axis=0)
    row, lane = iota((2 * pairs, width), 0), iota((2 * pairs, width), 1)
    member = (lane // CELLS == 2 * (row % pairs) + row // pairs).astype(bf16)
    wide = None
    for part in split(by_agg):
        term = lax.dot_general(part, member, (((0,), (0,)), ((), ())), preferred_element_type=f32)
        wide = term if wide is None else wide + term
    wide_ref[...] = wide
    for k in range(nbrs):
        copies[3 + k].wait()
        for p in range(pairs):
            cols = pl.ds(p * LANES, LANES)
            term = fine_ref[k, :, cols].astype(f32) * wide_ref[:, cols]
            total = term[:8]
            for r in range(8, CELLS, 8):
                total = total + term[r : r + 8]
            weighed_ref[k * pairs + p] = total
    lane = iota((CELLS, LANES), 1)
    for p in range(pairs):
        cols = pl.ds(p * LANES, LANES)
        left = smoother_ref[:, cols]
        rights = []
        for k in range(nbrs):
            block = fine_ref[k, :, cols]
            zero = jnp.zeros_like(block)
            apart = [jnp.where(lane < CELLS, block, zero), jnp.where(lane < CELLS, zero, block)]
            rights.append(jnp.concatenate(apart, axis=0))
        both = dot(left, jnp.concatenate(rights, axis=1))
        for k in range(nbrs):
            product = both[:, k * LANES : (k + 1) * LANES]
            products_ref[k, :, cols] = product if k else product + left.astype(f32) * reaction[p : p + 1]


def residual_kernel(
    devices, near_ref, far_ref, own_ref, selected_ref, weighed_ref, local_ref, out_ref, picked_ref,
):
    smoothed, _, _ = window_of(near_ref, far_ref, own_ref, device_index(), devices)
    picked_ref[...] = pick(smoothed, selected_ref[...])
    pairs = own_ref.shape[1]
    nbrs = picked_ref.shape[0] // pairs
    images = []
    for p in range(pairs):
        total = None
        for k in range(nbrs):
            term = weighed_ref[k * pairs + p] * picked_ref[pl.ds(k * pairs + p, 1), :]
            total = term if total is None else total + term
        images.append(jnp.sum(total, axis=0, keepdims=True))
    weighted = local_ref[0] - local_ref[1] * own_ref[0] - jnp.concatenate(images, axis=0)
    shape = (pairs, LANES)
    lane, who = iota(shape, 1), iota(shape, 0)
    row = jnp.zeros((1, LANES), f32)
    for half in range(2):
        inside = lane // CELLS == half
        restricted = jnp.sum(jnp.where(inside, weighted, 0.0), axis=1, keepdims=True)
        order = jnp.max(jnp.where(inside, own_ref[2], 0.0), axis=1, keepdims=True)
        spread = jnp.where(lane == 2 * who + half, restricted, 0.0)
        spread = spread + jnp.where(lane == 2 * (pairs + who) + half, order, 0.0)
        row = row + jnp.sum(spread, axis=0, keepdims=True)
    out_ref[...] = jnp.broadcast_to(row, out_ref.shape)


def finish(corr, near_ref, far_ref, own_ref, devices, selected_ref, products_ref, result_ref,
           picked_ref, high_ref, low_ref):
    smoothed, weights, _ = window_of(near_ref, far_ref, own_ref, device_index(), devices)
    corrected = smoothed + weights * corr
    mine = corrected[HALO_ROWS : HALO_ROWS + own_ref.shape[1]]
    image = apply_smoothed_fine(corrected, products_ref, selected_ref[...], picked_ref, high_ref, low_ref)
    result_ref[...] = mine + (own_ref[0] - image)


def place(group, own_blocks):
    return jnp.bitwise_xor(group // own_blocks, lax.axis_index("coarse")) * own_blocks + group % own_blocks


def pairs_of(x):
    half = x.shape[0] // 2
    return jnp.concatenate([x[:half], x[half:]], axis=1)


def masked_rows(x, mask_lists, pair_at, held_ref):
    pairs = x.shape[0]
    high, low = split(x)
    held_ref[pl.ds(0, pairs), :] = high.astype(f32)
    held_ref[pl.ds(pairs, pairs), :] = low.astype(f32)
    parts = []
    for part in range(2):
        rows = [
            jnp.broadcast_to(held_ref[pl.ds(part * pairs + p, 1), :], (2 * pairs, LANES)).astype(bf16)
            for p in range(pairs)
        ]
        parts.append(rows)
    return jnp.concatenate(
        [
            jnp.concatenate([mask * rows[pair_at(c)] for c, mask in enumerate(masks)], axis=1)
            for masks in mask_lists
            for rows in parts
        ],
        axis=0,
    )


def inverse_product(x, inverse_ref, held_ref):
    pairs = x.shape[0]
    groups = 2 * pairs
    row, lane = iota((groups, LANES), 0), iota((groups, LANES), 1)
    masks = [((row % pairs == p) & (row // pairs == lane // CELLS)).astype(bf16) for p in range(pairs)]
    sums = dot(masked_rows(x, [masks], lambda c: c, held_ref), inverse_ref[...])
    return pairs_of(sums[:groups] + sums[groups:])


def slot_pair(rows_ref, first, count):
    turned = rows_ref[pl.ds(first, CELLS * count), :].astype(bf16).T
    return turned if count == 2 else jnp.concatenate([turned, jnp.zeros_like(turned)], axis=1)


def target_rows(x, target_ref, start, stop, own_blocks, held_ref):
    groups, half = target_ref.shape[0], target_ref.shape[1] // 2
    per_part = half // LANES // (groups // own_blocks)
    per_block = own_blocks // 2
    masks = [[target_ref[:, pl.ds(t * half + c, LANES)] for c in range(start, stop, LANES)] for t in range(2)]

    def pair_at(chunk):
        chunk = chunk + start // LANES
        return chunk // per_part * per_block + chunk % per_block

    return masked_rows(x, masks, pair_at, held_ref)


def first_sweep_kernel(
    gathered_ref, mine_ref, beside_ref, first2_ref, second2_ref, first3_ref,
    side_ref, begun_ref, inverse_ref, target_ref, blocks_ref, sums_ref, held_ref,
):
    part_refs = (mine_ref, beside_ref, first2_ref, first3_ref)
    width = mine_ref.shape[1]
    own_blocks = width // CELLS
    pairs = side_ref.shape[0]
    groups = 2 * pairs
    base = 8 + CELLS
    nbrs = (mine_ref.shape[0] - base) // CELLS
    early = (first2_ref.shape[0] - base) // CELLS
    for i, ref in enumerate(part_refs):
        inverse_ref[pl.ds(i * width, width), :] = ref[pl.ds(8, CELLS), :].astype(bf16).T

    gathered = gathered_ref[...]
    devs = gathered.shape[0]
    lane = iota((8, LANES), 1)
    row = iota((groups, LANES), 0)
    number = 2 * (row % pairs) + row // pairs
    lefts, rights = [], []
    for start in range(0, devs, 32):
        value = jnp.zeros((8, LANES), f32)
        order = jnp.zeros((8, LANES), f32)
        for i in range(4):
            piece = gathered[start + 8 * i : start + 8 * i + 8]
            here = lane // 32 == i
            value = jnp.where(here, pltpu.roll(piece, 32 * i, 1) if i else piece, value)
            order = jnp.where(here, pltpu.roll(piece, (32 * i + 96) % LANES, 1) if i != 1 else piece, order)
        order = order.astype(i32)
        group, unit = place(order // CELLS, own_blocks), order % CELLS
        for s in range(8):
            left = jnp.where(number == group[s : s + 1], value[s : s + 1], 0.0)
            lefts.append(jnp.concatenate(split(left), axis=0))
            rights.append((iota((CELLS, LANES), 0) == unit[s : s + 1]).astype(bf16))
    side = dot_t(jnp.concatenate(lefts, axis=1), jnp.concatenate(rights, axis=1))
    side = pairs_of(side[:groups] + side[groups:])
    side_ref[...] = side
    begun = inverse_product(side, inverse_ref, held_ref)
    begun_ref[...] = begun

    row = iota((groups, width), 0)
    number = 2 * (row % pairs) + row // pairs
    twos = (nbrs + 1) // 2
    half = twos * width * len(part_refs)
    for i, ref in enumerate(part_refs):
        targets = place(ref[pl.ds(0, 8), :].astype(i32), own_blocks)
        for k in range(2 * twos):
            cols = pl.ds(k % 2 * half + (i * twos + k // 2) * width, width)
            chosen = number == targets[k : k + 1] if k < nbrs else jnp.zeros(row.shape, jnp.bool_)
            target_ref[:, cols] = chosen.astype(bf16)
        for q in range(twos):
            rows = pl.ds((i * twos + q) * width, width)
            count = min(2, nbrs - 2 * q)
            if i < 2 or 2 * q < early:
                blocks_ref[rows, :] = slot_pair(ref, base + 2 * q * CELLS, count)
            elif i == 2:
                blocks_ref[rows, :] = slot_pair(second2_ref, (2 * q - early) * CELLS, count)

    sums_ref[...] = dot(target_rows(begun, target_ref, 0, blocks_ref.shape[0], own_blocks, held_ref), blocks_ref[...])


def solve_kernel(
    devices, side_ref, begun_ref, inverse_ref, target_ref, blocks_ref, sums_ref, near_ref, far_ref, own_ref, selected_ref,
    second3_ref, products_ref,
    out_any, correction_any,
    last_ref, held_ref, result_ref, correction_ref,
    picked_ref, high_ref, low_ref, out_sem_ref,
):
    width = second3_ref.shape[1]
    own_blocks = width // CELLS
    groups, half = target_ref.shape[0], target_ref.shape[1] // 2
    pairs = groups // 2
    late = second3_ref.shape[0] // CELLS
    for q in range(0, late, 2):
        last_ref[pl.ds(q // 2 * width, width), :] = slot_pair(second3_ref, q * CELLS, min(2, late - q))
    side = side_ref[...]
    correction = begun_ref[...]
    split_at = blocks_ref.shape[0]
    for sweep in range(SWEEPS - 1):
        if sweep == 0:
            sums = sums_ref[...]
            spread = target_rows(correction, target_ref, split_at, half, own_blocks, held_ref)
        else:
            spread = target_rows(correction, target_ref, 0, half, own_blocks, held_ref)
            sums = dot(spread[:, :split_at], blocks_ref[...])
            spread = spread[:, split_at:]
        sums = sums + dot(spread, last_ref[...])
        image = sums[:groups] + sums[groups : 2 * groups]
        other = sums[2 * groups : 3 * groups] + sums[3 * groups :]
        image = pairs_of(image[:, :CELLS] + other[:, CELLS:])
        correction = correction + inverse_product(side - image, inverse_ref, held_ref)
    correction_ref[...] = correction[: own_blocks // 2]
    correction_copy = pltpu.make_async_copy(correction_ref, correction_any, out_sem_ref.at[0])
    correction_copy.start()

    order = window_of(near_ref, far_ref, own_ref, device_index(), devices)[2].astype(i32)
    rows = order.shape[0]
    unit = jnp.concatenate([order[:, :CELLS], order[:, CELLS:]], axis=0)
    chosen = (iota(unit.shape, 1) == unit % CELLS).astype(bf16)
    by_block = jnp.concatenate([correction[:, :CELLS], correction[:, CELLS:]], axis=0)
    values = dot_t(chosen, jnp.concatenate(split(by_block), axis=0))
    group = place(unit[:, : 2 * groups] // CELLS, own_blocks)
    group = group // 2 + group % 2 * pairs
    values = jnp.sum(jnp.where(iota(values.shape, 1) % groups == group, values, 0.0), axis=1, keepdims=True)
    corr = by_half([values[:rows], values[rows:]], (rows, LANES))
    finish(corr, near_ref, far_ref, own_ref, devices, selected_ref, products_ref, result_ref,
           picked_ref, high_ref, low_ref)
    result_copy = pltpu.make_async_copy(result_ref, out_any, out_sem_ref.at[1])
    result_copy.start()
    correction_copy.wait()
    result_copy.wait()


def finish_kernel(
    devices, corr_ref, near_ref, far_ref, own_ref, selected_ref, products_ref, result_ref, picked_ref, high_ref, low_ref,
):
    finish(corr_ref[...], near_ref, far_ref, own_ref, devices, selected_ref, products_ref, result_ref,
           picked_ref, high_ref, low_ref)


def call(kernel, out_shape, ins, outs=None, scratch=()):
    spaces = dict(s=pltpu.SMEM, v=pltpu.VMEM, a=pl.ANY)
    many = isinstance(out_shape, tuple)
    specs = tuple(pl.BlockSpec(memory_space=spaces[c]) for c in outs or "v" * (len(out_shape) if many else 1))
    run = pl.pallas_call(
        kernel,
        out_shape=out_shape,
        in_specs=[pl.BlockSpec(memory_space=spaces[c]) for c in ins],
        out_specs=specs if many else specs[0],
        scratch_shapes=list(scratch),
        compiler_params=pltpu.CompilerParams(vmem_limit_bytes=VMEM_LIMIT),
    )

    def placed(*operands):
        return run(*(pltpu.with_memory_space_constraint(x, pltpu.HBM) if c == "a" else x for x, c in zip(operands, ins)))

    return placed


def shape_of(*dims):
    return jax.ShapeDtypeStruct(dims, f32)


def coarse_by_parts(restricted, coarse_order, coarse_values, coarse_rows, coarse_inverse):
    own = coarse_inverse.shape[1]
    own_blocks = own // CELLS
    total = own * lax.axis_size("coarse")
    start = lax.axis_index("coarse") * own
    side = jnp.zeros((total,), f32).at[coarse_order].add(restricted)
    side = lax.dynamic_slice_in_dim(lax.psum(side, BOTH), start, own)
    values = coarse_values.astype(f32).reshape(-1, CELLS, own_blocks, CELLS)
    inverse = coarse_inverse.astype(f32).reshape(CELLS, own_blocks, CELLS)

    def scale(x):
        x = x.reshape(own_blocks, CELLS)
        return jnp.einsum("oji,ji->jo", inverse, x, precision=lax.Precision.HIGHEST).reshape(-1)

    correction = scale(side)
    for _ in range(SWEEPS - 1):
        x = correction.reshape(own_blocks, CELLS)
        sums = jnp.einsum("vfmd,md->vmf", values, x, precision=lax.Precision.HIGHEST)
        image = jax.ops.segment_sum(
            sums.reshape(-1, CELLS), coarse_rows.reshape(-1), num_segments=total // CELLS
        ).reshape(-1)
        image = lax.dynamic_slice_in_dim(lax.psum(image, "coarse"), start, own)
        correction = correction + scale(side - image)
    return correction, lax.all_gather(correction, "coarse", axis=0, tiled=True)


def shards(
    devices, rhs, fine_values, fine_columns, smoother, reaction, pit_counts, weights, coarse_order,
    coarse_values, coarse_rows, coarse_inverse,
):
    cells = rhs.shape[0]
    pairs = cells // LANES
    aggs = 2 * pairs
    nbrs = fine_columns.shape[0]
    parts = lax.axis_size("coarse")
    rhs, reaction, weights = (x.reshape(pairs, LANES) for x in (rhs, reaction, weights))
    rows = pairs + 2 * HALO_ROWS
    vector = pltpu.VMEM((pairs, LANES), f32)
    products = [pltpu.VMEM((CELLS, cells), bf16)] * 2
    picked = pltpu.VMEM((nbrs * pairs, LANES), f32)
    copies = pltpu.SemaphoreType.DMA((4,))
    edge = shape_of(3, HALO_ROWS, LANES)

    copied = parts == 4 and devices % 32 == 0 and devices <= 64
    start_shapes = (
        edge, edge, shape_of(3, pairs, LANES), jax.ShapeDtypeStruct(smoother.shape, bf16)
    )
    start_ins = (rhs, weights, coarse_order.reshape(1, aggs), smoother)
    start_scratch = [vector, vector, pltpu.VMEM((1, aggs), i32)]
    if copied:
        deep = coarse_values.shape[0] * CELLS
        width = coarse_inverse.shape[1]
        early = EARLY * CELLS
        near, onward, own, smoother_here, packed, first, second = call(
            start_pack_kernel,
            (*start_shapes, shape_of(8 + CELLS + deep, width), shape_of(8 + CELLS + early, width),
             shape_of(deep - early, width)),
            "aaaaaaa",
            scratch=[
                *start_scratch, pltpu.VMEM(coarse_rows.shape[::-1], i32), pltpu.VMEM((deep, width), bf16),
                pltpu.VMEM(coarse_inverse.shape, bf16), *products, pltpu.SemaphoreType.DMA((7,)),
            ],
        )(*start_ins, coarse_rows.T, coarse_values.reshape(deep, width), coarse_inverse)
        swap = [(c, c ^ 1) for c in range(parts)]
        across = [(c, c ^ 2) for c in range(parts)]
        first2 = lax.ppermute(first, "coarse", across)
    else:
        near, onward, own, smoother_here = call(start_kernel, start_shapes, "aaaa", scratch=[*start_scratch, *products, copies])(
            *start_ins
        )

    partner = [(d, d ^ 1) for d in range(devices)]
    chain = []
    for d in range(devices):
        target = d + 2 if d % 2 == 0 else d - 2
        chain.append((d, target if 0 <= target < devices else d ^ 1))
    onward = lax.ppermute(onward, BOTH, partner)
    near = lax.ppermute(near, BOTH, partner)

    far = lax.ppermute(onward, BOTH, chain)
    selected, weighed, local, smoothed_fine = call(
        prepare_kernel,
        (jax.ShapeDtypeStruct((aggs * nbrs, 4 * rows), bf16), shape_of(nbrs * pairs, 8, LANES), shape_of(2, pairs, LANES),
         shape_of(*fine_values.shape)),
        "svaaaav",
        scratch=[vector, vector, pltpu.VMEM(fine_columns.shape, i32), pltpu.VMEM(fine_values.shape, bf16), pltpu.VMEM((CELLS, cells), f32), pltpu.SemaphoreType.DMA((3 + nbrs,))],
    )(pit_counts, own, rhs, reaction, fine_columns, fine_values, smoother_here)

    if copied:
        beside = lax.ppermute(packed, "coarse", swap)
        first2, second, far, near, selected, beside = lax.optimization_barrier((first2, second, far, near, selected, beside))
        second2 = lax.ppermute(second, "coarse", across)
        first3 = lax.ppermute(first2, "coarse", swap)

    sent = call(
        functools.partial(residual_kernel, devices), shape_of(devices, LANES), "vvvvvv", scratch=[picked]
    )(near, far, own, selected, weighed, local)

    finish_scratch = [picked, *products]
    common = (near, far, own, selected)
    if copied:
        gathered = lax.all_to_all(sent, BOTH, 0, 0, tiled=True)
        first3, second2, gathered = lax.optimization_barrier((first3, second2, gathered))
        second3 = lax.ppermute(second2, "coarse", swap)
        unknowns = parts * width
        groups = unknowns // CELLS
        twos, late = (nbrs + 1) // 2, (nbrs - EARLY + 1) // 2
        begun = call(
            first_sweep_kernel,
            (shape_of(unknowns // LANES, LANES), shape_of(unknowns // LANES, LANES),
             jax.ShapeDtypeStruct((unknowns, CELLS), bf16), jax.ShapeDtypeStruct((groups, 2 * twos * unknowns), bf16),
             jax.ShapeDtypeStruct((twos * unknowns - late * width, LANES), bf16), shape_of(4 * groups, LANES)),
            "vvvvvv",
            scratch=[pltpu.VMEM((groups, LANES), f32)],
        )(gathered, packed, beside, first2, second2, first3)
        result, correction = call(
            functools.partial(solve_kernel, devices),
            (shape_of(pairs, LANES), shape_of(width // LANES, LANES)),
            "vvvvvv" + "vvvv" + "vv",
            outs="aa",
            scratch=[
                pltpu.VMEM((late * width, LANES), bf16), pltpu.VMEM((groups, LANES), f32), vector,
                pltpu.VMEM((width // LANES, LANES), f32), *finish_scratch, pltpu.SemaphoreType.DMA((2,)),
            ],
        )(*begun, *common, second3, smoothed_fine)
        correction = correction.reshape(-1)
    else:
        correction, everywhere = coarse_by_parts(
            sent[0, :aggs], coarse_order, coarse_values, coarse_rows, coarse_inverse
        )
        index = device_index()
        low = jnp.where(index == 0, 0.0, jnp.where(index % 2 == 0, far[2], near[2]))
        high = jnp.where(index == devices - 1, 0.0, jnp.where(index % 2 == 0, near[2], far[2]))
        order = jnp.concatenate([low, own[2], high], axis=0).astype(i32)
        corr = jnp.repeat(everywhere[order[:, ::CELLS]], CELLS, axis=1)
        result = call(
            functools.partial(finish_kernel, devices), shape_of(pairs, LANES), "vvvvvv", scratch=finish_scratch
        )(corr, *common, smoothed_fine)
    return result.reshape(-1), correction


def solution(mesh):
    devices = mesh.shape["fine"] * mesh.shape["coarse"]
    in_specs = (
        P(BOTH),
        P(None, None, BOTH),
        P(None, BOTH),
        P(None, BOTH),
        P(BOTH),
        P(BOTH),
        P(BOTH),
        P(BOTH),
        P(None, None, "coarse"),
        P(None, "coarse"),
        P(None, "coarse"),
    )
    return jax.shard_map(
        functools.partial(shards, devices),
        mesh=mesh,
        in_specs=in_specs,
        out_specs=(P(BOTH), P("coarse")),
        check_vma=False,
    )
```

```python
import functools

import jax
import jax.numpy as jnp
from jax import lax
from jax.experimental import pallas as pl
from jax.experimental.pallas import tpu as pltpu
from jax.sharding import PartitionSpec as P

CELLS = 64
LANES = 128
HALO_ROWS = 8
SWEEPS = 4
EARLY = 2
BOTH = ("fine", "coarse")
f32, bf16, i32 = jnp.float32, jnp.bfloat16, jnp.int32
VMEM_LIMIT = 24 * 1024 * 1024


def iota(shape, axis):
    return lax.broadcasted_iota(i32, shape, axis)


def split(x):
    high = x.astype(bf16)
    return high, (x - high.astype(f32)).astype(bf16)


def dot(a, b):
    return lax.dot_general(a, b, (((1,), (0,)), ((), ())), preferred_element_type=f32)


def dot_t(a, b):
    return lax.dot_general(a, b, (((1,), (1,)), ((), ())), preferred_element_type=f32)


def cell_sums(high_ref, low_ref):
    width = high_ref.shape[1]
    pairs = width // LANES
    row, lane = iota((2 * pairs, width), 0), iota((2 * pairs, width), 1)
    member = (lane // CELLS == 2 * (row % pairs) + row // pairs).astype(bf16)
    sums = dot_t(member, high_ref[...]) + dot_t(member, low_ref[...])
    return jnp.concatenate([sums[:pairs], sums[pairs:]], axis=1)


def apply_smoother(vector, smoother_ref, high_ref, low_ref):
    for p in range(vector.shape[0]):
        cols = pl.ds(p * LANES, LANES)
        product = smoother_ref[:, cols].astype(f32) * vector[p : p + 1, :]
        high_ref[:, cols], low_ref[:, cols] = split(product)
    return cell_sums(high_ref, low_ref)


def selection(columns, half_rows, pairs):
    nbrs, aggs = columns.shape
    at, who = iota((pairs, aggs), 1), iota((pairs, aggs), 0)
    entry = iota((pairs, 4 * half_rows), 1) % (2 * half_rows)
    parts = []
    for half in range(2):
        for k in range(nbrs):
            chosen = jnp.where(at == 2 * who + half, columns[k : k + 1].astype(f32), 0.0)
            block = jnp.sum(chosen, axis=1, keepdims=True).astype(i32)
            place = block // 2 + jnp.where(block % 2 == half, 0, half_rows)
            parts.append((entry == place).astype(bf16))
    return jnp.concatenate(parts, axis=0)


def pick(window, selected):
    high, low = split(jnp.concatenate([window, pltpu.roll(window, CELLS, 1)], axis=0))
    picked = dot(selected, jnp.concatenate([high, low], axis=0))
    count = selected.shape[0] // 2
    lane = iota((count, LANES), 1)
    return jnp.where(lane < CELLS, picked[:count], picked[count:])


def apply_smoothed_fine(window, products_ref, selected, picked_ref, high_ref, low_ref):
    nbrs, _, width = products_ref.shape
    pairs = width // LANES
    picked_ref[...] = pick(window, selected)
    for p in range(pairs):
        cols = pl.ds(p * LANES, LANES)
        total = None
        for k in range(nbrs):
            term = products_ref[k, :, cols] * picked_ref[pl.ds(k * pairs + p, 1), :]
            total = term if total is None else total + term
        high_ref[:, cols], low_ref[:, cols] = split(total)
    return cell_sums(high_ref, low_ref)


def as_columns(row, pairs):
    shape = (pairs, row.shape[1])
    at, who = iota(shape, 1), iota(shape, 0)
    return [
        jnp.sum(jnp.where(at == 2 * who + half, row, 0.0), axis=1, keepdims=True)
        for half in range(2)
    ]


def by_half(columns, shape):
    return jnp.where(iota(shape, 1) < CELLS, columns[0], columns[1])


def fetch(sem_ref, *pairs):
    copies = [pltpu.make_async_copy(src, dst, sem_ref.at[i]) for i, (src, dst) in enumerate(pairs)]
    for copy in copies:
        copy.start()
    return copies


def start(rhs_ref, weights_ref, order_ref, smoother_ref, near_ref, onward_ref, own_ref, high_ref, low_ref):
    pairs = rhs_ref.shape[0]
    smoothed = apply_smoother(rhs_ref[...], smoother_ref, high_ref, low_ref)
    order = by_half(as_columns(order_ref[...].astype(f32), pairs), (pairs, LANES))
    even = lax.axis_index("coarse") % 2 == 0
    for i, part in enumerate((smoothed, weights_ref[...], order)):
        own_ref[i] = part
        bottom, top = part[:HALO_ROWS], part[pairs - HALO_ROWS :]
        near_ref[i] = jnp.where(even, top, bottom)
        onward_ref[i] = jnp.where(even, bottom, top)


def start_kernel(
    rhs_any, weights_any, order_any, smoother_any, near_ref, onward_ref, own_ref, smoother_ref,
    rhs_ref, weights_ref, order_ref, high_ref, low_ref, sem_ref,
):
    copies = fetch(
        sem_ref, (smoother_any, smoother_ref), (rhs_any, rhs_ref), (weights_any, weights_ref), (order_any, order_ref)
    )
    for copy in copies:
        copy.wait()
    start(rhs_ref, weights_ref, order_ref, smoother_ref, near_ref, onward_ref, own_ref, high_ref, low_ref)


def start_pack_kernel(
    rhs_any, weights_any, order_any, smoother_any, rows_any, values_any, inverse_any,
    near_ref, onward_ref, own_ref, smoother_ref, packed_ref, first_ref, second_ref,
    rhs_ref, weights_ref, order_ref, rows_ref, values_ref, inverse_ref, high_ref, low_ref, sem_ref,
):
    copies = fetch(
        sem_ref, (smoother_any, smoother_ref), (rhs_any, rhs_ref), (weights_any, weights_ref), (order_any, order_ref),
        (values_any, values_ref), (inverse_any, inverse_ref), (rows_any, rows_ref),
    )
    for copy in copies[:4]:
        copy.wait()
    start(rhs_ref, weights_ref, order_ref, smoother_ref, near_ref, onward_ref, own_ref, high_ref, low_ref)
    for copy in copies[4:]:
        copy.wait()
    own_blocks, nbrs = rows_ref.shape
    deep, width = values_ref.shape
    at, slot = iota((8, nbrs), 1), iota((8, nbrs), 0)
    block = iota((8, width), 1) // CELLS
    rows = jnp.zeros((8, width), f32)
    for j in range(own_blocks):
        targets = jnp.where(at == slot, rows_ref[j : j + 1, :].astype(f32), 0.0)
        rows = jnp.where(block == j, jnp.sum(targets, axis=1, keepdims=True), rows)
    inverse = inverse_ref[...].astype(f32)
    for ref in (packed_ref, first_ref):
        ref[pl.ds(0, 8), :] = rows
        ref[pl.ds(8, CELLS), :] = inverse
    base = 8 + CELLS
    early = first_ref.shape[0] - base
    for r in range(0, deep, CELLS):
        values = values_ref[pl.ds(r, CELLS), :].astype(f32)
        packed_ref[pl.ds(base + r, CELLS), :] = values
        if r < early:
            first_ref[pl.ds(base + r, CELLS), :] = values
        else:
            second_ref[pl.ds(r - early, CELLS), :] = values


def window_of(near_ref, far_ref, own_ref, device, devices):
    even = device % 2 == 0
    near, far = near_ref[...], far_ref[...]
    low = jnp.where(device == 0, 0.0, jnp.where(even, far, near))
    high = jnp.where(device == devices - 1, 0.0, jnp.where(even, near, far))
    return [jnp.concatenate([low[i], own_ref[i], high[i]], axis=0) for i in range(3)]


def device_index():
    return lax.axis_index("fine") * lax.axis_size("coarse") + lax.axis_index("coarse")


def prepare_kernel(
    counts_ref, own_ref, rhs_any, reaction_any, columns_any, fine_any, smoother_ref, selected_ref, weighed_ref, local_ref,
    products_ref, rhs_ref, reaction_ref, columns_ref, fine_ref, wide_ref, sem_ref,
):
    copies = fetch(
        sem_ref, (columns_any, columns_ref), (rhs_any, rhs_ref), (reaction_any, reaction_ref),
        *((fine_any.at[k], fine_ref.at[k]) for k in range(fine_ref.shape[0])),
    )
    for copy in copies[:3]:
        copy.wait()
    pairs = rhs_ref.shape[0]
    nbrs, _, width = fine_ref.shape
    weights = own_ref[1]
    agg = 2 * iota((pairs, LANES), 0) + iota((pairs, LANES), 1) // CELLS
    reaction = jnp.where(agg < counts_ref[0], reaction_ref[...], 0.0)
    local_ref[0] = weights * rhs_ref[...]
    local_ref[1] = weights * reaction
    selected_ref[...] = selection(columns_ref[...], pairs + 2 * HALO_ROWS, pairs)
    by_agg = jnp.concatenate([weights[:, :CELLS], weights[:, CELLS:]], axis=0)
    row, lane = iota((2 * pairs, width), 0), iota((2 * pairs, width), 1)
    member = (lane // CELLS == 2 * (row % pairs) + row // pairs).astype(bf16)
    wide = None
    for part in split(by_agg):
        term = lax.dot_general(part, member, (((0,), (0,)), ((), ())), preferred_element_type=f32)
        wide = term if wide is None else wide + term
    wide_ref[...] = wide
    for k in range(nbrs):
        copies[3 + k].wait()
        for p in range(pairs):
            cols = pl.ds(p * LANES, LANES)
            term = fine_ref[k, :, cols].astype(f32) * wide_ref[:, cols]
            total = term[:8]
            for r in range(8, CELLS, 8):
                total = total + term[r : r + 8]
            weighed_ref[k * pairs + p] = total
    lane = iota((CELLS, LANES), 1)
    for p in range(pairs):
        cols = pl.ds(p * LANES, LANES)
        left = smoother_ref[:, cols]
        rights = []
        for k in range(nbrs):
            block = fine_ref[k, :, cols]
            zero = jnp.zeros_like(block)
            apart = [jnp.where(lane < CELLS, block, zero), jnp.where(lane < CELLS, zero, block)]
            rights.append(jnp.concatenate(apart, axis=0))
        both = dot(left, jnp.concatenate(rights, axis=1))
        for k in range(nbrs):
            product = both[:, k * LANES : (k + 1) * LANES]
            products_ref[k, :, cols] = product if k else product + left.astype(f32) * reaction[p : p + 1]


def residual_kernel(
    devices, near_ref, far_ref, own_ref, selected_ref, weighed_ref, local_ref, out_ref, picked_ref,
):
    smoothed, _, _ = window_of(near_ref, far_ref, own_ref, device_index(), devices)
    picked_ref[...] = pick(smoothed, selected_ref[...])
    pairs = own_ref.shape[1]
    nbrs = picked_ref.shape[0] // pairs
    images = []
    for p in range(pairs):
        total = None
        for k in range(nbrs):
            term = weighed_ref[k * pairs + p] * picked_ref[pl.ds(k * pairs + p, 1), :]
            total = term if total is None else total + term
        images.append(jnp.sum(total, axis=0, keepdims=True))
    weighted = local_ref[0] - local_ref[1] * own_ref[0] - jnp.concatenate(images, axis=0)
    shape = (pairs, LANES)
    lane, who = iota(shape, 1), iota(shape, 0)
    row = jnp.zeros((1, LANES), f32)
    for half in range(2):
        inside = lane // CELLS == half
        restricted = jnp.sum(jnp.where(inside, weighted, 0.0), axis=1, keepdims=True)
        order = jnp.max(jnp.where(inside, own_ref[2], 0.0), axis=1, keepdims=True)
        spread = jnp.where(lane == 2 * who + half, restricted, 0.0)
        spread = spread + jnp.where(lane == 2 * (pairs + who) + half, order, 0.0)
        row = row + jnp.sum(spread, axis=0, keepdims=True)
    out_ref[...] = jnp.broadcast_to(row, out_ref.shape)


def finish(corr, near_ref, far_ref, own_ref, devices, selected_ref, products_ref, result_ref,
           picked_ref, high_ref, low_ref):
    smoothed, weights, _ = window_of(near_ref, far_ref, own_ref, device_index(), devices)
    corrected = smoothed + weights * corr
    mine = corrected[HALO_ROWS : HALO_ROWS + own_ref.shape[1]]
    image = apply_smoothed_fine(corrected, products_ref, selected_ref[...], picked_ref, high_ref, low_ref)
    result_ref[...] = mine + (own_ref[0] - image)


def place(group, own_blocks):
    return jnp.bitwise_xor(group // own_blocks, lax.axis_index("coarse")) * own_blocks + group % own_blocks


def pairs_of(x):
    half = x.shape[0] // 2
    return jnp.concatenate([x[:half], x[half:]], axis=1)


def masked_rows(x, mask_lists, pair_at, held_ref):
    pairs = x.shape[0]
    high, low = split(x)
    held_ref[pl.ds(0, pairs), :] = high.astype(f32)
    held_ref[pl.ds(pairs, pairs), :] = low.astype(f32)
    parts = []
    for part in range(2):
        rows = [
            jnp.broadcast_to(held_ref[pl.ds(part * pairs + p, 1), :], (2 * pairs, LANES)).astype(bf16)
            for p in range(pairs)
        ]
        parts.append(rows)
    return jnp.concatenate(
        [
            jnp.concatenate([mask * rows[pair_at(c)] for c, mask in enumerate(masks)], axis=1)
            for masks in mask_lists
            for rows in parts
        ],
        axis=0,
    )


def inverse_product(x, inverse_ref, held_ref):
    pairs = x.shape[0]
    groups = 2 * pairs
    row, lane = iota((groups, LANES), 0), iota((groups, LANES), 1)
    masks = [((row % pairs == p) & (row // pairs == lane // CELLS)).astype(bf16) for p in range(pairs)]
    sums = dot(masked_rows(x, [masks], lambda c: c, held_ref), inverse_ref[...])
    return pairs_of(sums[:groups] + sums[groups:])


def slot_pair(rows_ref, first, count):
    turned = rows_ref[pl.ds(first, CELLS * count), :].astype(bf16).T
    return turned if count == 2 else jnp.concatenate([turned, jnp.zeros_like(turned)], axis=1)


def target_rows(x, target_ref, start, stop, own_blocks, held_ref):
    groups, half = target_ref.shape[0], target_ref.shape[1] // 2
    per_part = half // LANES // (groups // own_blocks)
    per_block = own_blocks // 2
    masks = [[target_ref[:, pl.ds(t * half + c, LANES)] for c in range(start, stop, LANES)] for t in range(2)]

    def pair_at(chunk):
        chunk = chunk + start // LANES
        return chunk // per_part * per_block + chunk % per_block

    return masked_rows(x, masks, pair_at, held_ref)


def first_sweep_kernel(
    gathered_ref, mine_ref, beside_ref, first2_ref, second2_ref, first3_ref,
    side_ref, begun_ref, inverse_ref, target_ref, blocks_ref, sums_ref, held_ref,
):
    part_refs = (mine_ref, beside_ref, first2_ref, first3_ref)
    width = mine_ref.shape[1]
    own_blocks = width // CELLS
    pairs = side_ref.shape[0]
    groups = 2 * pairs
    base = 8 + CELLS
    nbrs = (mine_ref.shape[0] - base) // CELLS
    early = (first2_ref.shape[0] - base) // CELLS
    for i, ref in enumerate(part_refs):
        inverse_ref[pl.ds(i * width, width), :] = ref[pl.ds(8, CELLS), :].astype(bf16).T

    gathered = gathered_ref[...]
    devs = gathered.shape[0]
    lane = iota((8, LANES), 1)
    row = iota((groups, LANES), 0)
    number = 2 * (row % pairs) + row // pairs
    lefts, rights = [], []
    for start in range(0, devs, 32):
        value = jnp.zeros((8, LANES), f32)
        order = jnp.zeros((8, LANES), f32)
        for i in range(4):
            piece = gathered[start + 8 * i : start + 8 * i + 8]
            here = lane // 32 == i
            value = jnp.where(here, pltpu.roll(piece, 32 * i, 1) if i else piece, value)
            order = jnp.where(here, pltpu.roll(piece, (32 * i + 96) % LANES, 1) if i != 1 else piece, order)
        order = order.astype(i32)
        group, unit = place(order // CELLS, own_blocks), order % CELLS
        for s in range(8):
            left = jnp.where(number == group[s : s + 1], value[s : s + 1], 0.0)
            lefts.append(jnp.concatenate(split(left), axis=0))
            rights.append((iota((CELLS, LANES), 0) == unit[s : s + 1]).astype(bf16))
    side = dot_t(jnp.concatenate(lefts, axis=1), jnp.concatenate(rights, axis=1))
    side = pairs_of(side[:groups] + side[groups:])
    side_ref[...] = side
    begun = inverse_product(side, inverse_ref, held_ref)
    begun_ref[...] = begun

    row = iota((groups, width), 0)
    number = 2 * (row % pairs) + row // pairs
    twos = (nbrs + 1) // 2
    half = twos * width * len(part_refs)
    for i, ref in enumerate(part_refs):
        targets = place(ref[pl.ds(0, 8), :].astype(i32), own_blocks)
        for k in range(2 * twos):
            cols = pl.ds(k % 2 * half + (i * twos + k // 2) * width, width)
            chosen = number == targets[k : k + 1] if k < nbrs else jnp.zeros(row.shape, jnp.bool_)
            target_ref[:, cols] = chosen.astype(bf16)
        for q in range(twos):
            rows = pl.ds((i * twos + q) * width, width)
            count = min(2, nbrs - 2 * q)
            if i < 2 or 2 * q < early:
                blocks_ref[rows, :] = slot_pair(ref, base + 2 * q * CELLS, count)
            elif i == 2:
                blocks_ref[rows, :] = slot_pair(second2_ref, (2 * q - early) * CELLS, count)

    sums_ref[...] = dot(target_rows(begun, target_ref, 0, blocks_ref.shape[0], own_blocks, held_ref), blocks_ref[...])


def solve_kernel(
    devices, side_ref, begun_ref, inverse_ref, target_ref, blocks_ref, sums_ref, near_ref, far_ref, own_ref, selected_ref,
    second3_ref, products_ref,
    out_any, correction_any,
    last_ref, held_ref, result_ref, correction_ref,
    picked_ref, high_ref, low_ref, out_sem_ref,
):
    width = second3_ref.shape[1]
    own_blocks = width // CELLS
    groups, half = target_ref.shape[0], target_ref.shape[1] // 2
    pairs = groups // 2
    late = second3_ref.shape[0] // CELLS
    for q in range(0, late, 2):
        last_ref[pl.ds(q // 2 * width, width), :] = slot_pair(second3_ref, q * CELLS, min(2, late - q))
    side = side_ref[...]
    correction = begun_ref[...]
    split_at = blocks_ref.shape[0]
    for sweep in range(SWEEPS - 1):
        if sweep == 0:
            sums = sums_ref[...]
            spread = target_rows(correction, target_ref, split_at, half, own_blocks, held_ref)
        else:
            spread = target_rows(correction, target_ref, 0, half, own_blocks, held_ref)
            sums = dot(spread[:, :split_at], blocks_ref[...])
            spread = spread[:, split_at:]
        sums = sums + dot(spread, last_ref[...])
        image = sums[:groups] + sums[groups : 2 * groups]
        other = sums[2 * groups : 3 * groups] + sums[3 * groups :]
        image = pairs_of(image[:, :CELLS] + other[:, CELLS:])
        correction = correction + inverse_product(side - image, inverse_ref, held_ref)
    correction_ref[...] = correction[: own_blocks // 2]
    correction_copy = pltpu.make_async_copy(correction_ref, correction_any, out_sem_ref.at[0])
    correction_copy.start()

    order = window_of(near_ref, far_ref, own_ref, device_index(), devices)[2].astype(i32)
    rows = order.shape[0]
    unit = jnp.concatenate([order[:, :CELLS], order[:, CELLS:]], axis=0)
    chosen = (iota(unit.shape, 1) == unit % CELLS).astype(bf16)
    by_block = jnp.concatenate([correction[:, :CELLS], correction[:, CELLS:]], axis=0)
    values = dot_t(chosen, jnp.concatenate(split(by_block), axis=0))
    group = place(unit[:, : 2 * groups] // CELLS, own_blocks)
    group = group // 2 + group % 2 * pairs
    values = jnp.sum(jnp.where(iota(values.shape, 1) % groups == group, values, 0.0), axis=1, keepdims=True)
    corr = by_half([values[:rows], values[rows:]], (rows, LANES))
    finish(corr, near_ref, far_ref, own_ref, devices, selected_ref, products_ref, result_ref,
           picked_ref, high_ref, low_ref)
    result_copy = pltpu.make_async_copy(result_ref, out_any, out_sem_ref.at[1])
    result_copy.start()
    correction_copy.wait()
    result_copy.wait()


def finish_kernel(
    devices, corr_ref, near_ref, far_ref, own_ref, selected_ref, products_ref, result_ref, picked_ref, high_ref, low_ref,
):
    finish(corr_ref[...], near_ref, far_ref, own_ref, devices, selected_ref, products_ref, result_ref,
           picked_ref, high_ref, low_ref)


def call(kernel, out_shape, ins, outs=None, scratch=(), cost=None):
    spaces = dict(s=pltpu.SMEM, v=pltpu.VMEM, a=pl.ANY)
    many = isinstance(out_shape, tuple)
    specs = tuple(pl.BlockSpec(memory_space=spaces[c]) for c in outs or "v" * (len(out_shape) if many else 1))
    run = pl.pallas_call(
        kernel,
        out_shape=out_shape,
        in_specs=[pl.BlockSpec(memory_space=spaces[c]) for c in ins],
        out_specs=specs if many else specs[0],
        scratch_shapes=list(scratch),
        compiler_params=pltpu.CompilerParams(vmem_limit_bytes=VMEM_LIMIT),
        cost_estimate=cost and pl.CostEstimate(flops=cost, bytes_accessed=0, transcendentals=0),
    )

    def placed(*operands):
        return run(*(pltpu.with_memory_space_constraint(x, pltpu.HBM) if c == "a" else x for x, c in zip(operands, ins)))

    return placed


def shape_of(*dims):
    return jax.ShapeDtypeStruct(dims, f32)


def coarse_by_parts(restricted, coarse_order, coarse_values, coarse_rows, coarse_inverse):
    own = coarse_inverse.shape[1]
    own_blocks = own // CELLS
    total = own * lax.axis_size("coarse")
    start = lax.axis_index("coarse") * own
    side = jnp.zeros((total,), f32).at[coarse_order].add(restricted)
    side = lax.dynamic_slice_in_dim(lax.psum(side, BOTH), start, own)
    values = coarse_values.astype(f32).reshape(-1, CELLS, own_blocks, CELLS)
    inverse = coarse_inverse.astype(f32).reshape(CELLS, own_blocks, CELLS)

    def scale(x):
        x = x.reshape(own_blocks, CELLS)
        return jnp.einsum("oji,ji->jo", inverse, x, precision=lax.Precision.HIGHEST).reshape(-1)

    correction = scale(side)
    for _ in range(SWEEPS - 1):
        x = correction.reshape(own_blocks, CELLS)
        sums = jnp.einsum("vfmd,md->vmf", values, x, precision=lax.Precision.HIGHEST)
        image = jax.ops.segment_sum(
            sums.reshape(-1, CELLS), coarse_rows.reshape(-1), num_segments=total // CELLS
        ).reshape(-1)
        image = lax.dynamic_slice_in_dim(lax.psum(image, "coarse"), start, own)
        correction = correction + scale(side - image)
    return correction, lax.all_gather(correction, "coarse", axis=0, tiled=True)


def shards(
    devices, rhs, fine_values, fine_columns, smoother, reaction, pit_counts, weights, coarse_order,
    coarse_values, coarse_rows, coarse_inverse,
):
    cells = rhs.shape[0]
    pairs = cells // LANES
    aggs = 2 * pairs
    nbrs = fine_columns.shape[0]
    parts = lax.axis_size("coarse")
    rhs, reaction, weights = (x.reshape(pairs, LANES) for x in (rhs, reaction, weights))
    rows = pairs + 2 * HALO_ROWS
    vector = pltpu.VMEM((pairs, LANES), f32)
    products = [pltpu.VMEM((CELLS, cells), bf16)] * 2
    picked = pltpu.VMEM((nbrs * pairs, LANES), f32)
    copies = pltpu.SemaphoreType.DMA((4,))
    edge = shape_of(3, HALO_ROWS, LANES)

    copied = parts == 4 and devices % 32 == 0 and devices <= 64
    start_shapes = (
        edge, edge, shape_of(3, pairs, LANES), jax.ShapeDtypeStruct(smoother.shape, bf16)
    )
    start_ins = (rhs, weights, coarse_order.reshape(1, aggs), smoother)
    start_scratch = [vector, vector, pltpu.VMEM((1, aggs), i32)]
    if copied:
        deep = coarse_values.shape[0] * CELLS
        width = coarse_inverse.shape[1]
        early = EARLY * CELLS
        near, onward, own, smoother_here, packed, first, second = call(
            start_pack_kernel,
            (*start_shapes, shape_of(8 + CELLS + deep, width), shape_of(8 + CELLS + early, width),
             shape_of(deep - early, width)),
            "aaaaaaa",
            scratch=[
                *start_scratch, pltpu.VMEM(coarse_rows.shape[::-1], i32), pltpu.VMEM((deep, width), bf16),
                pltpu.VMEM(coarse_inverse.shape, bf16), *products, pltpu.SemaphoreType.DMA((7,)),
            ],
        )(*start_ins, coarse_rows.T, coarse_values.reshape(deep, width), coarse_inverse)
        swap = [(c, c ^ 1) for c in range(parts)]
        across = [(c, c ^ 2) for c in range(parts)]
        first2 = lax.ppermute(first, "coarse", across)
    else:
        near, onward, own, smoother_here = call(start_kernel, start_shapes, "aaaa", scratch=[*start_scratch, *products, copies])(
            *start_ins
        )

    partner = [(d, d ^ 1) for d in range(devices)]
    chain = []
    for d in range(devices):
        target = d + 2 if d % 2 == 0 else d - 2
        chain.append((d, target if 0 <= target < devices else d ^ 1))
    onward = lax.ppermute(onward, BOTH, partner)
    near = lax.ppermute(near, BOTH, partner)

    far = lax.ppermute(onward, BOTH, chain)
    selected, weighed, local, smoothed_fine = call(
        prepare_kernel,
        (jax.ShapeDtypeStruct((aggs * nbrs, 4 * rows), bf16), shape_of(nbrs * pairs, 8, LANES), shape_of(2, pairs, LANES),
         shape_of(*fine_values.shape)),
        "svaaaav",
        scratch=[vector, vector, pltpu.VMEM(fine_columns.shape, i32), pltpu.VMEM(fine_values.shape, bf16), pltpu.VMEM((CELLS, cells), f32), pltpu.SemaphoreType.DMA((3 + nbrs,))],
    )(pit_counts, own, rhs, reaction, fine_columns, fine_values, smoother_here)

    if copied:
        first2, second, selected = lax.optimization_barrier((first2, second, selected))
        beside = lax.ppermute(packed, "coarse", swap)
        second2 = lax.ppermute(second, "coarse", across)
        first3 = lax.ppermute(first2, "coarse", swap)

    sent = call(
        functools.partial(residual_kernel, devices), shape_of(devices, LANES), "vvvvvv", scratch=[picked], cost=10_000_000_000
    )(near, far, own, selected, weighed, local)

    finish_scratch = [picked, *products]
    common = (near, far, own, selected)
    if copied:
        gathered = lax.all_to_all(sent, BOTH, 0, 0, tiled=True)
        first3, second2, gathered = lax.optimization_barrier((first3, second2, gathered))
        second3 = lax.ppermute(second2, "coarse", swap)
        unknowns = parts * width
        groups = unknowns // CELLS
        twos, late = (nbrs + 1) // 2, (nbrs - EARLY + 1) // 2
        begun = call(
            first_sweep_kernel,
            (shape_of(unknowns // LANES, LANES), shape_of(unknowns // LANES, LANES),
             jax.ShapeDtypeStruct((unknowns, CELLS), bf16), jax.ShapeDtypeStruct((groups, 2 * twos * unknowns), bf16),
             jax.ShapeDtypeStruct((twos * unknowns - late * width, LANES), bf16), shape_of(4 * groups, LANES)),
            "vvvvvv",
            scratch=[pltpu.VMEM((groups, LANES), f32)],
        )(gathered, packed, beside, first2, second2, first3)
        result, correction = call(
            functools.partial(solve_kernel, devices),
            (shape_of(pairs, LANES), shape_of(width // LANES, LANES)),
            "vvvvvv" + "vvvv" + "vv",
            outs="aa",
            scratch=[
                pltpu.VMEM((late * width, LANES), bf16), pltpu.VMEM((groups, LANES), f32), vector,
                pltpu.VMEM((width // LANES, LANES), f32), *finish_scratch, pltpu.SemaphoreType.DMA((2,)),
            ],
        )(*begun, *common, second3, smoothed_fine)
        correction = correction.reshape(-1)
    else:
        correction, everywhere = coarse_by_parts(
            sent[0, :aggs], coarse_order, coarse_values, coarse_rows, coarse_inverse
        )
        index = device_index()
        low = jnp.where(index == 0, 0.0, jnp.where(index % 2 == 0, far[2], near[2]))
        high = jnp.where(index == devices - 1, 0.0, jnp.where(index % 2 == 0, near[2], far[2]))
        order = jnp.concatenate([low, own[2], high], axis=0).astype(i32)
        corr = jnp.repeat(everywhere[order[:, ::CELLS]], CELLS, axis=1)
        result = call(
            functools.partial(finish_kernel, devices), shape_of(pairs, LANES), "vvvvvv", scratch=finish_scratch
        )(corr, *common, smoothed_fine)
    return result.reshape(-1), correction


def solution(mesh):
    devices = mesh.shape["fine"] * mesh.shape["coarse"]
    in_specs = (
        P(BOTH),
        P(None, None, BOTH),
        P(None, BOTH),
        P(None, BOTH),
        P(BOTH),
        P(BOTH),
        P(BOTH),
        P(BOTH),
        P(None, None, "coarse"),
        P(None, "coarse"),
        P(None, "coarse"),
    )
    return jax.shard_map(
        functools.partial(shards, devices),
        mesh=mesh,
        in_specs=in_specs,
        out_specs=(P(BOTH), P("coarse")),
        check_vma=False,
    )
```

```python
import functools

import jax
import jax.numpy as jnp
from jax import lax
from jax.experimental import pallas as pl
from jax.experimental.pallas import tpu as pltpu
from jax.sharding import PartitionSpec as P

CELLS = 64
LANES = 128
HALO_ROWS = 8
SWEEPS = 4
EARLY = 0
BOTH = ("fine", "coarse")
f32, bf16, i32 = jnp.float32, jnp.bfloat16, jnp.int32
VMEM_LIMIT = 24 * 1024 * 1024


def iota(shape, axis):
    return lax.broadcasted_iota(i32, shape, axis)


def split(x):
    high = x.astype(bf16)
    return high, (x - high.astype(f32)).astype(bf16)


def dot(a, b):
    return lax.dot_general(a, b, (((1,), (0,)), ((), ())), preferred_element_type=f32)


def dot_t(a, b):
    return lax.dot_general(a, b, (((1,), (1,)), ((), ())), preferred_element_type=f32)


def cell_sums(high_ref, low_ref):
    width = high_ref.shape[1]
    pairs = width // LANES
    row, lane = iota((2 * pairs, width), 0), iota((2 * pairs, width), 1)
    member = (lane // CELLS == 2 * (row % pairs) + row // pairs).astype(bf16)
    sums = dot_t(member, high_ref[...]) + dot_t(member, low_ref[...])
    return jnp.concatenate([sums[:pairs], sums[pairs:]], axis=1)


def apply_smoother(vector, smoother_ref, high_ref, low_ref):
    for p in range(vector.shape[0]):
        cols = pl.ds(p * LANES, LANES)
        product = smoother_ref[:, cols].astype(f32) * vector[p : p + 1, :]
        high_ref[:, cols], low_ref[:, cols] = split(product)
    return cell_sums(high_ref, low_ref)


def selection(columns, half_rows, pairs):
    nbrs, aggs = columns.shape
    at, who = iota((pairs, aggs), 1), iota((pairs, aggs), 0)
    chosen = [
        jnp.where(at == 2 * who + half, columns[k : k + 1].astype(f32), 0.0)
        for half in range(2)
        for k in range(nbrs)
    ]
    block = dot(jnp.concatenate(chosen, axis=0).astype(bf16), jnp.ones((aggs, 4 * half_rows), bf16)).astype(i32)
    half = iota(block.shape, 0) // (nbrs * pairs)
    place = block // 2 + jnp.where(block % 2 == half, 0, half_rows)
    return (iota(block.shape, 1) % (2 * half_rows) == place).astype(bf16)


def pick(window, selected):
    high, low = split(jnp.concatenate([window, pltpu.roll(window, CELLS, 1)], axis=0))
    picked = dot(selected, jnp.concatenate([high, low], axis=0))
    count = selected.shape[0] // 2
    lane = iota((count, LANES), 1)
    return jnp.where(lane < CELLS, picked[:count], picked[count:])


def apply_smoothed_fine(window, products_ref, selected, picked_ref, high_ref, low_ref):
    nbrs, _, width = products_ref.shape
    pairs = width // LANES
    picked_ref[...] = pick(window, selected)
    for p in range(pairs):
        cols = pl.ds(p * LANES, LANES)
        total = None
        for k in range(nbrs):
            term = products_ref[k, :, cols] * picked_ref[pl.ds(k * pairs + p, 1), :]
            total = term if total is None else total + term
        high_ref[:, cols], low_ref[:, cols] = split(total)
    return cell_sums(high_ref, low_ref)


def as_columns(row, pairs):
    shape = (pairs, row.shape[1])
    at, who = iota(shape, 1), iota(shape, 0)
    return [
        jnp.sum(jnp.where(at == 2 * who + half, row, 0.0), axis=1, keepdims=True)
        for half in range(2)
    ]


def by_half(columns, shape):
    return jnp.where(iota(shape, 1) < CELLS, columns[0], columns[1])


def fetch(sem_ref, *pairs):
    copies = [pltpu.make_async_copy(src, dst, sem_ref.at[i]) for i, (src, dst) in enumerate(pairs)]
    for copy in copies:
        copy.start()
    return copies


def start(rhs_ref, weights_ref, order_ref, smoother_ref, near_ref, onward_ref, own_ref, high_ref, low_ref):
    pairs = rhs_ref.shape[0]
    smoothed = apply_smoother(rhs_ref[...], smoother_ref, high_ref, low_ref)
    order = by_half(as_columns(order_ref[...].astype(f32), pairs), (pairs, LANES))
    even = lax.axis_index("coarse") % 2 == 0
    for i, part in enumerate((smoothed, weights_ref[...], order)):
        own_ref[i] = part
        bottom, top = part[:HALO_ROWS], part[pairs - HALO_ROWS :]
        near_ref[i] = jnp.where(even, top, bottom)
        onward_ref[i] = jnp.where(even, bottom, top)


def start_kernel(
    rhs_any, weights_any, order_any, smoother_any, near_ref, onward_ref, own_ref, smoother_ref,
    rhs_ref, weights_ref, order_ref, high_ref, low_ref, sem_ref,
):
    copies = fetch(
        sem_ref, (smoother_any, smoother_ref), (rhs_any, rhs_ref), (weights_any, weights_ref), (order_any, order_ref)
    )
    for copy in copies:
        copy.wait()
    start(rhs_ref, weights_ref, order_ref, smoother_ref, near_ref, onward_ref, own_ref, high_ref, low_ref)


def start_pack_kernel(
    rhs_any, weights_any, order_any, smoother_any, rows_any, values_any, inverse_any,
    near_ref, onward_ref, own_ref, smoother_ref, packed_ref, first_ref, second_ref,
    rhs_ref, weights_ref, order_ref, rows_ref, values_ref, inverse_ref, high_ref, low_ref, sem_ref,
):
    copies = fetch(
        sem_ref, (smoother_any, smoother_ref), (rhs_any, rhs_ref), (weights_any, weights_ref), (order_any, order_ref),
        (values_any, values_ref), (inverse_any, inverse_ref), (rows_any, rows_ref),
    )
    for copy in copies[:4]:
        copy.wait()
    start(rhs_ref, weights_ref, order_ref, smoother_ref, near_ref, onward_ref, own_ref, high_ref, low_ref)
    for copy in copies[4:]:
        copy.wait()
    own_blocks, nbrs = rows_ref.shape
    deep, width = values_ref.shape
    at, slot = iota((8, nbrs), 1), iota((8, nbrs), 0)
    block = iota((8, width), 1) // CELLS
    rows = jnp.zeros((8, width), f32)
    for j in range(own_blocks):
        targets = jnp.where(at == slot, rows_ref[j : j + 1, :].astype(f32), 0.0)
        rows = jnp.where(block == j, jnp.sum(targets, axis=1, keepdims=True), rows)
    inverse = inverse_ref[...].astype(f32)
    for ref in (packed_ref, first_ref):
        ref[pl.ds(0, 8), :] = rows
        ref[pl.ds(8, CELLS), :] = inverse
    base = 8 + CELLS
    early = first_ref.shape[0] - base
    for r in range(0, deep, CELLS):
        values = values_ref[pl.ds(r, CELLS), :].astype(f32)
        packed_ref[pl.ds(base + r, CELLS), :] = values
        if r < early:
            first_ref[pl.ds(base + r, CELLS), :] = values
        else:
            second_ref[pl.ds(r - early, CELLS), :] = values


def window_of(near_ref, far_ref, own_ref, device, devices):
    even = device % 2 == 0
    near, far = near_ref[...], far_ref[...]
    low = jnp.where(device == 0, 0.0, jnp.where(even, far, near))
    high = jnp.where(device == devices - 1, 0.0, jnp.where(even, near, far))
    return [jnp.concatenate([low[i], own_ref[i], high[i]], axis=0) for i in range(3)]


def device_index():
    return lax.axis_index("fine") * lax.axis_size("coarse") + lax.axis_index("coarse")


def prepare_kernel(
    counts_ref, own_ref, rhs_any, reaction_any, columns_any, fine_any, selected_ref, weighed_ref, local_ref,
    masked_ref, fine_ref, rhs_ref, reaction_ref, columns_ref, wide_ref, sem_ref,
):
    copies = fetch(
        sem_ref, (columns_any, columns_ref), (rhs_any, rhs_ref), (reaction_any, reaction_ref),
        *((fine_any.at[k], fine_ref.at[k]) for k in range(fine_ref.shape[0])),
    )
    nbrs, _, width = fine_ref.shape
    pairs = width // LANES
    weights = own_ref[1]
    by_agg = jnp.concatenate([weights[:, :CELLS], weights[:, CELLS:]], axis=0)
    row, lane = iota((2 * pairs, width), 0), iota((2 * pairs, width), 1)
    member = (lane // CELLS == 2 * (row % pairs) + row // pairs).astype(bf16)
    wide = None
    for part in split(by_agg):
        term = lax.dot_general(part, member, (((0,), (0,)), ((), ())), preferred_element_type=f32)
        wide = term if wide is None else wide + term
    wide_ref[...] = wide
    for copy in copies[:3]:
        copy.wait()
    agg = 2 * iota((pairs, LANES), 0) + iota((pairs, LANES), 1) // CELLS
    reaction = jnp.where(agg < counts_ref[0], reaction_ref[...], 0.0)
    local_ref[0] = weights * rhs_ref[...]
    local_ref[1] = weights * reaction
    masked_ref[...] = reaction
    selected_ref[...] = selection(columns_ref[...], pairs + 2 * HALO_ROWS, pairs)
    for k in range(nbrs):
        copies[3 + k].wait()
        for p in range(pairs):
            cols = pl.ds(p * LANES, LANES)
            term = fine_ref[k, :, cols].astype(f32) * wide_ref[:, cols]
            total = term[:8]
            for r in range(8, CELLS, 8):
                total = total + term[r : r + 8]
            weighed_ref[k * pairs + p] = total


def products_kernel(reaction_ref, fine_ref, smoother_ref, products_ref):
    nbrs, _, width = fine_ref.shape
    pairs = width // LANES
    lane = iota((CELLS, LANES), 1)
    for p in range(pairs):
        cols = pl.ds(p * LANES, LANES)
        left = smoother_ref[:, cols]
        rights = []
        for k in range(nbrs):
            block = fine_ref[k, :, cols]
            zero = jnp.zeros_like(block)
            apart = [jnp.where(lane < CELLS, block, zero), jnp.where(lane < CELLS, zero, block)]
            rights.append(jnp.concatenate(apart, axis=0))
        both = dot(left, jnp.concatenate(rights, axis=1))
        for k in range(nbrs):
            product = both[:, k * LANES : (k + 1) * LANES]
            products_ref[k, :, cols] = product if k else product + left.astype(f32) * reaction_ref[p : p + 1, :]


def residual_kernel(
    devices, near_ref, far_ref, own_ref, selected_ref, weighed_ref, local_ref, out_ref, picked_ref,
):
    smoothed, _, _ = window_of(near_ref, far_ref, own_ref, device_index(), devices)
    picked_ref[...] = pick(smoothed, selected_ref[...])
    pairs = own_ref.shape[1]
    nbrs = picked_ref.shape[0] // pairs
    images = []
    for p in range(pairs):
        total = None
        for k in range(nbrs):
            term = weighed_ref[k * pairs + p] * picked_ref[pl.ds(k * pairs + p, 1), :]
            total = term if total is None else total + term
        images.append(jnp.sum(total, axis=0, keepdims=True))
    weighted = local_ref[0] - local_ref[1] * own_ref[0] - jnp.concatenate(images, axis=0)
    shape = (pairs, LANES)
    lane, who = iota(shape, 1), iota(shape, 0)
    row = jnp.zeros((1, LANES), f32)
    for half in range(2):
        inside = lane // CELLS == half
        restricted = jnp.sum(jnp.where(inside, weighted, 0.0), axis=1, keepdims=True)
        order = jnp.max(jnp.where(inside, own_ref[2], 0.0), axis=1, keepdims=True)
        spread = jnp.where(lane == 2 * who + half, restricted, 0.0)
        spread = spread + jnp.where(lane == 2 * (pairs + who) + half, order, 0.0)
        row = row + jnp.sum(spread, axis=0, keepdims=True)
    out_ref[...] = jnp.broadcast_to(row, out_ref.shape)


def finish(corr, near_ref, far_ref, own_ref, devices, selected_ref, products_ref, result_ref,
           picked_ref, high_ref, low_ref):
    smoothed, weights, _ = window_of(near_ref, far_ref, own_ref, device_index(), devices)
    corrected = smoothed + weights * corr
    mine = corrected[HALO_ROWS : HALO_ROWS + own_ref.shape[1]]
    image = apply_smoothed_fine(corrected, products_ref, selected_ref[...], picked_ref, high_ref, low_ref)
    result_ref[...] = mine + (own_ref[0] - image)


def place(group, own_blocks):
    return jnp.bitwise_xor(group // own_blocks, lax.axis_index("coarse")) * own_blocks + group % own_blocks


def pairs_of(x):
    half = x.shape[0] // 2
    return jnp.concatenate([x[:half], x[half:]], axis=1)


def masked_rows(x, mask_lists, pair_at, held_ref):
    pairs = x.shape[0]
    high, low = split(x)
    held_ref[pl.ds(0, pairs), :] = high.astype(f32)
    held_ref[pl.ds(pairs, pairs), :] = low.astype(f32)
    parts = []
    for part in range(2):
        rows = [
            jnp.broadcast_to(held_ref[pl.ds(part * pairs + p, 1), :], (2 * pairs, LANES)).astype(bf16)
            for p in range(pairs)
        ]
        parts.append(rows)
    return jnp.concatenate(
        [
            jnp.concatenate([mask * rows[pair_at(c)] for c, mask in enumerate(masks)], axis=1)
            for masks in mask_lists
            for rows in parts
        ],
        axis=0,
    )


def inverse_product(x, inverse_ref, held_ref):
    pairs = x.shape[0]
    groups = 2 * pairs
    row, lane = iota((groups, LANES), 0), iota((groups, LANES), 1)
    masks = [((row % pairs == p) & (row // pairs == lane // CELLS)).astype(bf16) for p in range(pairs)]
    sums = dot(masked_rows(x, [masks], lambda c: c, held_ref), inverse_ref[...])
    return pairs_of(sums[:groups] + sums[groups:])


def slot_pair(rows_ref, first, count):
    turned = rows_ref[pl.ds(first, CELLS * count), :].astype(bf16).T
    return turned if count == 2 else jnp.concatenate([turned, jnp.zeros_like(turned)], axis=1)


def target_rows(x, target_ref, start, stop, own_blocks, held_ref):
    groups, half = target_ref.shape[0], target_ref.shape[1] // 2
    per_part = half // LANES // (groups // own_blocks)
    per_block = own_blocks // 2
    masks = [[target_ref[:, pl.ds(t * half + c, LANES)] for c in range(start, stop, LANES)] for t in range(2)]

    def pair_at(chunk):
        chunk = chunk + start // LANES
        return chunk // per_part * per_block + chunk % per_block

    return masked_rows(x, masks, pair_at, held_ref)


def first_sweep_kernel(
    gathered_ref, mine_ref, beside_ref, first2_ref, second2_ref, first3_ref,
    side_ref, begun_ref, inverse_ref, target_ref, blocks_ref, sums_ref, held_ref,
):
    part_refs = (mine_ref, beside_ref, first2_ref, first3_ref)
    width = mine_ref.shape[1]
    own_blocks = width // CELLS
    pairs = side_ref.shape[0]
    groups = 2 * pairs
    base = 8 + CELLS
    nbrs = (mine_ref.shape[0] - base) // CELLS
    early = (first2_ref.shape[0] - base) // CELLS
    for i, ref in enumerate(part_refs):
        inverse_ref[pl.ds(i * width, width), :] = ref[pl.ds(8, CELLS), :].astype(bf16).T

    gathered = gathered_ref[...]
    devs = gathered.shape[0]
    lane = iota((8, LANES), 1)
    row = iota((groups, LANES), 0)
    number = 2 * (row % pairs) + row // pairs
    lefts, rights = [], []
    for start in range(0, devs, 32):
        value = jnp.zeros((8, LANES), f32)
        order = jnp.zeros((8, LANES), f32)
        for i in range(4):
            piece = gathered[start + 8 * i : start + 8 * i + 8]
            here = lane // 32 == i
            value = jnp.where(here, pltpu.roll(piece, 32 * i, 1) if i else piece, value)
            order = jnp.where(here, pltpu.roll(piece, (32 * i + 96) % LANES, 1) if i != 1 else piece, order)
        order = order.astype(i32)
        group, unit = place(order // CELLS, own_blocks), order % CELLS
        for s in range(8):
            left = jnp.where(number == group[s : s + 1], value[s : s + 1], 0.0)
            lefts.append(jnp.concatenate(split(left), axis=0))
            rights.append((iota((CELLS, LANES), 0) == unit[s : s + 1]).astype(bf16))
    side = dot_t(jnp.concatenate(lefts, axis=1), jnp.concatenate(rights, axis=1))
    side = pairs_of(side[:groups] + side[groups:])
    side_ref[...] = side
    begun = inverse_product(side, inverse_ref, held_ref)
    begun_ref[...] = begun

    row = iota((groups, width), 0)
    number = 2 * (row % pairs) + row // pairs
    twos = (nbrs + 1) // 2
    half = twos * width * len(part_refs)
    for i, ref in enumerate(part_refs):
        targets = place(ref[pl.ds(0, 8), :].astype(i32), own_blocks)
        for k in range(2 * twos):
            cols = pl.ds(k % 2 * half + (i * twos + k // 2) * width, width)
            chosen = number == targets[k : k + 1] if k < nbrs else jnp.zeros(row.shape, jnp.bool_)
            target_ref[:, cols] = chosen.astype(bf16)
        for q in range(twos):
            rows = pl.ds((i * twos + q) * width, width)
            count = min(2, nbrs - 2 * q)
            if i < 2 or 2 * q < early:
                blocks_ref[rows, :] = slot_pair(ref, base + 2 * q * CELLS, count)
            elif i == 2:
                blocks_ref[rows, :] = slot_pair(second2_ref, (2 * q - early) * CELLS, count)

    sums_ref[...] = dot(target_rows(begun, target_ref, 0, blocks_ref.shape[0], own_blocks, held_ref), blocks_ref[...])


def solve_kernel(
    devices, side_ref, begun_ref, inverse_ref, target_ref, blocks_ref, sums_ref, near_ref, far_ref, own_ref, selected_ref,
    second3_ref, products_ref,
    out_any, correction_any,
    last_ref, held_ref, result_ref, correction_ref,
    picked_ref, high_ref, low_ref, out_sem_ref,
):
    width = second3_ref.shape[1]
    own_blocks = width // CELLS
    groups, half = target_ref.shape[0], target_ref.shape[1] // 2
    pairs = groups // 2
    late = second3_ref.shape[0] // CELLS
    for q in range(0, late, 2):
        last_ref[pl.ds(q // 2 * width, width), :] = slot_pair(second3_ref, q * CELLS, min(2, late - q))
    side = side_ref[...]
    correction = begun_ref[...]
    split_at = blocks_ref.shape[0]
    for sweep in range(SWEEPS - 1):
        if sweep == 0:
            sums = sums_ref[...]
            spread = target_rows(correction, target_ref, split_at, half, own_blocks, held_ref)
        else:
            spread = target_rows(correction, target_ref, 0, half, own_blocks, held_ref)
            sums = dot(spread[:, :split_at], blocks_ref[...])
            spread = spread[:, split_at:]
        sums = sums + dot(spread, last_ref[...])
        image = sums[:groups] + sums[groups : 2 * groups]
        other = sums[2 * groups : 3 * groups] + sums[3 * groups :]
        image = pairs_of(image[:, :CELLS] + other[:, CELLS:])
        correction = correction + inverse_product(side - image, inverse_ref, held_ref)
    correction_ref[...] = correction[: own_blocks // 2]
    correction_copy = pltpu.make_async_copy(correction_ref, correction_any, out_sem_ref.at[0])
    correction_copy.start()

    order = window_of(near_ref, far_ref, own_ref, device_index(), devices)[2].astype(i32)
    rows = order.shape[0]
    unit = jnp.concatenate([order[:, :CELLS], order[:, CELLS:]], axis=0)
    chosen = (iota(unit.shape, 1) == unit % CELLS).astype(bf16)
    by_block = jnp.concatenate([correction[:, :CELLS], correction[:, CELLS:]], axis=0)
    values = dot_t(chosen, jnp.concatenate(split(by_block), axis=0))
    group = place(unit[:, : 2 * groups] // CELLS, own_blocks)
    group = group // 2 + group % 2 * pairs
    values = jnp.sum(jnp.where(iota(values.shape, 1) % groups == group, values, 0.0), axis=1, keepdims=True)
    corr = by_half([values[:rows], values[rows:]], (rows, LANES))
    finish(corr, near_ref, far_ref, own_ref, devices, selected_ref, products_ref, result_ref,
           picked_ref, high_ref, low_ref)
    result_copy = pltpu.make_async_copy(result_ref, out_any, out_sem_ref.at[1])
    result_copy.start()
    correction_copy.wait()
    result_copy.wait()


def finish_kernel(
    devices, corr_ref, near_ref, far_ref, own_ref, selected_ref, products_ref, result_ref, picked_ref, high_ref, low_ref,
):
    finish(corr_ref[...], near_ref, far_ref, own_ref, devices, selected_ref, products_ref, result_ref,
           picked_ref, high_ref, low_ref)


def call(kernel, out_shape, ins, outs=None, scratch=(), cost=None):
    spaces = dict(s=pltpu.SMEM, v=pltpu.VMEM, a=pl.ANY)
    many = isinstance(out_shape, tuple)
    specs = tuple(pl.BlockSpec(memory_space=spaces[c]) for c in outs or "v" * (len(out_shape) if many else 1))
    run = pl.pallas_call(
        kernel,
        out_shape=out_shape,
        in_specs=[pl.BlockSpec(memory_space=spaces[c]) for c in ins],
        out_specs=specs if many else specs[0],
        scratch_shapes=list(scratch),
        compiler_params=pltpu.CompilerParams(vmem_limit_bytes=VMEM_LIMIT),
        cost_estimate=cost and pl.CostEstimate(flops=cost, bytes_accessed=0, transcendentals=0),
    )

    def placed(*operands):
        return run(*(pltpu.with_memory_space_constraint(x, pltpu.HBM) if c == "a" else x for x, c in zip(operands, ins)))

    return placed


def shape_of(*dims):
    return jax.ShapeDtypeStruct(dims, f32)


def coarse_by_parts(restricted, coarse_order, coarse_values, coarse_rows, coarse_inverse):
    own = coarse_inverse.shape[1]
    own_blocks = own // CELLS
    total = own * lax.axis_size("coarse")
    start = lax.axis_index("coarse") * own
    side = jnp.zeros((total,), f32).at[coarse_order].add(restricted)
    side = lax.dynamic_slice_in_dim(lax.psum(side, BOTH), start, own)
    values = coarse_values.astype(f32).reshape(-1, CELLS, own_blocks, CELLS)
    inverse = coarse_inverse.astype(f32).reshape(CELLS, own_blocks, CELLS)

    def scale(x):
        x = x.reshape(own_blocks, CELLS)
        return jnp.einsum("oji,ji->jo", inverse, x, precision=lax.Precision.HIGHEST).reshape(-1)

    correction = scale(side)
    for _ in range(SWEEPS - 1):
        x = correction.reshape(own_blocks, CELLS)
        sums = jnp.einsum("vfmd,md->vmf", values, x, precision=lax.Precision.HIGHEST)
        image = jax.ops.segment_sum(
            sums.reshape(-1, CELLS), coarse_rows.reshape(-1), num_segments=total // CELLS
        ).reshape(-1)
        image = lax.dynamic_slice_in_dim(lax.psum(image, "coarse"), start, own)
        correction = correction + scale(side - image)
    return correction, lax.all_gather(correction, "coarse", axis=0, tiled=True)


def shards(
    devices, rhs, fine_values, fine_columns, smoother, reaction, pit_counts, weights, coarse_order,
    coarse_values, coarse_rows, coarse_inverse,
):
    cells = rhs.shape[0]
    pairs = cells // LANES
    aggs = 2 * pairs
    nbrs = fine_columns.shape[0]
    parts = lax.axis_size("coarse")
    rhs, reaction, weights = (x.reshape(pairs, LANES) for x in (rhs, reaction, weights))
    rows = pairs + 2 * HALO_ROWS
    vector = pltpu.VMEM((pairs, LANES), f32)
    products = [pltpu.VMEM((CELLS, cells), bf16)] * 2
    picked = pltpu.VMEM((nbrs * pairs, LANES), f32)
    copies = pltpu.SemaphoreType.DMA((4,))
    edge = shape_of(3, HALO_ROWS, LANES)

    copied = parts == 4 and devices % 32 == 0 and devices <= 64
    start_shapes = (
        edge, edge, shape_of(3, pairs, LANES), jax.ShapeDtypeStruct(smoother.shape, bf16)
    )
    start_ins = (rhs, weights, coarse_order.reshape(1, aggs), smoother)
    start_scratch = [vector, vector, pltpu.VMEM((1, aggs), i32)]
    if copied:
        deep = coarse_values.shape[0] * CELLS
        width = coarse_inverse.shape[1]
        early = EARLY * CELLS
        near, onward, own, smoother_here, packed, first, second = call(
            start_pack_kernel,
            (*start_shapes, shape_of(8 + CELLS + deep, width), shape_of(8 + CELLS + early, width),
             shape_of(deep - early, width)),
            "aaaaaaa",
            scratch=[
                *start_scratch, pltpu.VMEM(coarse_rows.shape[::-1], i32), pltpu.VMEM((deep, width), bf16),
                pltpu.VMEM(coarse_inverse.shape, bf16), *products, pltpu.SemaphoreType.DMA((7,)),
            ],
        )(*start_ins, coarse_rows.T, coarse_values.reshape(deep, width), coarse_inverse)
        swap = [(c, c ^ 1) for c in range(parts)]
        across = [(c, c ^ 2) for c in range(parts)]
        first2 = lax.ppermute(first, "coarse", across)
    else:
        near, onward, own, smoother_here = call(start_kernel, start_shapes, "aaaa", scratch=[*start_scratch, *products, copies])(
            *start_ins
        )

    partner = [(d, d ^ 1) for d in range(devices)]
    chain = []
    for d in range(devices):
        target = d + 2 if d % 2 == 0 else d - 2
        chain.append((d, target if 0 <= target < devices else d ^ 1))
    onward = lax.ppermute(onward, BOTH, partner)
    near = lax.ppermute(near, BOTH, partner)

    if copied:
        second, onward = lax.optimization_barrier((second, onward))
    far = lax.ppermute(onward, BOTH, chain)
    selected, weighed, local, masked, fine_here = call(
        prepare_kernel,
        (jax.ShapeDtypeStruct((aggs * nbrs, 4 * rows), bf16), shape_of(nbrs * pairs, 8, LANES), shape_of(2, pairs, LANES),
         shape_of(pairs, LANES), jax.ShapeDtypeStruct(fine_values.shape, bf16)),
        "svaaaa",
        scratch=[vector, vector, pltpu.VMEM(fine_columns.shape, i32), pltpu.VMEM((CELLS, cells), f32), pltpu.SemaphoreType.DMA((3 + nbrs,))],
        cost=10_000_000_000,
    )(pit_counts, own, rhs, reaction, fine_columns, fine_values)
    smoothed_fine = call(products_kernel, shape_of(*fine_values.shape), "vvv")(masked, fine_here, smoother_here)

    if copied:
        beside = lax.ppermute(packed, "coarse", swap)
        second2 = lax.ppermute(second, "coarse", across)
        first3 = lax.ppermute(first2, "coarse", swap)

    sent = call(
        functools.partial(residual_kernel, devices), shape_of(devices, LANES), "vvvvvv", scratch=[picked], cost=None
    )(near, far, own, selected, weighed, local)

    finish_scratch = [picked, *products]
    common = (near, far, own, selected)
    if copied:
        gathered = lax.all_to_all(sent, BOTH, 0, 0, tiled=True)
        first3, second2, gathered = lax.optimization_barrier((first3, second2, gathered))
        second3 = lax.ppermute(second2, "coarse", swap)
        unknowns = parts * width
        groups = unknowns // CELLS
        twos, late = (nbrs + 1) // 2, (nbrs - EARLY + 1) // 2
        begun = call(
            first_sweep_kernel,
            (shape_of(unknowns // LANES, LANES), shape_of(unknowns // LANES, LANES),
             jax.ShapeDtypeStruct((unknowns, CELLS), bf16), jax.ShapeDtypeStruct((groups, 2 * twos * unknowns), bf16),
             jax.ShapeDtypeStruct((twos * unknowns - late * width, LANES), bf16), shape_of(4 * groups, LANES)),
            "vvvvvv",
            scratch=[pltpu.VMEM((groups, LANES), f32)],
        )(gathered, packed, beside, first2, second2, first3)
        result, correction = call(
            functools.partial(solve_kernel, devices),
            (shape_of(pairs, LANES), shape_of(width // LANES, LANES)),
            "vvvvvv" + "vvvv" + "vv",
            outs="aa",
            scratch=[
                pltpu.VMEM((late * width, LANES), bf16), pltpu.VMEM((groups, LANES), f32), vector,
                pltpu.VMEM((width // LANES, LANES), f32), *finish_scratch, pltpu.SemaphoreType.DMA((2,)),
            ],
        )(*begun, *common, second3, smoothed_fine)
        correction = correction.reshape(-1)
    else:
        correction, everywhere = coarse_by_parts(
            sent[0, :aggs], coarse_order, coarse_values, coarse_rows, coarse_inverse
        )
        index = device_index()
        low = jnp.where(index == 0, 0.0, jnp.where(index % 2 == 0, far[2], near[2]))
        high = jnp.where(index == devices - 1, 0.0, jnp.where(index % 2 == 0, near[2], far[2]))
        order = jnp.concatenate([low, own[2], high], axis=0).astype(i32)
        corr = jnp.repeat(everywhere[order[:, ::CELLS]], CELLS, axis=1)
        result = call(
            functools.partial(finish_kernel, devices), shape_of(pairs, LANES), "vvvvvv", scratch=finish_scratch
        )(corr, *common, smoothed_fine)
    return result.reshape(-1), correction


def solution(mesh):
    devices = mesh.shape["fine"] * mesh.shape["coarse"]
    in_specs = (
        P(BOTH),
        P(None, None, BOTH),
        P(None, BOTH),
        P(None, BOTH),
        P(BOTH),
        P(BOTH),
        P(BOTH),
        P(BOTH),
        P(None, None, "coarse"),
        P(None, "coarse"),
        P(None, "coarse"),
    )
    return jax.shard_map(
        functools.partial(shards, devices),
        mesh=mesh,
        in_specs=in_specs,
        out_specs=(P(BOTH), P("coarse")),
        check_vma=False,
    )
```

```python
import functools

import jax
import jax.numpy as jnp
from jax import lax
from jax.experimental import pallas as pl
from jax.experimental.pallas import tpu as pltpu
from jax.sharding import PartitionSpec as P

CELLS = 64
LANES = 128
HALO_ROWS = 8
SWEEPS = 4
EARLY = 0
BOTH = ("fine", "coarse")
f32, bf16, i32 = jnp.float32, jnp.bfloat16, jnp.int32
VMEM_LIMIT = 24 * 1024 * 1024


def iota(shape, axis):
    return lax.broadcasted_iota(i32, shape, axis)


def split(x):
    high = x.astype(bf16)
    return high, (x - high.astype(f32)).astype(bf16)


def dot(a, b):
    return lax.dot_general(a, b, (((1,), (0,)), ((), ())), preferred_element_type=f32)


def dot_t(a, b):
    return lax.dot_general(a, b, (((1,), (1,)), ((), ())), preferred_element_type=f32)


def cell_sums(high_ref, low_ref):
    width = high_ref.shape[1]
    pairs = width // LANES
    row, lane = iota((2 * pairs, width), 0), iota((2 * pairs, width), 1)
    member = (lane // CELLS == 2 * (row % pairs) + row // pairs).astype(bf16)
    sums = dot_t(member, high_ref[...]) + dot_t(member, low_ref[...])
    return jnp.concatenate([sums[:pairs], sums[pairs:]], axis=1)


def apply_smoother(vector, smoother_ref, high_ref, low_ref):
    for p in range(vector.shape[0]):
        cols = pl.ds(p * LANES, LANES)
        product = smoother_ref[:, cols].astype(f32) * vector[p : p + 1, :]
        high_ref[:, cols], low_ref[:, cols] = split(product)
    return cell_sums(high_ref, low_ref)


def selection(columns, half_rows, pairs):
    nbrs, aggs = columns.shape
    at, who = iota((pairs, aggs), 1), iota((pairs, aggs), 0)
    chosen = [
        jnp.where(at == 2 * who + half, columns[k : k + 1].astype(f32), 0.0)
        for half in range(2)
        for k in range(nbrs)
    ]
    block = dot(jnp.concatenate(chosen, axis=0).astype(bf16), jnp.ones((aggs, 4 * half_rows), bf16)).astype(i32)
    half = iota(block.shape, 0) // (nbrs * pairs)
    place = block // 2 + jnp.where(block % 2 == half, 0, half_rows)
    return (iota(block.shape, 1) % (2 * half_rows) == place).astype(bf16)


def pick(window, selected):
    high, low = split(jnp.concatenate([window, pltpu.roll(window, CELLS, 1)], axis=0))
    picked = dot(selected, jnp.concatenate([high, low], axis=0))
    count = selected.shape[0] // 2
    lane = iota((count, LANES), 1)
    return jnp.where(lane < CELLS, picked[:count], picked[count:])


def apply_smoothed_fine(window, products_ref, selected, picked_ref, high_ref, low_ref):
    nbrs, _, width = products_ref.shape
    pairs = width // LANES
    picked_ref[...] = pick(window, selected)
    for p in range(pairs):
        cols = pl.ds(p * LANES, LANES)
        total = None
        for k in range(nbrs):
            term = products_ref[k, :, cols] * picked_ref[pl.ds(k * pairs + p, 1), :]
            total = term if total is None else total + term
        high_ref[:, cols], low_ref[:, cols] = split(total)
    return cell_sums(high_ref, low_ref)


def as_columns(row, pairs):
    shape = (pairs, row.shape[1])
    at, who = iota(shape, 1), iota(shape, 0)
    return [
        jnp.sum(jnp.where(at == 2 * who + half, row, 0.0), axis=1, keepdims=True)
        for half in range(2)
    ]


def by_half(columns, shape):
    return jnp.where(iota(shape, 1) < CELLS, columns[0], columns[1])


def fetch(sem_ref, *pairs):
    copies = [pltpu.make_async_copy(src, dst, sem_ref.at[i]) for i, (src, dst) in enumerate(pairs)]
    for copy in copies:
        copy.start()
    return copies


def start(rhs_ref, weights_ref, order_ref, smoother_ref, near_ref, onward_ref, own_ref, high_ref, low_ref):
    pairs = rhs_ref.shape[0]
    smoothed = apply_smoother(rhs_ref[...], smoother_ref, high_ref, low_ref)
    order = by_half(as_columns(order_ref[...].astype(f32), pairs), (pairs, LANES))
    even = lax.axis_index("coarse") % 2 == 0
    for i, part in enumerate((smoothed, weights_ref[...], order)):
        own_ref[i] = part
        bottom, top = part[:HALO_ROWS], part[pairs - HALO_ROWS :]
        near_ref[i] = jnp.where(even, top, bottom)
        onward_ref[i] = jnp.where(even, bottom, top)


def start_kernel(
    rhs_any, weights_any, order_any, smoother_any, near_ref, onward_ref, own_ref, smoother_ref,
    rhs_ref, weights_ref, order_ref, high_ref, low_ref, sem_ref,
):
    copies = fetch(
        sem_ref, (smoother_any, smoother_ref), (rhs_any, rhs_ref), (weights_any, weights_ref), (order_any, order_ref)
    )
    for copy in copies:
        copy.wait()
    start(rhs_ref, weights_ref, order_ref, smoother_ref, near_ref, onward_ref, own_ref, high_ref, low_ref)


def start_pack_kernel(
    rhs_any, weights_any, order_any, smoother_any, rows_any, values_any, inverse_any,
    near_ref, onward_ref, own_ref, smoother_ref, packed_ref, first_ref, second_ref,
    rhs_ref, weights_ref, order_ref, rows_ref, values_ref, inverse_ref, high_ref, low_ref, sem_ref,
):
    copies = fetch(
        sem_ref, (smoother_any, smoother_ref), (rhs_any, rhs_ref), (weights_any, weights_ref), (order_any, order_ref),
        (values_any, values_ref), (inverse_any, inverse_ref), (rows_any, rows_ref),
    )
    for copy in copies[:4]:
        copy.wait()
    start(rhs_ref, weights_ref, order_ref, smoother_ref, near_ref, onward_ref, own_ref, high_ref, low_ref)
    for copy in copies[4:]:
        copy.wait()
    own_blocks, nbrs = rows_ref.shape
    deep, width = values_ref.shape
    at, slot = iota((8, nbrs), 1), iota((8, nbrs), 0)
    block = iota((8, width), 1) // CELLS
    rows = jnp.zeros((8, width), f32)
    for j in range(own_blocks):
        targets = jnp.where(at == slot, rows_ref[j : j + 1, :].astype(f32), 0.0)
        rows = jnp.where(block == j, jnp.sum(targets, axis=1, keepdims=True), rows)
    inverse = inverse_ref[...].astype(f32)
    for ref in (packed_ref, first_ref):
        ref[pl.ds(0, 8), :] = rows
        ref[pl.ds(8, CELLS), :] = inverse
    base = 8 + CELLS
    early = first_ref.shape[0] - base
    for r in range(0, deep, CELLS):
        values = values_ref[pl.ds(r, CELLS), :].astype(f32)
        packed_ref[pl.ds(base + r, CELLS), :] = values
        if r < early:
            first_ref[pl.ds(base + r, CELLS), :] = values
        else:
            second_ref[pl.ds(r - early, CELLS), :] = values


def window_of(near_ref, far_ref, own_ref, device, devices):
    even = device % 2 == 0
    near, far = near_ref[...], far_ref[...]
    low = jnp.where(device == 0, 0.0, jnp.where(even, far, near))
    high = jnp.where(device == devices - 1, 0.0, jnp.where(even, near, far))
    return [jnp.concatenate([low[i], own_ref[i], high[i]], axis=0) for i in range(3)]


def device_index():
    return lax.axis_index("fine") * lax.axis_size("coarse") + lax.axis_index("coarse")


def prepare_kernel(
    counts_ref, own_ref, rhs_any, reaction_any, columns_any, fine_any, selected_ref, weighed_ref, local_ref,
    masked_ref, fine_ref, rhs_ref, reaction_ref, columns_ref, wide_ref, sem_ref,
):
    copies = fetch(
        sem_ref, (columns_any, columns_ref), (rhs_any, rhs_ref), (reaction_any, reaction_ref),
        *((fine_any.at[k], fine_ref.at[k]) for k in range(fine_ref.shape[0])),
    )
    nbrs, _, width = fine_ref.shape
    pairs = width // LANES
    weights = own_ref[1]
    by_agg = jnp.concatenate([weights[:, :CELLS], weights[:, CELLS:]], axis=0)
    row, lane = iota((2 * pairs, width), 0), iota((2 * pairs, width), 1)
    member = (lane // CELLS == 2 * (row % pairs) + row // pairs).astype(bf16)
    wide = None
    for part in split(by_agg):
        term = lax.dot_general(part, member, (((0,), (0,)), ((), ())), preferred_element_type=f32)
        wide = term if wide is None else wide + term
    wide_ref[...] = wide
    for copy in copies[:3]:
        copy.wait()
    agg = 2 * iota((pairs, LANES), 0) + iota((pairs, LANES), 1) // CELLS
    reaction = jnp.where(agg < counts_ref[0], reaction_ref[...], 0.0)
    local_ref[0] = weights * rhs_ref[...]
    local_ref[1] = weights * reaction
    masked_ref[...] = reaction
    selected_ref[...] = selection(columns_ref[...], pairs + 2 * HALO_ROWS, pairs)
    for k in range(nbrs):
        copies[3 + k].wait()
        for p in range(pairs):
            cols = pl.ds(p * LANES, LANES)
            term = fine_ref[k, :, cols].astype(f32) * wide_ref[:, cols]
            total = term[:8]
            for r in range(8, CELLS, 8):
                total = total + term[r : r + 8]
            weighed_ref[k * pairs + p] = total


def products_kernel(reaction_ref, fine_ref, smoother_ref, products_ref):
    nbrs, _, width = fine_ref.shape
    pairs = width // LANES
    lane = iota((CELLS, LANES), 1)
    for p in range(pairs):
        cols = pl.ds(p * LANES, LANES)
        left = smoother_ref[:, cols]
        rights = []
        for k in range(nbrs):
            block = fine_ref[k, :, cols]
            zero = jnp.zeros_like(block)
            apart = [jnp.where(lane < CELLS, block, zero), jnp.where(lane < CELLS, zero, block)]
            rights.append(jnp.concatenate(apart, axis=0))
        both = dot(left, jnp.concatenate(rights, axis=1))
        for k in range(nbrs):
            product = both[:, k * LANES : (k + 1) * LANES]
            products_ref[k, :, cols] = product if k else product + left.astype(f32) * reaction_ref[p : p + 1, :]


def residual_kernel(
    devices, near_ref, far_ref, own_ref, selected_ref, weighed_ref, local_ref, out_ref, picked_ref,
):
    smoothed, _, _ = window_of(near_ref, far_ref, own_ref, device_index(), devices)
    picked_ref[...] = pick(smoothed, selected_ref[...])
    pairs = own_ref.shape[1]
    nbrs = picked_ref.shape[0] // pairs
    images = []
    for p in range(pairs):
        total = None
        for k in range(nbrs):
            term = weighed_ref[k * pairs + p] * picked_ref[pl.ds(k * pairs + p, 1), :]
            total = term if total is None else total + term
        images.append(jnp.sum(total, axis=0, keepdims=True))
    weighted = local_ref[0] - local_ref[1] * own_ref[0] - jnp.concatenate(images, axis=0)
    shape = (pairs, LANES)
    lane, who = iota(shape, 1), iota(shape, 0)
    row = jnp.zeros((1, LANES), f32)
    for half in range(2):
        inside = lane // CELLS == half
        restricted = jnp.sum(jnp.where(inside, weighted, 0.0), axis=1, keepdims=True)
        order = jnp.max(jnp.where(inside, own_ref[2], 0.0), axis=1, keepdims=True)
        spread = jnp.where(lane == 2 * who + half, restricted, 0.0)
        spread = spread + jnp.where(lane == 2 * (pairs + who) + half, order, 0.0)
        row = row + jnp.sum(spread, axis=0, keepdims=True)
    out_ref[...] = jnp.broadcast_to(row, out_ref.shape)


def finish(corr, near_ref, far_ref, own_ref, devices, selected_ref, products_ref, result_ref,
           picked_ref, high_ref, low_ref):
    smoothed, weights, _ = window_of(near_ref, far_ref, own_ref, device_index(), devices)
    corrected = smoothed + weights * corr
    mine = corrected[HALO_ROWS : HALO_ROWS + own_ref.shape[1]]
    image = apply_smoothed_fine(corrected, products_ref, selected_ref[...], picked_ref, high_ref, low_ref)
    result_ref[...] = mine + (own_ref[0] - image)


def place(group, own_blocks):
    return jnp.bitwise_xor(group // own_blocks, lax.axis_index("coarse")) * own_blocks + group % own_blocks


def pairs_of(x):
    half = x.shape[0] // 2
    return jnp.concatenate([x[:half], x[half:]], axis=1)


def masked_rows(x, mask_lists, pair_at, held_ref):
    pairs = x.shape[0]
    high, low = split(x)
    held_ref[pl.ds(0, pairs), :] = high.astype(f32)
    held_ref[pl.ds(pairs, pairs), :] = low.astype(f32)
    parts = []
    for part in range(2):
        rows = [
            jnp.broadcast_to(held_ref[pl.ds(part * pairs + p, 1), :], (2 * pairs, LANES)).astype(bf16)
            for p in range(pairs)
        ]
        parts.append(rows)
    return jnp.concatenate(
        [
            jnp.concatenate([mask * rows[pair_at(c)] for c, mask in enumerate(masks)], axis=1)
            for masks in mask_lists
            for rows in parts
        ],
        axis=0,
    )


def inverse_product(x, inverse_ref, held_ref):
    pairs = x.shape[0]
    groups = 2 * pairs
    row, lane = iota((groups, LANES), 0), iota((groups, LANES), 1)
    masks = [((row % pairs == p) & (row // pairs == lane // CELLS)).astype(bf16) for p in range(pairs)]
    sums = dot(masked_rows(x, [masks], lambda c: c, held_ref), inverse_ref[...])
    return pairs_of(sums[:groups] + sums[groups:])


def slot_pair(rows_ref, first, count):
    turned = rows_ref[pl.ds(first, CELLS * count), :].astype(bf16).T
    return turned if count == 2 else jnp.concatenate([turned, jnp.zeros_like(turned)], axis=1)


def target_rows(x, target_ref, start, stop, own_blocks, held_ref):
    groups, half = target_ref.shape[0], target_ref.shape[1] // 2
    per_part = half // LANES // (groups // own_blocks)
    per_block = own_blocks // 2
    masks = [[target_ref[:, pl.ds(t * half + c, LANES)] for c in range(start, stop, LANES)] for t in range(2)]

    def pair_at(chunk):
        chunk = chunk + start // LANES
        return chunk // per_part * per_block + chunk % per_block

    return masked_rows(x, masks, pair_at, held_ref)


def first_sweep_kernel(
    gathered_ref, mine_ref, beside_ref, first2_ref, second2_ref, first3_ref,
    side_ref, begun_ref, inverse_ref, target_ref, blocks_ref, sums_ref, held_ref,
):
    part_refs = (mine_ref, beside_ref, first2_ref, first3_ref)
    width = mine_ref.shape[1]
    own_blocks = width // CELLS
    pairs = side_ref.shape[0]
    groups = 2 * pairs
    base = 8 + CELLS
    nbrs = (mine_ref.shape[0] - base) // CELLS
    early = (first2_ref.shape[0] - base) // CELLS
    for i, ref in enumerate(part_refs):
        inverse_ref[pl.ds(i * width, width), :] = ref[pl.ds(8, CELLS), :].astype(bf16).T

    gathered = gathered_ref[...]
    devs = gathered.shape[0]
    lane = iota((8, LANES), 1)
    row = iota((groups, LANES), 0)
    number = 2 * (row % pairs) + row // pairs
    lefts, rights = [], []
    for start in range(0, devs, 32):
        value = jnp.zeros((8, LANES), f32)
        order = jnp.zeros((8, LANES), f32)
        for i in range(4):
            piece = gathered[start + 8 * i : start + 8 * i + 8]
            here = lane // 32 == i
            value = jnp.where(here, pltpu.roll(piece, 32 * i, 1) if i else piece, value)
            order = jnp.where(here, pltpu.roll(piece, (32 * i + 96) % LANES, 1) if i != 1 else piece, order)
        order = order.astype(i32)
        group, unit = place(order // CELLS, own_blocks), order % CELLS
        for s in range(8):
            left = jnp.where(number == group[s : s + 1], value[s : s + 1], 0.0)
            lefts.append(jnp.concatenate(split(left), axis=0))
            rights.append((iota((CELLS, LANES), 0) == unit[s : s + 1]).astype(bf16))
    side = dot_t(jnp.concatenate(lefts, axis=1), jnp.concatenate(rights, axis=1))
    side = pairs_of(side[:groups] + side[groups:])
    side_ref[...] = side
    begun = inverse_product(side, inverse_ref, held_ref)
    begun_ref[...] = begun

    row = iota((groups, width), 0)
    number = 2 * (row % pairs) + row // pairs
    twos = (nbrs + 1) // 2
    half = twos * width * len(part_refs)
    for i, ref in enumerate(part_refs):
        targets = place(ref[pl.ds(0, 8), :].astype(i32), own_blocks)
        for k in range(2 * twos):
            cols = pl.ds(k % 2 * half + (i * twos + k // 2) * width, width)
            chosen = number == targets[k : k + 1] if k < nbrs else jnp.zeros(row.shape, jnp.bool_)
            target_ref[:, cols] = chosen.astype(bf16)
        for q in range(twos):
            rows = pl.ds((i * twos + q) * width, width)
            count = min(2, nbrs - 2 * q)
            if i < 2 or 2 * q < early:
                blocks_ref[rows, :] = slot_pair(ref, base + 2 * q * CELLS, count)
            elif i == 2:
                blocks_ref[rows, :] = slot_pair(second2_ref, (2 * q - early) * CELLS, count)

    sums_ref[...] = dot(target_rows(begun, target_ref, 0, blocks_ref.shape[0], own_blocks, held_ref), blocks_ref[...])


def solve_kernel(
    devices, side_ref, begun_ref, inverse_ref, target_ref, blocks_ref, sums_ref, near_ref, far_ref, own_ref, selected_ref,
    second3_ref, products_ref,
    out_any, correction_any,
    last_ref, held_ref, result_ref, correction_ref,
    picked_ref, high_ref, low_ref, out_sem_ref,
):
    width = second3_ref.shape[1]
    own_blocks = width // CELLS
    groups, half = target_ref.shape[0], target_ref.shape[1] // 2
    pairs = groups // 2
    late = second3_ref.shape[0] // CELLS
    for q in range(0, late, 2):
        last_ref[pl.ds(q // 2 * width, width), :] = slot_pair(second3_ref, q * CELLS, min(2, late - q))
    side = side_ref[...]
    correction = begun_ref[...]
    split_at = blocks_ref.shape[0]
    for sweep in range(SWEEPS - 1):
        if sweep == 0:
            sums = sums_ref[...]
            spread = target_rows(correction, target_ref, split_at, half, own_blocks, held_ref)
        else:
            spread = target_rows(correction, target_ref, 0, half, own_blocks, held_ref)
            sums = dot(spread[:, :split_at], blocks_ref[...])
            spread = spread[:, split_at:]
        sums = sums + dot(spread, last_ref[...])
        image = sums[:groups] + sums[groups : 2 * groups]
        other = sums[2 * groups : 3 * groups] + sums[3 * groups :]
        image = pairs_of(image[:, :CELLS] + other[:, CELLS:])
        correction = correction + inverse_product(side - image, inverse_ref, held_ref)
    correction_ref[...] = correction[: own_blocks // 2]
    correction_copy = pltpu.make_async_copy(correction_ref, correction_any, out_sem_ref.at[0])
    correction_copy.start()

    order = window_of(near_ref, far_ref, own_ref, device_index(), devices)[2].astype(i32)
    rows = order.shape[0]
    unit = jnp.concatenate([order[:, :CELLS], order[:, CELLS:]], axis=0)
    chosen = (iota(unit.shape, 1) == unit % CELLS).astype(bf16)
    by_block = jnp.concatenate([correction[:, :CELLS], correction[:, CELLS:]], axis=0)
    values = dot_t(chosen, jnp.concatenate(split(by_block), axis=0))
    group = place(unit[:, : 2 * groups] // CELLS, own_blocks)
    group = group // 2 + group % 2 * pairs
    values = jnp.sum(jnp.where(iota(values.shape, 1) % groups == group, values, 0.0), axis=1, keepdims=True)
    corr = by_half([values[:rows], values[rows:]], (rows, LANES))
    finish(corr, near_ref, far_ref, own_ref, devices, selected_ref, products_ref, result_ref,
           picked_ref, high_ref, low_ref)
    result_copy = pltpu.make_async_copy(result_ref, out_any, out_sem_ref.at[1])
    result_copy.start()
    correction_copy.wait()
    result_copy.wait()


def finish_kernel(
    devices, corr_ref, near_ref, far_ref, own_ref, selected_ref, products_ref, result_ref, picked_ref, high_ref, low_ref,
):
    finish(corr_ref[...], near_ref, far_ref, own_ref, devices, selected_ref, products_ref, result_ref,
           picked_ref, high_ref, low_ref)


def call(kernel, out_shape, ins, outs=None, scratch=(), cost=None):
    spaces = dict(s=pltpu.SMEM, v=pltpu.VMEM, a=pl.ANY)
    many = isinstance(out_shape, tuple)
    specs = tuple(pl.BlockSpec(memory_space=spaces[c]) for c in outs or "v" * (len(out_shape) if many else 1))
    run = pl.pallas_call(
        kernel,
        out_shape=out_shape,
        in_specs=[pl.BlockSpec(memory_space=spaces[c]) for c in ins],
        out_specs=specs if many else specs[0],
        scratch_shapes=list(scratch),
        compiler_params=pltpu.CompilerParams(vmem_limit_bytes=VMEM_LIMIT),
        cost_estimate=cost and pl.CostEstimate(flops=cost, bytes_accessed=0, transcendentals=0),
    )

    def placed(*operands):
        return run(*(pltpu.with_memory_space_constraint(x, pltpu.HBM) if c == "a" else x for x, c in zip(operands, ins)))

    return placed


def shape_of(*dims):
    return jax.ShapeDtypeStruct(dims, f32)


def coarse_by_parts(restricted, coarse_order, coarse_values, coarse_rows, coarse_inverse):
    own = coarse_inverse.shape[1]
    own_blocks = own // CELLS
    total = own * lax.axis_size("coarse")
    start = lax.axis_index("coarse") * own
    side = jnp.zeros((total,), f32).at[coarse_order].add(restricted)
    side = lax.dynamic_slice_in_dim(lax.psum(side, BOTH), start, own)
    values = coarse_values.astype(f32).reshape(-1, CELLS, own_blocks, CELLS)
    inverse = coarse_inverse.astype(f32).reshape(CELLS, own_blocks, CELLS)

    def scale(x):
        x = x.reshape(own_blocks, CELLS)
        return jnp.einsum("oji,ji->jo", inverse, x, precision=lax.Precision.HIGHEST).reshape(-1)

    correction = scale(side)
    for _ in range(SWEEPS - 1):
        x = correction.reshape(own_blocks, CELLS)
        sums = jnp.einsum("vfmd,md->vmf", values, x, precision=lax.Precision.HIGHEST)
        image = jax.ops.segment_sum(
            sums.reshape(-1, CELLS), coarse_rows.reshape(-1), num_segments=total // CELLS
        ).reshape(-1)
        image = lax.dynamic_slice_in_dim(lax.psum(image, "coarse"), start, own)
        correction = correction + scale(side - image)
    return correction, lax.all_gather(correction, "coarse", axis=0, tiled=True)


def shards(
    devices, rhs, fine_values, fine_columns, smoother, reaction, pit_counts, weights, coarse_order,
    coarse_values, coarse_rows, coarse_inverse,
):
    cells = rhs.shape[0]
    pairs = cells // LANES
    aggs = 2 * pairs
    nbrs = fine_columns.shape[0]
    parts = lax.axis_size("coarse")
    rhs, reaction, weights = (x.reshape(pairs, LANES) for x in (rhs, reaction, weights))
    rows = pairs + 2 * HALO_ROWS
    vector = pltpu.VMEM((pairs, LANES), f32)
    products = [pltpu.VMEM((CELLS, cells), bf16)] * 2
    picked = pltpu.VMEM((nbrs * pairs, LANES), f32)
    copies = pltpu.SemaphoreType.DMA((4,))
    edge = shape_of(3, HALO_ROWS, LANES)

    copied = parts == 4 and devices % 32 == 0 and devices <= 64
    start_shapes = (
        edge, edge, shape_of(3, pairs, LANES), jax.ShapeDtypeStruct(smoother.shape, bf16)
    )
    start_ins = (rhs, weights, coarse_order.reshape(1, aggs), smoother)
    start_scratch = [vector, vector, pltpu.VMEM((1, aggs), i32)]
    if copied:
        deep = coarse_values.shape[0] * CELLS
        width = coarse_inverse.shape[1]
        early = EARLY * CELLS
        near, onward, own, smoother_here, packed, first, second = call(
            start_pack_kernel,
            (*start_shapes, shape_of(8 + CELLS + deep, width), shape_of(8 + CELLS + early, width),
             shape_of(deep - early, width)),
            "aaaaaaa",
            scratch=[
                *start_scratch, pltpu.VMEM(coarse_rows.shape[::-1], i32), pltpu.VMEM((deep, width), bf16),
                pltpu.VMEM(coarse_inverse.shape, bf16), *products, pltpu.SemaphoreType.DMA((7,)),
            ],
        )(*start_ins, coarse_rows.T, coarse_values.reshape(deep, width), coarse_inverse)
        swap = [(c, c ^ 1) for c in range(parts)]
        across = [(c, c ^ 2) for c in range(parts)]
        first2 = lax.ppermute(first, "coarse", across)
    else:
        near, onward, own, smoother_here = call(start_kernel, start_shapes, "aaaa", scratch=[*start_scratch, *products, copies])(
            *start_ins
        )

    partner = [(d, d ^ 1) for d in range(devices)]
    chain = []
    for d in range(devices):
        target = d + 2 if d % 2 == 0 else d - 2
        chain.append((d, target if 0 <= target < devices else d ^ 1))
    onward = lax.ppermute(onward, BOTH, partner)
    near, onward = lax.optimization_barrier((near, onward))
    near = lax.ppermute(near, BOTH, partner)

    if copied:
        second, packed, onward = lax.optimization_barrier((second, packed, onward))
    far = lax.ppermute(onward, BOTH, chain)
    selected, weighed, local, masked, fine_here = call(
        prepare_kernel,
        (jax.ShapeDtypeStruct((aggs * nbrs, 4 * rows), bf16), shape_of(nbrs * pairs, 8, LANES), shape_of(2, pairs, LANES),
         shape_of(pairs, LANES), jax.ShapeDtypeStruct(fine_values.shape, bf16)),
        "svaaaa",
        scratch=[vector, vector, pltpu.VMEM(fine_columns.shape, i32), pltpu.VMEM((CELLS, cells), f32), pltpu.SemaphoreType.DMA((3 + nbrs,))],
        cost=10_000_000_000,
    )(pit_counts, own, rhs, reaction, fine_columns, fine_values)
    smoothed_fine = call(products_kernel, shape_of(*fine_values.shape), "vvv")(masked, fine_here, smoother_here)

    if copied:
        beside = lax.ppermute(packed, "coarse", swap)
        second2 = lax.ppermute(second, "coarse", across)

    sent = call(
        functools.partial(residual_kernel, devices), shape_of(devices, LANES), "vvvvvv", scratch=[picked], cost=None
    )(near, far, own, selected, weighed, local)

    finish_scratch = [picked, *products]
    common = (near, far, own, selected)
    if copied:
        first2, _ = lax.optimization_barrier((first2, sent))
        first3 = lax.ppermute(first2, "coarse", swap)
        gathered = lax.all_to_all(sent, BOTH, 0, 0, tiled=True)
        first3, second2, gathered = lax.optimization_barrier((first3, second2, gathered))
        second3 = lax.ppermute(second2, "coarse", swap)
        unknowns = parts * width
        groups = unknowns // CELLS
        twos, late = (nbrs + 1) // 2, (nbrs - EARLY + 1) // 2
        begun = call(
            first_sweep_kernel,
            (shape_of(unknowns // LANES, LANES), shape_of(unknowns // LANES, LANES),
             jax.ShapeDtypeStruct((unknowns, CELLS), bf16), jax.ShapeDtypeStruct((groups, 2 * twos * unknowns), bf16),
             jax.ShapeDtypeStruct((twos * unknowns - late * width, LANES), bf16), shape_of(4 * groups, LANES)),
            "vvvvvv",
            scratch=[pltpu.VMEM((groups, LANES), f32)],
        )(gathered, packed, beside, first2, second2, first3)
        result, correction = call(
            functools.partial(solve_kernel, devices),
            (shape_of(pairs, LANES), shape_of(width // LANES, LANES)),
            "vvvvvv" + "vvvv" + "vv",
            outs="aa",
            scratch=[
                pltpu.VMEM((late * width, LANES), bf16), pltpu.VMEM((groups, LANES), f32), vector,
                pltpu.VMEM((width // LANES, LANES), f32), *finish_scratch, pltpu.SemaphoreType.DMA((2,)),
            ],
        )(*begun, *common, second3, smoothed_fine)
        correction = correction.reshape(-1)
    else:
        correction, everywhere = coarse_by_parts(
            sent[0, :aggs], coarse_order, coarse_values, coarse_rows, coarse_inverse
        )
        index = device_index()
        low = jnp.where(index == 0, 0.0, jnp.where(index % 2 == 0, far[2], near[2]))
        high = jnp.where(index == devices - 1, 0.0, jnp.where(index % 2 == 0, near[2], far[2]))
        order = jnp.concatenate([low, own[2], high], axis=0).astype(i32)
        corr = jnp.repeat(everywhere[order[:, ::CELLS]], CELLS, axis=1)
        result = call(
            functools.partial(finish_kernel, devices), shape_of(pairs, LANES), "vvvvvv", scratch=finish_scratch
        )(corr, *common, smoothed_fine)
    return result.reshape(-1), correction


def solution(mesh):
    devices = mesh.shape["fine"] * mesh.shape["coarse"]
    in_specs = (
        P(BOTH),
        P(None, None, BOTH),
        P(None, BOTH),
        P(None, BOTH),
        P(BOTH),
        P(BOTH),
        P(BOTH),
        P(BOTH),
        P(None, None, "coarse"),
        P(None, "coarse"),
        P(None, "coarse"),
    )
    return jax.shard_map(
        functools.partial(shards, devices),
        mesh=mesh,
        in_specs=in_specs,
        out_specs=(P(BOTH), P("coarse")),
        check_vma=False,
    )
```

```python
import functools

import jax
import jax.numpy as jnp
from jax import lax
from jax.experimental import pallas as pl
from jax.experimental.pallas import tpu as pltpu
from jax.sharding import PartitionSpec as P

CELLS = 64
LANES = 128
HALO_ROWS = 8
SWEEPS = 4
EARLY = 0
BOTH = ("fine", "coarse")
f32, bf16, i32 = jnp.float32, jnp.bfloat16, jnp.int32
VMEM_LIMIT = 24 * 1024 * 1024


def iota(shape, axis):
    return lax.broadcasted_iota(i32, shape, axis)


def split(x):
    high = x.astype(bf16)
    return high, (x - high.astype(f32)).astype(bf16)


def dot(a, b):
    return lax.dot_general(a, b, (((1,), (0,)), ((), ())), preferred_element_type=f32)


def dot_t(a, b):
    return lax.dot_general(a, b, (((1,), (1,)), ((), ())), preferred_element_type=f32)


def cell_sums(high_ref, low_ref):
    width = high_ref.shape[1]
    pairs = width // LANES
    row, lane = iota((2 * pairs, width), 0), iota((2 * pairs, width), 1)
    member = (lane // CELLS == 2 * (row % pairs) + row // pairs).astype(bf16)
    sums = dot_t(member, high_ref[...]) + dot_t(member, low_ref[...])
    return jnp.concatenate([sums[:pairs], sums[pairs:]], axis=1)


def apply_smoother(vector, smoother_ref, high_ref, low_ref):
    for p in range(vector.shape[0]):
        cols = pl.ds(p * LANES, LANES)
        product = smoother_ref[:, cols].astype(f32) * vector[p : p + 1, :]
        high_ref[:, cols], low_ref[:, cols] = split(product)
    return cell_sums(high_ref, low_ref)


def selection(columns, half_rows, pairs):
    nbrs, aggs = columns.shape
    at, who = iota((pairs, aggs), 1), iota((pairs, aggs), 0)
    chosen = [
        jnp.where(at == 2 * who + half, columns[k : k + 1].astype(f32), 0.0)
        for half in range(2)
        for k in range(nbrs)
    ]
    block = dot(jnp.concatenate(chosen, axis=0).astype(bf16), jnp.ones((aggs, 4 * half_rows), bf16)).astype(i32)
    half = iota(block.shape, 0) // (nbrs * pairs)
    place = block // 2 + jnp.where(block % 2 == half, 0, half_rows)
    return (iota(block.shape, 1) % (2 * half_rows) == place).astype(bf16)


def pick(window, selected):
    high, low = split(jnp.concatenate([window, pltpu.roll(window, CELLS, 1)], axis=0))
    picked = dot(selected, jnp.concatenate([high, low], axis=0))
    count = selected.shape[0] // 2
    lane = iota((count, LANES), 1)
    return jnp.where(lane < CELLS, picked[:count], picked[count:])


def apply_smoothed_fine(window, products_ref, selected, picked_ref, high_ref, low_ref):
    nbrs, _, width = products_ref.shape
    pairs = width // LANES
    picked_ref[...] = pick(window, selected)
    for p in range(pairs):
        cols = pl.ds(p * LANES, LANES)
        total = None
        for k in range(nbrs):
            term = products_ref[k, :, cols] * picked_ref[pl.ds(k * pairs + p, 1), :]
            total = term if total is None else total + term
        high_ref[:, cols], low_ref[:, cols] = split(total)
    return cell_sums(high_ref, low_ref)


def as_columns(row, pairs):
    shape = (pairs, row.shape[1])
    at, who = iota(shape, 1), iota(shape, 0)
    return [
        jnp.sum(jnp.where(at == 2 * who + half, row, 0.0), axis=1, keepdims=True)
        for half in range(2)
    ]


def by_half(columns, shape):
    return jnp.where(iota(shape, 1) < CELLS, columns[0], columns[1])


def fetch(sem_ref, *pairs):
    copies = [pltpu.make_async_copy(src, dst, sem_ref.at[i]) for i, (src, dst) in enumerate(pairs)]
    for copy in copies:
        copy.start()
    return copies


def start(rhs_ref, weights_ref, order_ref, smoother_ref, near_ref, onward_ref, own_ref, high_ref, low_ref):
    pairs = rhs_ref.shape[0]
    smoothed = apply_smoother(rhs_ref[...], smoother_ref, high_ref, low_ref)
    order = by_half(as_columns(order_ref[...].astype(f32), pairs), (pairs, LANES))
    even = lax.axis_index("coarse") % 2 == 0
    for i, part in enumerate((smoothed, weights_ref[...], order)):
        own_ref[i] = part
        bottom, top = part[:HALO_ROWS], part[pairs - HALO_ROWS :]
        near_ref[i] = jnp.where(even, top, bottom)
        onward_ref[i] = jnp.where(even, bottom, top)


def start_kernel(
    rhs_any, weights_any, order_any, smoother_any, near_ref, onward_ref, own_ref, smoother_ref,
    rhs_ref, weights_ref, order_ref, high_ref, low_ref, sem_ref,
):
    copies = fetch(
        sem_ref, (smoother_any, smoother_ref), (rhs_any, rhs_ref), (weights_any, weights_ref), (order_any, order_ref)
    )
    for copy in copies:
        copy.wait()
    start(rhs_ref, weights_ref, order_ref, smoother_ref, near_ref, onward_ref, own_ref, high_ref, low_ref)


def start_pack_kernel(
    rhs_any, weights_any, order_any, smoother_any, rows_any, values_any, inverse_any,
    near_ref, onward_ref, own_ref, smoother_ref, packed_ref, first_ref, second_ref,
    rhs_ref, weights_ref, order_ref, rows_ref, values_ref, inverse_ref, high_ref, low_ref, sem_ref,
):
    copies = fetch(
        sem_ref, (smoother_any, smoother_ref), (rhs_any, rhs_ref), (weights_any, weights_ref), (order_any, order_ref),
        (values_any, values_ref), (inverse_any, inverse_ref), (rows_any, rows_ref),
    )
    for copy in copies[:4]:
        copy.wait()
    start(rhs_ref, weights_ref, order_ref, smoother_ref, near_ref, onward_ref, own_ref, high_ref, low_ref)
    for copy in copies[4:]:
        copy.wait()
    own_blocks, nbrs = rows_ref.shape
    deep, width = values_ref.shape
    at, slot = iota((8, nbrs), 1), iota((8, nbrs), 0)
    block = iota((8, width), 1) // CELLS
    rows = jnp.zeros((8, width), f32)
    for j in range(own_blocks):
        targets = jnp.where(at == slot, rows_ref[j : j + 1, :].astype(f32), 0.0)
        rows = jnp.where(block == j, jnp.sum(targets, axis=1, keepdims=True), rows)
    inverse = inverse_ref[...].astype(f32)
    for ref in (packed_ref, first_ref):
        ref[pl.ds(0, 8), :] = rows
        ref[pl.ds(8, CELLS), :] = inverse
    base = 8 + CELLS
    early = first_ref.shape[0] - base
    for r in range(0, deep, CELLS):
        values = values_ref[pl.ds(r, CELLS), :].astype(f32)
        packed_ref[pl.ds(base + r, CELLS), :] = values
        if r < early:
            first_ref[pl.ds(base + r, CELLS), :] = values
        else:
            second_ref[pl.ds(r - early, CELLS), :] = values


def window_of(near_ref, far_ref, own_ref, device, devices):
    even = device % 2 == 0
    near, far = near_ref[...], far_ref[...]
    low = jnp.where(device == 0, 0.0, jnp.where(even, far, near))
    high = jnp.where(device == devices - 1, 0.0, jnp.where(even, near, far))
    return [jnp.concatenate([low[i], own_ref[i], high[i]], axis=0) for i in range(3)]


def device_index():
    return lax.axis_index("fine") * lax.axis_size("coarse") + lax.axis_index("coarse")


def prepare_kernel(
    counts_ref, own_ref, rhs_any, reaction_any, columns_any, fine_any, selected_ref, weighed_ref, local_ref,
    masked_ref, fine_ref, rhs_ref, reaction_ref, columns_ref, wide_ref, sem_ref,
):
    copies = fetch(
        sem_ref, (columns_any, columns_ref), (rhs_any, rhs_ref), (reaction_any, reaction_ref),
        *((fine_any.at[k], fine_ref.at[k]) for k in range(fine_ref.shape[0])),
    )
    nbrs, _, width = fine_ref.shape
    pairs = width // LANES
    weights = own_ref[1]
    by_agg = jnp.concatenate([weights[:, :CELLS], weights[:, CELLS:]], axis=0)
    row, lane = iota((2 * pairs, width), 0), iota((2 * pairs, width), 1)
    member = (lane // CELLS == 2 * (row % pairs) + row // pairs).astype(bf16)
    wide = None
    for part in split(by_agg):
        term = lax.dot_general(part, member, (((0,), (0,)), ((), ())), preferred_element_type=f32)
        wide = term if wide is None else wide + term
    wide_ref[...] = wide
    for copy in copies[:3]:
        copy.wait()
    agg = 2 * iota((pairs, LANES), 0) + iota((pairs, LANES), 1) // CELLS
    reaction = jnp.where(agg < counts_ref[0], reaction_ref[...], 0.0)
    local_ref[0] = weights * rhs_ref[...]
    local_ref[1] = weights * reaction
    masked_ref[...] = reaction
    selected_ref[...] = selection(columns_ref[...], pairs + 2 * HALO_ROWS, pairs)
    for k in range(nbrs):
        copies[3 + k].wait()
        for p in range(pairs):
            cols = pl.ds(p * LANES, LANES)
            term = fine_ref[k, :, cols].astype(f32) * wide_ref[:, cols]
            total = term[:8]
            for r in range(8, CELLS, 8):
                total = total + term[r : r + 8]
            weighed_ref[k * pairs + p] = total


def products_kernel(reaction_ref, fine_ref, smoother_ref, products_ref):
    nbrs, _, width = fine_ref.shape
    pairs = width // LANES
    lane = iota((CELLS, LANES), 1)
    for p in range(pairs):
        cols = pl.ds(p * LANES, LANES)
        left = smoother_ref[:, cols]
        rights = []
        for k in range(nbrs):
            block = fine_ref[k, :, cols]
            zero = jnp.zeros_like(block)
            apart = [jnp.where(lane < CELLS, block, zero), jnp.where(lane < CELLS, zero, block)]
            rights.append(jnp.concatenate(apart, axis=0))
        both = dot(left, jnp.concatenate(rights, axis=1))
        for k in range(nbrs):
            product = both[:, k * LANES : (k + 1) * LANES]
            products_ref[k, :, cols] = product if k else product + left.astype(f32) * reaction_ref[p : p + 1, :]


def residual_kernel(
    devices, near_ref, far_ref, own_ref, selected_ref, weighed_ref, local_ref, out_ref, picked_ref,
):
    smoothed, _, _ = window_of(near_ref, far_ref, own_ref, device_index(), devices)
    picked_ref[...] = pick(smoothed, selected_ref[...])
    pairs = own_ref.shape[1]
    nbrs = picked_ref.shape[0] // pairs
    images = []
    for p in range(pairs):
        total = None
        for k in range(nbrs):
            term = weighed_ref[k * pairs + p] * picked_ref[pl.ds(k * pairs + p, 1), :]
            total = term if total is None else total + term
        images.append(jnp.sum(total, axis=0, keepdims=True))
    weighted = local_ref[0] - local_ref[1] * own_ref[0] - jnp.concatenate(images, axis=0)
    shape = (pairs, LANES)
    lane, who = iota(shape, 1), iota(shape, 0)
    row = jnp.zeros((1, LANES), f32)
    for half in range(2):
        inside = lane // CELLS == half
        restricted = jnp.sum(jnp.where(inside, weighted, 0.0), axis=1, keepdims=True)
        order = jnp.max(jnp.where(inside, own_ref[2], 0.0), axis=1, keepdims=True)
        spread = jnp.where(lane == 2 * who + half, restricted, 0.0)
        spread = spread + jnp.where(lane == 2 * (pairs + who) + half, order, 0.0)
        row = row + jnp.sum(spread, axis=0, keepdims=True)
    out_ref[...] = jnp.broadcast_to(row, out_ref.shape)


def finish(corr, near_ref, far_ref, own_ref, devices, selected_ref, products_ref, result_ref,
           picked_ref, high_ref, low_ref):
    smoothed, weights, _ = window_of(near_ref, far_ref, own_ref, device_index(), devices)
    corrected = smoothed + weights * corr
    mine = corrected[HALO_ROWS : HALO_ROWS + own_ref.shape[1]]
    image = apply_smoothed_fine(corrected, products_ref, selected_ref[...], picked_ref, high_ref, low_ref)
    result_ref[...] = mine + (own_ref[0] - image)


def place(group, own_blocks):
    return jnp.bitwise_xor(group // own_blocks, lax.axis_index("coarse")) * own_blocks + group % own_blocks


def pairs_of(x):
    half = x.shape[0] // 2
    return jnp.concatenate([x[:half], x[half:]], axis=1)


def masked_rows(x, mask_lists, pair_at, held_ref):
    pairs = x.shape[0]
    high, low = split(x)
    held_ref[pl.ds(0, pairs), :] = high.astype(f32)
    held_ref[pl.ds(pairs, pairs), :] = low.astype(f32)
    parts = []
    for part in range(2):
        rows = [
            jnp.broadcast_to(held_ref[pl.ds(part * pairs + p, 1), :], (2 * pairs, LANES)).astype(bf16)
            for p in range(pairs)
        ]
        parts.append(rows)
    return jnp.concatenate(
        [
            jnp.concatenate([mask * rows[pair_at(c)] for c, mask in enumerate(masks)], axis=1)
            for masks in mask_lists
            for rows in parts
        ],
        axis=0,
    )


def inverse_product(x, inverse_ref, held_ref):
    pairs = x.shape[0]
    groups = 2 * pairs
    row, lane = iota((groups, LANES), 0), iota((groups, LANES), 1)
    masks = [((row % pairs == p) & (row // pairs == lane // CELLS)).astype(bf16) for p in range(pairs)]
    sums = dot(masked_rows(x, [masks], lambda c: c, held_ref), inverse_ref[...])
    return pairs_of(sums[:groups] + sums[groups:])


def slot_pair(rows_ref, first, count):
    turned = rows_ref[pl.ds(first, CELLS * count), :].astype(bf16).T
    return turned if count == 2 else jnp.concatenate([turned, jnp.zeros_like(turned)], axis=1)


def target_rows(x, target_ref, start, stop, own_blocks, held_ref):
    groups, half = target_ref.shape[0], target_ref.shape[1] // 2
    per_part = half // LANES // (groups // own_blocks)
    per_block = own_blocks // 2
    masks = [[target_ref[:, pl.ds(t * half + c, LANES)] for c in range(start, stop, LANES)] for t in range(2)]

    def pair_at(chunk):
        chunk = chunk + start // LANES
        return chunk // per_part * per_block + chunk % per_block

    return masked_rows(x, masks, pair_at, held_ref)


def first_sweep_kernel(
    gathered_ref, mine_ref, beside_ref, first2_ref, second2_ref, first3_ref,
    side_ref, begun_ref, inverse_ref, target_ref, blocks_ref, sums_ref, held_ref,
):
    part_refs = (mine_ref, beside_ref, first2_ref, first3_ref)
    width = mine_ref.shape[1]
    own_blocks = width // CELLS
    pairs = side_ref.shape[0]
    groups = 2 * pairs
    base = 8 + CELLS
    nbrs = (mine_ref.shape[0] - base) // CELLS
    early = (first2_ref.shape[0] - base) // CELLS
    for i, ref in enumerate(part_refs):
        inverse_ref[pl.ds(i * width, width), :] = ref[pl.ds(8, CELLS), :].astype(bf16).T

    gathered = gathered_ref[...]
    devs = gathered.shape[0]
    lane = iota((8, LANES), 1)
    row = iota((groups, LANES), 0)
    number = 2 * (row % pairs) + row // pairs
    lefts, rights = [], []
    for start in range(0, devs, 32):
        value = jnp.zeros((8, LANES), f32)
        order = jnp.zeros((8, LANES), f32)
        for i in range(4):
            piece = gathered[start + 8 * i : start + 8 * i + 8]
            here = lane // 32 == i
            value = jnp.where(here, pltpu.roll(piece, 32 * i, 1) if i else piece, value)
            order = jnp.where(here, pltpu.roll(piece, (32 * i + 96) % LANES, 1) if i != 1 else piece, order)
        order = order.astype(i32)
        group, unit = place(order // CELLS, own_blocks), order % CELLS
        for s in range(8):
            left = jnp.where(number == group[s : s + 1], value[s : s + 1], 0.0)
            lefts.append(jnp.concatenate(split(left), axis=0))
            rights.append((iota((CELLS, LANES), 0) == unit[s : s + 1]).astype(bf16))
    side = dot_t(jnp.concatenate(lefts, axis=1), jnp.concatenate(rights, axis=1))
    side = pairs_of(side[:groups] + side[groups:])
    side_ref[...] = side
    begun = inverse_product(side, inverse_ref, held_ref)
    begun_ref[...] = begun

    row = iota((groups, width), 0)
    number = 2 * (row % pairs) + row // pairs
    twos = (nbrs + 1) // 2
    half = twos * width * len(part_refs)
    for i, ref in enumerate(part_refs):
        targets = place(ref[pl.ds(0, 8), :].astype(i32), own_blocks)
        for k in range(2 * twos):
            cols = pl.ds(k % 2 * half + (i * twos + k // 2) * width, width)
            chosen = number == targets[k : k + 1] if k < nbrs else jnp.zeros(row.shape, jnp.bool_)
            target_ref[:, cols] = chosen.astype(bf16)
        for q in range(twos):
            rows = pl.ds((i * twos + q) * width, width)
            count = min(2, nbrs - 2 * q)
            if i < 2 or 2 * q < early:
                blocks_ref[rows, :] = slot_pair(ref, base + 2 * q * CELLS, count)
            elif i == 2:
                blocks_ref[rows, :] = slot_pair(second2_ref, (2 * q - early) * CELLS, count)

    sums_ref[...] = dot(target_rows(begun, target_ref, 0, blocks_ref.shape[0], own_blocks, held_ref), blocks_ref[...])


def solve_kernel(
    devices, side_ref, begun_ref, inverse_ref, target_ref, blocks_ref, sums_ref, near_ref, far_ref, own_ref, selected_ref,
    second3_ref, products_ref,
    out_any, correction_any,
    last_ref, held_ref, result_ref, correction_ref,
    picked_ref, high_ref, low_ref, out_sem_ref,
):
    width = second3_ref.shape[1]
    own_blocks = width // CELLS
    groups, half = target_ref.shape[0], target_ref.shape[1] // 2
    pairs = groups // 2
    late = second3_ref.shape[0] // CELLS
    for q in range(0, late, 2):
        last_ref[pl.ds(q // 2 * width, width), :] = slot_pair(second3_ref, q * CELLS, min(2, late - q))
    side = side_ref[...]
    correction = begun_ref[...]
    split_at = blocks_ref.shape[0]
    for sweep in range(SWEEPS - 1):
        if sweep == 0:
            sums = sums_ref[...]
            spread = target_rows(correction, target_ref, split_at, half, own_blocks, held_ref)
        else:
            spread = target_rows(correction, target_ref, 0, half, own_blocks, held_ref)
            sums = dot(spread[:, :split_at], blocks_ref[...])
            spread = spread[:, split_at:]
        sums = sums + dot(spread, last_ref[...])
        image = sums[:groups] + sums[groups : 2 * groups]
        other = sums[2 * groups : 3 * groups] + sums[3 * groups :]
        image = pairs_of(image[:, :CELLS] + other[:, CELLS:])
        correction = correction + inverse_product(side - image, inverse_ref, held_ref)
    correction_ref[...] = correction[: own_blocks // 2]
    correction_copy = pltpu.make_async_copy(correction_ref, correction_any, out_sem_ref.at[0])
    correction_copy.start()

    order = window_of(near_ref, far_ref, own_ref, device_index(), devices)[2].astype(i32)
    rows = order.shape[0]
    unit = jnp.concatenate([order[:, :CELLS], order[:, CELLS:]], axis=0)
    chosen = (iota(unit.shape, 1) == unit % CELLS).astype(bf16)
    by_block = jnp.concatenate([correction[:, :CELLS], correction[:, CELLS:]], axis=0)
    values = dot_t(chosen, jnp.concatenate(split(by_block), axis=0))
    group = place(unit[:, : 2 * groups] // CELLS, own_blocks)
    group = group // 2 + group % 2 * pairs
    values = jnp.sum(jnp.where(iota(values.shape, 1) % groups == group, values, 0.0), axis=1, keepdims=True)
    corr = by_half([values[:rows], values[rows:]], (rows, LANES))
    finish(corr, near_ref, far_ref, own_ref, devices, selected_ref, products_ref, result_ref,
           picked_ref, high_ref, low_ref)
    result_copy = pltpu.make_async_copy(result_ref, out_any, out_sem_ref.at[1])
    result_copy.start()
    correction_copy.wait()
    result_copy.wait()


def finish_kernel(
    devices, corr_ref, near_ref, far_ref, own_ref, selected_ref, products_ref, result_ref, picked_ref, high_ref, low_ref,
):
    finish(corr_ref[...], near_ref, far_ref, own_ref, devices, selected_ref, products_ref, result_ref,
           picked_ref, high_ref, low_ref)


def call(kernel, out_shape, ins, outs=None, scratch=(), cost=None):
    spaces = dict(s=pltpu.SMEM, v=pltpu.VMEM, a=pl.ANY)
    many = isinstance(out_shape, tuple)
    specs = tuple(pl.BlockSpec(memory_space=spaces[c]) for c in outs or "v" * (len(out_shape) if many else 1))
    run = pl.pallas_call(
        kernel,
        out_shape=out_shape,
        in_specs=[pl.BlockSpec(memory_space=spaces[c]) for c in ins],
        out_specs=specs if many else specs[0],
        scratch_shapes=list(scratch),
        compiler_params=pltpu.CompilerParams(vmem_limit_bytes=VMEM_LIMIT),
        cost_estimate=cost and pl.CostEstimate(flops=cost, bytes_accessed=0, transcendentals=0),
    )

    def placed(*operands):
        return run(*(pltpu.with_memory_space_constraint(x, pltpu.HBM) if c == "a" else x for x, c in zip(operands, ins)))

    return placed


def shape_of(*dims):
    return jax.ShapeDtypeStruct(dims, f32)


def coarse_by_parts(restricted, coarse_order, coarse_values, coarse_rows, coarse_inverse):
    own = coarse_inverse.shape[1]
    own_blocks = own // CELLS
    total = own * lax.axis_size("coarse")
    start = lax.axis_index("coarse") * own
    side = jnp.zeros((total,), f32).at[coarse_order].add(restricted)
    side = lax.dynamic_slice_in_dim(lax.psum(side, BOTH), start, own)
    values = coarse_values.astype(f32).reshape(-1, CELLS, own_blocks, CELLS)
    inverse = coarse_inverse.astype(f32).reshape(CELLS, own_blocks, CELLS)

    def scale(x):
        x = x.reshape(own_blocks, CELLS)
        return jnp.einsum("oji,ji->jo", inverse, x, precision=lax.Precision.HIGHEST).reshape(-1)

    correction = scale(side)
    for _ in range(SWEEPS - 1):
        x = correction.reshape(own_blocks, CELLS)
        sums = jnp.einsum("vfmd,md->vmf", values, x, precision=lax.Precision.HIGHEST)
        image = jax.ops.segment_sum(
            sums.reshape(-1, CELLS), coarse_rows.reshape(-1), num_segments=total // CELLS
        ).reshape(-1)
        image = lax.dynamic_slice_in_dim(lax.psum(image, "coarse"), start, own)
        correction = correction + scale(side - image)
    return correction, lax.all_gather(correction, "coarse", axis=0, tiled=True)


def shards(
    devices, rhs, fine_values, fine_columns, smoother, reaction, pit_counts, weights, coarse_order,
    coarse_values, coarse_rows, coarse_inverse,
):
    cells = rhs.shape[0]
    pairs = cells // LANES
    aggs = 2 * pairs
    nbrs = fine_columns.shape[0]
    parts = lax.axis_size("coarse")
    rhs, reaction, weights = (x.reshape(pairs, LANES) for x in (rhs, reaction, weights))
    rows = pairs + 2 * HALO_ROWS
    vector = pltpu.VMEM((pairs, LANES), f32)
    products = [pltpu.VMEM((CELLS, cells), bf16)] * 2
    picked = pltpu.VMEM((nbrs * pairs, LANES), f32)
    copies = pltpu.SemaphoreType.DMA((4,))
    edge = shape_of(3, HALO_ROWS, LANES)

    copied = parts == 4 and devices % 32 == 0 and devices <= 64
    start_shapes = (
        edge, edge, shape_of(3, pairs, LANES), jax.ShapeDtypeStruct(smoother.shape, bf16)
    )
    start_ins = (rhs, weights, coarse_order.reshape(1, aggs), smoother)
    start_scratch = [vector, vector, pltpu.VMEM((1, aggs), i32)]
    if copied:
        deep = coarse_values.shape[0] * CELLS
        width = coarse_inverse.shape[1]
        early = EARLY * CELLS
        near, onward, own, smoother_here, packed, first, second = call(
            start_pack_kernel,
            (*start_shapes, shape_of(8 + CELLS + deep, width), shape_of(8 + CELLS + early, width),
             shape_of(deep - early, width)),
            "aaaaaaa",
            scratch=[
                *start_scratch, pltpu.VMEM(coarse_rows.shape[::-1], i32), pltpu.VMEM((deep, width), bf16),
                pltpu.VMEM(coarse_inverse.shape, bf16), *products, pltpu.SemaphoreType.DMA((7,)),
            ],
        )(*start_ins, coarse_rows.T, coarse_values.reshape(deep, width), coarse_inverse)
        swap = [(c, c ^ 1) for c in range(parts)]
        across = [(c, c ^ 2) for c in range(parts)]
        first2 = lax.ppermute(first, "coarse", across)
    else:
        near, onward, own, smoother_here = call(start_kernel, start_shapes, "aaaa", scratch=[*start_scratch, *products, copies])(
            *start_ins
        )

    partner = [(d, d ^ 1) for d in range(devices)]
    chain = []
    for d in range(devices):
        target = d + 2 if d % 2 == 0 else d - 2
        chain.append((d, target if 0 <= target < devices else d ^ 1))
    onward = lax.ppermute(onward, BOTH, partner)
    near, onward = lax.optimization_barrier((near, onward))
    near = lax.ppermute(near, BOTH, partner)

    if copied:
        second, packed, onward = lax.optimization_barrier((second, packed, onward))
    far = lax.ppermute(onward, BOTH, chain)
    selected, weighed, local, masked, fine_here = call(
        prepare_kernel,
        (jax.ShapeDtypeStruct((aggs * nbrs, 4 * rows), bf16), shape_of(nbrs * pairs, 8, LANES), shape_of(2, pairs, LANES),
         shape_of(pairs, LANES), jax.ShapeDtypeStruct(fine_values.shape, bf16)),
        "svaaaa",
        scratch=[vector, vector, pltpu.VMEM(fine_columns.shape, i32), pltpu.VMEM((CELLS, cells), f32), pltpu.SemaphoreType.DMA((3 + nbrs,))],
        cost=10_000_000_000,
    )(pit_counts, own, rhs, reaction, fine_columns, fine_values)
    smoothed_fine = call(products_kernel, shape_of(*fine_values.shape), "vvv")(masked, fine_here, smoother_here)

    if copied:
        beside = lax.ppermute(packed, "coarse", swap)
        second2 = lax.ppermute(second, "coarse", across)
        first3 = lax.ppermute(first2, "coarse", swap)

    sent = call(
        functools.partial(residual_kernel, devices), shape_of(devices, LANES), "vvvvvv", scratch=[picked], cost=None
    )(near, far, own, selected, weighed, local)

    finish_scratch = [picked, *products]
    common = (near, far, own, selected)
    if copied:
        gathered = lax.all_to_all(sent, BOTH, 0, 0, tiled=True)
        first3, second2, gathered = lax.optimization_barrier((first3, second2, gathered))
        second3 = lax.ppermute(second2, "coarse", swap)
        unknowns = parts * width
        groups = unknowns // CELLS
        twos, late = (nbrs + 1) // 2, (nbrs - EARLY + 1) // 2
        begun = call(
            first_sweep_kernel,
            (shape_of(unknowns // LANES, LANES), shape_of(unknowns // LANES, LANES),
             jax.ShapeDtypeStruct((unknowns, CELLS), bf16), jax.ShapeDtypeStruct((groups, 2 * twos * unknowns), bf16),
             jax.ShapeDtypeStruct((twos * unknowns - late * width, LANES), bf16), shape_of(4 * groups, LANES)),
            "vvvvvv",
            scratch=[pltpu.VMEM((groups, LANES), f32)],
        )(gathered, packed, beside, first2, second2, first3)
        result, correction = call(
            functools.partial(solve_kernel, devices),
            (shape_of(pairs, LANES), shape_of(width // LANES, LANES)),
            "vvvvvv" + "vvvv" + "vv",
            outs="aa",
            scratch=[
                pltpu.VMEM((late * width, LANES), bf16), pltpu.VMEM((groups, LANES), f32), vector,
                pltpu.VMEM((width // LANES, LANES), f32), *finish_scratch, pltpu.SemaphoreType.DMA((2,)),
            ],
        )(*begun, *common, second3, smoothed_fine)
        correction = correction.reshape(-1)
    else:
        correction, everywhere = coarse_by_parts(
            sent[0, :aggs], coarse_order, coarse_values, coarse_rows, coarse_inverse
        )
        index = device_index()
        low = jnp.where(index == 0, 0.0, jnp.where(index % 2 == 0, far[2], near[2]))
        high = jnp.where(index == devices - 1, 0.0, jnp.where(index % 2 == 0, near[2], far[2]))
        order = jnp.concatenate([low, own[2], high], axis=0).astype(i32)
        corr = jnp.repeat(everywhere[order[:, ::CELLS]], CELLS, axis=1)
        result = call(
            functools.partial(finish_kernel, devices), shape_of(pairs, LANES), "vvvvvv", scratch=finish_scratch
        )(corr, *common, smoothed_fine)
    return result.reshape(-1), correction


def solution(mesh):
    devices = mesh.shape["fine"] * mesh.shape["coarse"]
    in_specs = (
        P(BOTH),
        P(None, None, BOTH),
        P(None, BOTH),
        P(None, BOTH),
        P(BOTH),
        P(BOTH),
        P(BOTH),
        P(BOTH),
        P(None, None, "coarse"),
        P(None, "coarse"),
        P(None, "coarse"),
    )
    return jax.shard_map(
        functools.partial(shards, devices),
        mesh=mesh,
        in_specs=in_specs,
        out_specs=(P(BOTH), P("coarse")),
        check_vma=False,
    )
```
